32 devices in a mesh: grp: 2 (over y), band: 4 (over z), var: 2 (over x), sub: 2 (over core).
Axes of the slice: x: 2, y: 2, z: 4, core: 2. Of those that a mesh axis runs over, the one named last changes fastest.
Arguments:
- ocean_fields: bfloat16 [576, 4, 48, 128], P(('grp', 'band', 'sub'), None, 'var'), parts along dimension 0, may hold values from -6 to 6
- ocean_dest: int32 [288, 1], P(('band', 'sub')), may hold values from 0 to 3, as said below
- ocean_weights: bfloat16 [4, 2, 4, 14, 128, 128], P('band', 'sub'), may hold values from -0.5 to 0.5
- ocean_tiles: int32 [4, 2, 4, 14], P('band', 'sub'), may hold values from 0 to 15, as said below
- atmos_fields: bfloat16 [576, 4, 48, 128], P(('grp', 'band', 'sub'), None, 'var'), parts along dimension 0, may hold values from -6 to 6
- atmos_dest: int32 [288, 1], P(('band', 'sub')), may hold values from 0 to 3, as said below
- atmos_weights: bfloat16 [4, 2, 4, 14, 128, 128], P('band', 'sub'), may hold values from -0.5 to 0.5
- atmos_tiles: int32 [4, 2, 4, 14], P('band', 'sub'), may hold values from 0 to 15, as said below
- land_fraction: float32 [4, 2, 8, 2, 128], P('band', 'sub'), may hold values from 0 to 1
- embed_weight: bfloat16 [12288, 1024], P(('var', 'sub')), may hold values from -0.0546875 to 0.0546875
- embed_bias: float32 [1024], replicated, may hold values from -4 to 4
- embed_gain: float32 [1024], replicated, may hold values from 0.5 to 1.5
Outputs:
- patch_embed: bfloat16 [2, 8, 4, 8, 1024], P('sub', 'var', None, ('grp', 'band')), parts along dimension 3
The draws below stay inside these ranges and needn't reach their ends.
There are 2 independent parts, one for each index of `grp`. The reference program is written for one: setup_inputs(seed, part) draws one part's arguments, and reference() takes and returns one part's arrays. A program takes and returns all parts, laid end to end along the dimension named above; an argument that names none is the same for every part. Nothing has to cross between parts.
Inputs may be any that keep to these rules, and one draw needn't show every extreme that they name: `ocean_dest`: each device holds at least 4 and at most 14 blocks naming each band; one band is named by exactly 14 blocks on every device. `atmos_dest`: each device holds at least 4 and at most 14 blocks naming each band; one band is named by exactly 14 blocks on every device. `ocean_tiles`: for each band b and half h, the entries [b, h, j, r] with r < 4 name every half-patch. `atmos_tiles`: for each band b and half h, the entries [b, h, j, r] with r < 4 name every half-patch.
All inputs are finite; a program needn't handle non-finite values.
Results may differ from the reference program's by a relative error of at most 0.0045.
Values may be sent and summed in bfloat16 or wider, within the bound.
No kernel may reach another device: no remote copies, remote signals or barrier semaphores. Data moves between devices by JAX's collectives and lax.ppermute only.
A program may use at most 128 MiB of HBM per device.

```python
import jax
import jax.numpy as jnp
from jax import lax

VARS = 48
EMB = 1024
HT = 128
BR = 128
NB = 36
TPD = 8
BASE = 4
EXTRA = 10
CAP = 14
TIME = 4
OB = 288
N_BAND = 4
N_SUB = 2


def route_blocks(key, depth):
    devices = N_BAND * N_SUB
    spare = NB - BASE * N_BAND
    tickets = N_BAND * EXTRA
    key_pop, key_hot, key_score, key_order = jax.random.split(key, 4)
    popular = jax.random.permutation(key_pop, N_BAND).astype(jnp.int32)
    rank_of = jnp.argsort(popular).astype(jnp.int32)
    picks = jax.random.randint(key_hot, (depth, devices), 0, N_BAND)
    hot_band = popular[jnp.min(picks, axis=0)]
    ticket_band = jnp.repeat(jnp.arange(N_BAND, dtype=jnp.int32), EXTRA)
    noise = jax.random.randint(key_score, (devices, tickets), 0, 1024)
    favour = (N_BAND - rank_of[ticket_band]) * 256
    forced = ((ticket_band[None, :] == hot_band[:, None]) | (ticket_band[None, :] == popular[0])).astype(jnp.int32) * 65536
    score = (noise + favour[None, :] + forced) * tickets + jnp.arange(tickets, dtype=jnp.int32)[None, :]
    unused, chosen = lax.top_k(score, spare)
    extra_bands = ticket_band[chosen]
    base_row = jnp.repeat(jnp.arange(N_BAND, dtype=jnp.int32), BASE)
    base_bands = jnp.broadcast_to(base_row[None, :], (devices, BASE * N_BAND))
    bands = jnp.concatenate([base_bands, extra_bands], axis=1)
    order_keys = jax.random.split(key_order, devices)
    shuffled = jax.vmap(lambda k, row: jax.random.permutation(k, row))(order_keys, bands)
    return shuffled.reshape(OB, 1).astype(jnp.int32)


def half_patch_table(key):
    owners = N_BAND * N_SUB
    key_perm, key_rest = jax.random.split(key)
    perms = jax.vmap(lambda k: jax.random.permutation(k, 2 * TPD))(jax.random.split(key_perm, owners)).astype(jnp.int32)
    source = jnp.arange(N_BAND, dtype=jnp.int32)[:, None]
    slot = jnp.arange(CAP, dtype=jnp.int32)[None, :]
    spot = (slot * N_BAND + source) % (2 * TPD)
    covered = perms[:, spot]
    loose = jax.random.randint(key_rest, (owners, N_BAND, CAP), 0, 2 * TPD).astype(jnp.int32)
    tiles = jnp.where(slot[None, :, :] < BASE, covered, loose)
    return tiles.reshape(N_BAND, N_SUB, N_BAND, CAP).astype(jnp.int32)


def draw_ocean_dest(key, part):
    key = jax.random.fold_in(key, 3)
    return route_blocks(key, 2)


def draw_atmos_dest(key, part):
    key = jax.random.fold_in(key, 5)
    return route_blocks(key, 3)


def draw_ocean_tiles(key, part):
    key = jax.random.fold_in(key, 7)
    return half_patch_table(key)


def draw_atmos_tiles(key, part):
    key = jax.random.fold_in(key, 9)
    return half_patch_table(key)


def shard_levels(rng, extent, shards, smallest, top_value):
    factor_of, own = 1.0, jax.random.fold_in(rng, 6)
    for axis_at, blocks in shards:
        steps = jnp.exp(jax.random.uniform(jax.random.fold_in(own, axis_at), (blocks,), jnp.float32, smallest / len(shards), top_value / len(shards)))
        factor_of = factor_of * jnp.repeat(steps, extent[axis_at] // blocks).reshape([-1 if axis == axis_at else 1 for axis in range(len(extent))])
    return factor_of


def gaussian(key, extent, spread, reach, shards=(), kind=jnp.bfloat16):
    result = spread * jax.random.normal(key, extent, jnp.float32)
    if shards:
        result = result * shard_levels(key, extent, shards, -0.22, 0.18)
    return jnp.clip(result, -reach, reach).astype(kind)


def setup_inputs(seed: int = 0, part: int = 0) -> dict:
    key_list = jax.random.split(jax.random.key(seed), 13)
    part_splits = jax.random.split(jax.random.fold_in(key_list[12], part), 13)
    return {
        "ocean_fields": gaussian(part_splits[0], (OB, TIME, VARS, BR), 1.0, 6.0, ((0, 8), (2, 2))),
        "ocean_dest": draw_ocean_dest(jax.random.fold_in(key_list[12], 71), part),
        "ocean_weights": gaussian(key_list[2], (N_BAND, N_SUB, N_BAND, CAP, BR, HT), BR ** -0.5, 0.5, ((0, 4), (1, 2))),
        "ocean_tiles": draw_ocean_tiles(jax.random.fold_in(key_list[12], 71), part),
        "atmos_fields": gaussian(part_splits[4], (OB, TIME, VARS, BR), 1.0, 6.0, ((0, 8), (2, 2))),
        "atmos_dest": draw_atmos_dest(jax.random.fold_in(key_list[12], 71), part),
        "atmos_weights": gaussian(key_list[6], (N_BAND, N_SUB, N_BAND, CAP, BR, HT), BR ** -0.5, 0.5, ((0, 4), (1, 2))),
        "atmos_tiles": draw_atmos_tiles(jax.random.fold_in(key_list[12], 71), part),
        "land_fraction": jnp.clip(1.0 * jax.random.uniform(key_list[8], (N_BAND, N_SUB, TPD, 2, HT), jnp.float32) ** shard_levels(key_list[8], (N_BAND, N_SUB, TPD, 2, HT), ((0, 4), (1, 2)), -0.2, 0.2), 0.0, 1.0),
        "embed_weight": gaussian(key_list[9], (VARS * 2 * HT, EMB), (VARS * 2 * HT) ** -0.5, 0.0546875, ((0, 4),)),
        "embed_bias": gaussian(key_list[10], (EMB,), 1.0, 4.0, (), jnp.float32),
        "embed_gain": jnp.clip(1.0 + 0.1 * jax.random.normal(key_list[11], (EMB,), jnp.float32), 0.5, 1.5),
    }


def regrid(fields, targets, weights, tile_lookup):
    block_count = fields.shape[0]
    serial = jnp.arange(block_count, dtype=jnp.int32)
    device = serial // NB
    source_band = device // N_SUB
    half_lon = device % N_SUB
    dest_band = targets[:, 0].astype(jnp.int32)
    earlier = (device[:, None] == device[None, :]) & (dest_band[:, None] == dest_band[None, :]) & (serial[None, :] < serial[:, None])
    position = lax.optimization_barrier(jnp.sum(earlier.astype(jnp.int32), axis=1)).astype(jnp.int32)
    block_weights = weights[dest_band, half_lon, source_band, position].astype(jnp.float32)
    tile_ids = tile_lookup[dest_band, half_lon, source_band, position].astype(jnp.int32)
    stacked = fields.reshape(block_count, TIME * VARS, BR).astype(jnp.float32)
    products = jnp.einsum('gmb,gbh->gmh', stacked, block_weights, precision=lax.Precision.HIGHEST)
    accum_field = jnp.zeros((N_BAND, N_SUB, 2 * TPD, TIME * VARS, HT), jnp.float32)
    return accum_field.at[dest_band, half_lon, tile_ids].add(products)

def reference(ocean_fields, ocean_dest, ocean_weights, ocean_tiles, atmos_fields, atmos_dest, atmos_weights, atmos_tiles, land_fraction, embed_weight, embed_bias, embed_gain):
    ocean_remap = regrid(ocean_fields, ocean_dest, ocean_weights, ocean_tiles)
    atmos_remap = regrid(atmos_fields, atmos_dest, atmos_weights, atmos_tiles)
    land_frac = land_fraction.reshape(N_BAND, N_SUB, 2 * TPD, 1, HT)
    merged = (land_frac * atmos_remap + (1.0 - land_frac) * ocean_remap).astype(jnp.bfloat16)
    merged = merged.reshape(N_BAND, N_SUB, TPD, 2, TIME, VARS, HT).transpose(1, 2, 0, 4, 5, 3, 6)
    row_feats = merged.reshape(N_SUB * TPD * N_BAND * TIME, VARS * 2 * HT)
    summed = jnp.dot(row_feats, embed_weight, preferred_element_type=jnp.float32) + embed_bias
    inverse = lax.rsqrt(lax.optimization_barrier(jnp.mean(summed * summed, axis=-1, keepdims=True)) + 1e-05)
    finished = (summed * inverse * embed_gain).astype(jnp.bfloat16)
    return finished.reshape(N_SUB, TPD, N_BAND, TIME, EMB)
```

```python
import functools

import jax
import jax.numpy as jnp
from jax import lax
from jax.experimental import pallas as pl
from jax.experimental.pallas import tpu as pltpu
from jax.sharding import PartitionSpec as P

REPL = ("grp", "var")


def slot_tables(dest, band_count, cap):
    count = dest.shape[0]
    serial = jnp.arange(count, dtype=jnp.int32)
    band_of = dest[:, 0]
    earlier = (band_of[:, None] == band_of[None, :]) & (serial[None, :] < serial[:, None])
    position = jnp.sum(earlier.astype(jnp.int32), axis=1)
    slot = band_of * cap + position
    hit = slot[None, :] == jnp.arange(band_count * cap, dtype=jnp.int32)[:, None]
    block = jnp.sum(jnp.where(hit, serial[None, :], 0), axis=1)
    used = jnp.any(hit, axis=1)
    return block.reshape(band_count, cap), used.reshape(band_count, cap)


def regrid_kernel(part_slots, table, where, *refs):
    part_count = len(part_slots)
    fields, land = refs[0], refs[1]
    parts = refs[2 : 2 + part_count]
    out, acc = refs[-2], refs[-1]
    acc[...] = jnp.zeros_like(acc)
    slots = table.shape[2]
    band = where[0]
    for at, (part, size) in enumerate(zip(parts, part_slots)):
        first = where[1 + at]

        def product(s, part=part, first=first):
            block = table[0, band, first + s]
            scale = table[2, band, first + s]
            w = part[0, s] if len(part.shape) == 4 else part[s]
            dense = jnp.dot(fields[block], w, preferred_element_type=jnp.float32)
            return dense * land[band, pl.ds(scale, 1), :]

        for s in range(size):
            tile = table[1, band, first + s]
            acc[tile] += product(s)
    out[0] = acc[...].astype(out.dtype)


def regrid(table, where, fields, land, parts, part_slots, own, previous, band_count, tiles):
    rows, cells = fields.shape[1], parts[0].shape[-1]
    whole = lambda a: pl.BlockSpec(a.shape, lambda i, t, w, n=a.ndim: (0,) * n)
    part_specs = []
    for part in parts:
        if own:
            part_specs.append(pl.BlockSpec((1,) + part.shape[1:], lambda i, t, w: (w[0], 0, 0, 0)))
        else:
            part_specs.append(whole(part))
    in_specs = [whole(fields), whole(land)] + part_specs
    operands = [fields, land] + list(parts)
    aliases = {}
    if previous is not None:
        aliases = {2 + len(operands): 0}
        in_specs.append(pl.BlockSpec(memory_space=pl.ANY))
        operands.append(previous)
    total = sum(part_slots)
    return pl.pallas_call(
        functools.partial(regrid_kernel, tuple(part_slots)),
        out_shape=jax.ShapeDtypeStruct((band_count, tiles, rows, cells), jnp.bfloat16),
        grid_spec=pltpu.PrefetchScalarGridSpec(
            num_scalar_prefetch=2,
            grid=(1,),
            in_specs=in_specs,
            out_specs=pl.BlockSpec((1, tiles, rows, cells), lambda i, t, w: (w[0], 0, 0, 0)),
            scratch_shapes=[pltpu.VMEM((tiles, rows, cells), jnp.float32)],
        ),
        input_output_aliases=aliases,
        cost_estimate=pl.CostEstimate(
            flops=2 * total * rows * cells * cells, bytes_accessed=6 << 20, transcendentals=0
        ),
        compiler_params=pltpu.CompilerParams(vmem_limit_bytes=24 << 20),
    )(table, where, *operands)


def other(x, axis):
    return lax.ppermute(x, axis, [(0, 1), (1, 0)])


def per_device(
    ocean_fields,
    ocean_dest,
    ocean_weights,
    ocean_tiles,
    atmos_fields,
    atmos_dest,
    atmos_weights,
    atmos_tiles,
    land_fraction,
    embed_weight,
    embed_bias,
    embed_gain,
):
    nb = lax.axis_size("band")
    nv = lax.axis_size("var")
    ng = lax.axis_size("grp")
    rep = nv * ng
    cap = ocean_weights.shape[3]
    cells = ocean_weights.shape[-1]
    block_count, steps, local_vars, _ = ocean_fields.shape
    patches = land_fraction.shape[2]
    tiles = 2 * patches
    slots = 2 * cap
    me = lax.axis_index("band")
    x, y = lax.axis_index("var"), lax.axis_index("grp")
    quarter = y * nv + x

    embed_other = other(embed_weight, "sub")

    ocean_w = ocean_weights.reshape(nb, cap, cells, cells)
    atmos_w = atmos_weights.reshape(nb, cap, cells, cells)
    both = jnp.concatenate([ocean_w, atmos_w], axis=1).reshape(nb, slots * cells, cells)
    share_rows = slots * cells // rep

    tile_ids = jnp.concatenate([ocean_tiles.reshape(nb, cap), atmos_tiles.reshape(nb, cap)], axis=1)
    flat = tile_ids.reshape(-1).astype(jnp.float32)
    tile_rows = -(-flat.shape[0] // cells)
    flat = jnp.pad(flat, (0, tile_rows * cells - flat.shape[0])).reshape(tile_rows, cells)
    meta = lax.all_gather(
        jnp.concatenate([land_fraction.reshape(tiles, cells), flat], axis=0), "band", axis=0
    )
    land_all = meta[:, :tiles]
    land_all = jnp.concatenate(
        [1.0 - land_all, land_all, jnp.zeros((nb, 8, cells), jnp.float32)], axis=1
    )
    tile_all = meta[:, tiles:].reshape(nb, -1)[:, : nb * slots].reshape(nb, nb, slots)
    tile_all = lax.dynamic_index_in_dim(tile_all, me, 1, keepdims=False).astype(jnp.int32)
    ocean_block, ocean_used = slot_tables(ocean_dest, nb, cap)
    atmos_block, atmos_used = slot_tables(atmos_dest, nb, cap)
    block_all = jnp.concatenate([ocean_block, atmos_block + block_count], axis=1)
    used_all = jnp.concatenate([ocean_used, atmos_used], axis=1)
    grid_row = jnp.where(jnp.arange(slots) < cap, 0, tiles)[None, :]
    scale_all = jnp.where(used_all, tile_all + grid_row, 2 * tiles)
    table = jnp.stack([block_all, tile_all, scale_all]).astype(jnp.int32)
    fields = jnp.concatenate([ocean_fields, atmos_fields], axis=0).reshape(
        2 * block_count, steps * local_vars, cells
    )

    call = functools.partial(regrid, band_count=nb, tiles=tiles)
    own_where = jnp.stack([me, jnp.int32(0), jnp.int32(cap)]).astype(jnp.int32)
    partial_rows = call(
        table, own_where, fields, land_all, [ocean_w, atmos_w], [cap, cap], True, None
    )
    order = [1, nb - 1] + list(range(2, nb - 1))
    for shift in order[: nb - 1]:
        target = (me + shift) % nb
        piece = lax.dynamic_slice(
            both, (target, quarter * share_rows, 0), (1, share_rows, cells)
        )[0]
        piece = lax.ppermute(piece, "band", [(b, (b + shift) % nb) for b in range(nb)])
        band = (me - shift) % nb
        if nv == 2 and ng == 2 and slots % rep == 0:
            each = slots // rep
            head = (each + 1) // 2
            piece = piece.reshape(each, cells, cells)
            by_x = other(piece, "var")
            by_y = other(piece, "grp")
            on_y = other(by_x[:head], "grp")
            on_x = other(by_y[head:], "var")
            qx = y * nv + (1 - x)
            qy = (1 - y) * nv + x
            qd = (1 - y) * nv + (1 - x)
            parts = [piece, by_x, by_y, on_y, on_x]
            sizes = [each, each, each, head, each - head]
            firsts = [quarter * each, qx * each, qy * each, qd * each, qd * each + head]
        else:
            parts = [
                lax.all_gather(piece, REPL, axis=0, tiled=True).reshape(slots, cells, cells)
            ]
            sizes, firsts = [slots], [jnp.int32(0)]
        where = jnp.stack([band] + firsts).astype(jnp.int32)
        partial_rows = call(
            table, where, fields, land_all, parts, sizes, False, partial_rows
        )

    share, local_steps = patches // nv, steps // nb
    rows = partial_rows.reshape(nb, nv, share, 2, nb, local_steps, local_vars, cells)
    rows = rows.transpose(4, 1, 2, 0, 5, 6, 3, 7)
    rows = rows.reshape(-1, 2, local_vars // 2 * 2 * cells)
    sub = lax.axis_index("sub")
    mine = lax.dynamic_index_in_dim(rows, sub, 1, keepdims=False)
    theirs = lax.dynamic_index_in_dim(rows, 1 - sub, 1, keepdims=False)
    summed = jnp.dot(mine, embed_weight, preferred_element_type=jnp.float32)
    summed = summed + jnp.dot(theirs, embed_other, preferred_element_type=jnp.float32)
    width = summed.shape[-1]
    sent = summed.astype(jnp.bfloat16).reshape(nb * nv, -1, width)
    got = lax.all_to_all(sent, ("band", "var"), split_axis=0, concat_axis=0, tiled=True)
    shifted = jnp.sum(got.astype(jnp.float32), axis=0) + embed_bias
    inverse = lax.rsqrt(jnp.mean(shifted * shifted, axis=-1, keepdims=True) + 1e-05)
    finished = (shifted * inverse * embed_gain).astype(jnp.bfloat16)
    return finished.reshape(1, share, nb, local_steps, width)


def solution(mesh):
    in_specs = (
        P(("grp", "band", "sub"), None, "var", None),
        P(("band", "sub"), None),
        P("band", "sub", None, None, None, None),
        P("band", "sub", None, None),
        P(("grp", "band", "sub"), None, "var", None),
        P(("band", "sub"), None),
        P("band", "sub", None, None, None, None),
        P("band", "sub", None, None),
        P("band", "sub", None, None, None),
        P(("var", "sub"), None),
        P(),
        P(),
    )
    out_specs = P("sub", "var", None, ("grp", "band"), None)
    return jax.shard_map(
        per_device, mesh=mesh, in_specs=in_specs, out_specs=out_specs, check_vma=False
    )
```

```python
import functools

import jax
import jax.numpy as jnp
from jax import lax
from jax.experimental import pallas as pl
from jax.experimental.pallas import tpu as pltpu
from jax.sharding import PartitionSpec as P

REPL = ("grp", "var")
META = 48


def slot_tables(dest, band_count, cap):
    count = dest.shape[0]
    serial = jnp.arange(count, dtype=jnp.int32)
    band_of = dest[:, 0]
    earlier = (band_of[:, None] == band_of[None, :]) & (serial[None, :] < serial[:, None])
    position = jnp.sum(earlier.astype(jnp.int32), axis=1)
    slot = band_of * cap + position
    hit = slot[None, :] == jnp.arange(band_count * cap, dtype=jnp.int32)[:, None]
    block = jnp.sum(jnp.where(hit, serial[None, :], 0), axis=1)
    used = jnp.any(hit, axis=1)
    return block.reshape(band_count, cap), used.reshape(band_count, cap)


def regrid_kernel(own, per_part, table, where, fields, *refs):
    out, scale = refs[-2], refs[-1]
    cells = fields.shape[-1]
    halves, _, half_tiles = out.shape[:3]
    tiles = halves * half_tiles
    if own:
        ocean, atmos, land_ref = refs[:3]
        land = land_ref[...]
        part = lambda at, s: (ocean, atmos)[at][0, s]
        part_count = 2
    else:
        parts = refs[0]
        first = per_part * cells
        part = lambda at, s: parts[at, pl.ds(s * cells, cells), :]
        part_count = parts.shape[0]
        if len(refs) > 1 and refs[1].shape == (META, cells):
            meta, first = refs[1], 0
            rows = meta[pl.ds(0, 2 * tiles), :].astype(jnp.float32)
        else:
            rows = parts[0, pl.ds(first, 2 * tiles), :].astype(jnp.float32)
        land = rows[:tiles] + rows[tiles:]
    scale[pl.ds(0, tiles), :] = 1.0 - land
    scale[pl.ds(tiles, tiles), :] = land
    scale[pl.ds(2 * tiles, 8), :] = jnp.zeros((8, cells), jnp.float32)
    out[...] = jnp.zeros_like(out)
    for at in range(part_count):
        for s in range(per_part):
            slot = at * per_part + s
            tile = table[1, slot]
            dense = jnp.dot(fields[table[0, slot]], part(at, s), preferred_element_type=jnp.float32)
            out[tile // half_tiles, 0, tile % half_tiles] += (
                dense * scale[pl.ds(table[2, slot], 1), :]
            )


def regrid(table, where, fields, operands, own, per_part, previous, shape):
    rows, cells = fields.shape[1:]
    whole = lambda a: pl.BlockSpec(a.shape, lambda i, t, w, n=a.ndim: (0,) * n)
    in_specs = [whole(fields)]
    for a in operands:
        if own and a.ndim == 4:
            in_specs.append(pl.BlockSpec((1,) + a.shape[1:], lambda i, t, w: (w[0], 0, 0, 0)))
        else:
            in_specs.append(whole(a))
    operands = [fields] + list(operands)
    aliases = {}
    if previous is not None:
        aliases = {2 + len(operands): 0}
        in_specs.append(pl.BlockSpec(memory_space=pl.ANY))
        operands.append(previous)
    halves, bands, half_tiles = shape
    total = table.shape[1]
    return pl.pallas_call(
        functools.partial(regrid_kernel, own, per_part),
        out_shape=jax.ShapeDtypeStruct(shape + (rows, cells), jnp.float32),
        grid_spec=pltpu.PrefetchScalarGridSpec(
            num_scalar_prefetch=2,
            grid=(1,),
            in_specs=in_specs,
            out_specs=pl.BlockSpec(
                (halves, 1, half_tiles, rows, cells), lambda i, t, w: (0, w[0], 0, 0, 0)
            ),
            scratch_shapes=[pltpu.VMEM((2 * halves * half_tiles + 8, cells), jnp.float32)],
        ),
        input_output_aliases=aliases,
        cost_estimate=pl.CostEstimate(
            flops=2 * total * rows * cells * cells, bytes_accessed=6 << 20, transcendentals=0
        ),
        compiler_params=pltpu.CompilerParams(vmem_limit_bytes=24 << 20),
    )(table, where, *operands)


def embed_kernel(steps, sub, partial, mine, theirs, out, total, left, right):
    at = pl.program_id(0)
    cells = partial.shape[1]
    step_rows = mine.shape[0]
    step_vars = step_rows // (2 * cells)
    half_vars = step_vars * pl.num_programs(0)
    stride = 2 * steps * 2 * half_vars
    block = out.shape[0] * out.shape[1] // steps
    for x_ref, half in ((left, sub[0]), (right, 1 - sub[0])):
        for v in range(step_vars):
            for q in range(2):
                for t in range(steps):
                    start = q * steps * 2 * half_vars + t * 2 * half_vars
                    start = start + half * half_vars + at * step_vars + v
                    x_ref[pl.ds(t * block, block), pl.ds((v * 2 + q) * cells, cells)] = partial[
                        pl.ds(start, block, stride), :
                    ].astype(x_ref.dtype)

    @pl.when(at == 0)
    def _():
        total[...] = jnp.zeros_like(total)

    total[...] += jnp.dot(left[...], mine[...], preferred_element_type=jnp.float32) + jnp.dot(
        right[...], theirs[...], preferred_element_type=jnp.float32
    )

    @pl.when(at == pl.num_programs(0) - 1)
    def _():
        out[...] = total[...].reshape(out.shape).astype(out.dtype)


def embed(partial, sub, mine, theirs, steps, local_vars, chunks):
    cells, width = partial.shape[-1], mine.shape[-1]
    half_vars = local_vars // 2
    step_vars = 2 if half_vars % 2 == 0 else 1
    grid = half_vars // step_vars
    step_rows = step_vars * 2 * cells
    flat = partial.reshape(-1, cells)
    rows = flat.shape[0] // (2 * local_vars)
    weight_spec = pl.BlockSpec((step_rows, width), lambda i, s: (i, 0))
    return pl.pallas_call(
        functools.partial(embed_kernel, steps),
        out_shape=jax.ShapeDtypeStruct((chunks, rows // chunks, width), jnp.bfloat16),
        grid_spec=pltpu.PrefetchScalarGridSpec(
            num_scalar_prefetch=1,
            grid=(grid,),
            in_specs=[
                pl.BlockSpec(flat.shape, lambda i, s: (0, 0)),
                weight_spec,
                weight_spec,
            ],
            out_specs=pl.BlockSpec((chunks, rows // chunks, width), lambda i, s: (0, 0, 0)),
            scratch_shapes=[
                pltpu.VMEM((rows, width), jnp.float32),
                pltpu.VMEM((rows, step_rows), jnp.bfloat16),
                pltpu.VMEM((rows, step_rows), jnp.bfloat16),
            ],
        ),
        cost_estimate=pl.CostEstimate(
            flops=4 * rows * mine.shape[0] * width,
            bytes_accessed=4 * mine.shape[0] * width,
            transcendentals=0,
        ),
        compiler_params=pltpu.CompilerParams(
            vmem_limit_bytes=56 << 20 if rows > 1024 else 24 << 20
        ),
    )(sub, flat, mine, theirs)


def per_device(
    ocean_fields,
    ocean_dest,
    ocean_weights,
    ocean_tiles,
    atmos_fields,
    atmos_dest,
    atmos_weights,
    atmos_tiles,
    land_fraction,
    embed_weight,
    embed_bias,
    embed_gain,
):
    nb = lax.axis_size("band")
    nv = lax.axis_size("var")
    ng = lax.axis_size("grp")
    rep = nv * ng
    cap = ocean_weights.shape[3]
    cells = ocean_weights.shape[-1]
    block_count, steps, local_vars, _ = ocean_fields.shape
    patches = land_fraction.shape[2]
    tiles = 2 * patches
    slots = 2 * cap
    share = patches // nv
    me = lax.axis_index("band")
    x, y = lax.axis_index("var"), lax.axis_index("grp")
    quarter = y * nv + x

    embed_other = lax.ppermute(embed_weight, "sub", [(0, 1), (1, 0)])

    ocean_w = ocean_weights.reshape(nb, cap, cells, cells)
    atmos_w = atmos_weights.reshape(nb, cap, cells, cells)
    aligned = ng == 2 and cap % nv == 0
    share_rows = slots * cells // rep
    if not aligned:
        both = jnp.concatenate([ocean_w, atmos_w], axis=1).reshape(nb, slots * cells, cells)

    def share_of(target):
        if aligned:
            each = cap // nv
            start, size = (target, x * each, 0, 0), (1, each, cells, cells)
            piece = jnp.where(
                y == 0,
                lax.dynamic_slice(ocean_w, start, size),
                lax.dynamic_slice(atmos_w, start, size),
            )
            return piece.reshape(share_rows, cells)
        return lax.dynamic_slice(
            both, (target, quarter * share_rows, 0), (1, share_rows, cells)
        )[0]

    land = land_fraction.reshape(tiles, cells)
    high = lax.reduce_precision(land, 8, 7)
    low = (land - high).astype(jnp.bfloat16)
    tile_ids = jnp.concatenate([ocean_tiles.reshape(nb, cap), atmos_tiles.reshape(nb, cap)], axis=1)
    tile_rows = jnp.pad(tile_ids.astype(jnp.bfloat16), ((0, 0), (0, cells - slots)))

    def meta_of(target):
        row = lax.dynamic_slice(tile_rows, (target, 0), (1, cells))
        return jnp.concatenate(
            [high.astype(jnp.bfloat16), low, jnp.broadcast_to(row, (META - 2 * tiles, cells))]
        )

    ocean_block, ocean_used = slot_tables(ocean_dest, nb, cap)
    atmos_block, atmos_used = slot_tables(atmos_dest, nb, cap)
    block_all = jnp.concatenate([ocean_block, atmos_block + block_count], axis=1)
    used_all = jnp.concatenate([ocean_used, atmos_used], axis=1)
    grid_row = jnp.where(jnp.arange(slots) < cap, 0, tiles)
    fields = jnp.concatenate([ocean_fields, atmos_fields], axis=0).reshape(
        2 * block_count, steps * local_vars, cells
    )

    def table_of(band, tile):
        block = lax.dynamic_index_in_dim(block_all, band, 0, keepdims=False)
        used = lax.dynamic_index_in_dim(used_all, band, 0, keepdims=False)
        scale = jnp.where(used, tile + grid_row, 2 * tiles)
        return jnp.stack([block, tile, scale]).astype(jnp.int32)

    shape = (nv, nb, share * 2)
    own_tile = lax.dynamic_index_in_dim(tile_ids, me, 0, keepdims=False)
    partial = regrid(
        table_of(me, own_tile), me[None], fields, [ocean_w, atmos_w, land], True, cap, None, shape
    )
    order = ([1, nb - 1] + list(range(2, nb - 1)))[: nb - 1]
    gathered, arrived = [], None
    for shift in order:
        target = (me + shift) % nb
        piece = jnp.concatenate([share_of(target), meta_of(target)], axis=0)
        if arrived is not None:
            piece, arrived = lax.optimization_barrier((piece, arrived))
            gathered.append(lax.all_gather(arrived, REPL, axis=0))
        arrived = lax.ppermute(piece, "band", [(b, (b + shift) % nb) for b in range(nb)])
    gathered.append(lax.all_gather(arrived, REPL, axis=0))
    for shift, parts in zip(order, gathered):
        band = (me - shift) % nb
        tile = parts[0, share_rows + 2 * tiles, :slots].astype(jnp.int32)
        table = table_of(band, tile)
        if aligned:
            operands, per_part = [parts], slots // rep
        else:
            operands = [parts[:, :share_rows].reshape(1, slots * cells, cells), parts[0, share_rows:]]
            per_part = slots
        partial = regrid(table, band[None], fields, operands, False, per_part, partial, shape)

    sub = lax.axis_index("sub")
    sent = embed(partial, sub[None], embed_weight, embed_other, steps, local_vars, nb * nv)
    got = lax.all_to_all(sent, ("band", "var"), split_axis=0, concat_axis=0, tiled=True)
    shifted = jnp.sum(got.astype(jnp.float32), axis=0) + embed_bias
    inverse = lax.rsqrt(jnp.mean(shifted * shifted, axis=-1, keepdims=True) + 1e-05)
    finished = (shifted * inverse * embed_gain).astype(jnp.bfloat16)
    width = finished.shape[-1]
    finished = finished.reshape(nb, share, steps // nb, width).transpose(1, 0, 2, 3)
    return finished[None]


def solution(mesh):
    in_specs = (
        P(("grp", "band", "sub"), None, "var", None),
        P(("band", "sub"), None),
        P("band", "sub", None, None, None, None),
        P("band", "sub", None, None),
        P(("grp", "band", "sub"), None, "var", None),
        P(("band", "sub"), None),
        P("band", "sub", None, None, None, None),
        P("band", "sub", None, None),
        P("band", "sub", None, None, None),
        P(("var", "sub"), None),
        P(),
        P(),
    )
    out_specs = P("sub", "var", None, ("grp", "band"), None)
    return jax.shard_map(
        per_device, mesh=mesh, in_specs=in_specs, out_specs=out_specs, check_vma=False
    )
```

```python
import functools

import jax
import jax.numpy as jnp
from jax import lax
from jax.experimental import pallas as pl
from jax.experimental.pallas import tpu as pltpu
from jax.sharding import PartitionSpec as P

REPL = ("grp", "var")


def slot_tables(dest, band_count, cap):
    count = dest.shape[0]
    serial = jnp.arange(count, dtype=jnp.int32)
    band_of = dest[:, 0]
    earlier = (band_of[:, None] == band_of[None, :]) & (serial[None, :] < serial[:, None])
    position = jnp.sum(earlier.astype(jnp.int32), axis=1)
    slot = band_of * cap + position
    hit = slot[None, :] == jnp.arange(band_count * cap, dtype=jnp.int32)[:, None]
    block = jnp.sum(jnp.where(hit, serial[None, :], 0), axis=1)
    used = jnp.any(hit, axis=1)
    return block.reshape(band_count, cap), used.reshape(band_count, cap)


def pack_kernel(shifts, head, each, ocean, atmos, ocean_tiles, atmos_tiles, land, *refs):
    outs, sem = refs[:-1], refs[-1]
    me, bands = lax.axis_index("band"), ocean.shape[0]
    x, y = lax.axis_index("var"), lax.axis_index("grp")
    cells = land.shape[-1]
    tiles = land.shape[0]

    def copies(weights):
        found = []
        for at, shift in enumerate(shifts):
            target = lax.rem(me + shift, bands)
            for half, (first, size) in enumerate(((0, head), (head, each - head))):
                start = pl.multiple_of((x * each + first) * cells, cells)
                found.append(
                    pltpu.make_async_copy(
                        weights.at[target, pl.ds(start, size * cells), :],
                        outs[2 * at + half].at[pl.ds(0, size * cells), :],
                        sem.at[2 * at + half],
                    )
                )
        return found

    @pl.when(y == 0)
    def _():
        for copy in copies(ocean):
            copy.start()

    @pl.when(y == 1)
    def _():
        for copy in copies(atmos):
            copy.start()

    fraction = land[...]
    high = fraction.astype(jnp.bfloat16)
    low = (fraction - high.astype(jnp.float32)).astype(jnp.bfloat16)
    cap = ocean_tiles.shape[-1]
    for at, shift in enumerate(shifts):
        target = lax.rem(me + shift, bands)
        out, base = outs[2 * at], head * cells
        out[pl.ds(base, tiles), :] = high
        out[pl.ds(base + tiles, tiles), :] = low
        out[pl.ds(base + 2 * tiles, 32), :] = jnp.zeros((32, cells), jnp.bfloat16)
        for grid, ids in enumerate((ocean_tiles, atmos_tiles)):
            row = ids[pl.ds(target, 1), :].astype(jnp.float32)
            out[pl.ds(base + 2 * tiles + 16 * grid, 16), pl.ds(0, cap)] = jnp.broadcast_to(
                row, (16, cap)
            ).astype(jnp.bfloat16)
    for copy in copies(ocean):
        copy.wait()


def pack(shifts, head, each, ocean, atmos, ocean_tiles, atmos_tiles, land):
    cells = land.shape[-1]
    meta = 2 * land.shape[0] + 32
    any_spec = pl.BlockSpec(memory_space=pltpu.HBM)
    vmem = pl.BlockSpec(memory_space=pltpu.VMEM)
    sizes = [head * cells + meta, (each - head) * cells] * len(shifts)
    return pl.pallas_call(
        functools.partial(pack_kernel, shifts, head, each),
        out_shape=[jax.ShapeDtypeStruct((n, cells), jnp.bfloat16) for n in sizes],
        in_specs=[any_spec, any_spec, vmem, vmem, vmem],
        out_specs=[vmem] * len(sizes),
        scratch_shapes=[pltpu.SemaphoreType.DMA((len(sizes),))],
        cost_estimate=pl.CostEstimate(flops=0, bytes_accessed=2 << 20, transcendentals=0),
        compiler_params=pltpu.CompilerParams(vmem_limit_bytes=16 << 20),
    )(ocean, atmos, ocean_tiles, atmos_tiles, land)


def regrid_kernel(own, steps, meta_at, part_slots, table, where, fields, *refs):
    out, acc, scale = refs[-3:]
    parts, rest = refs[: len(part_slots)], refs[len(part_slots) :]
    rows, cells = fields.shape[1:]
    tiles = acc.shape[0] // rows
    if own:
        land = rest[0][...]
    else:
        meta, first = (parts[0], meta_at) if meta_at else (rest[0], 0)
        high = meta[pl.ds(first, tiles), :].astype(jnp.float32)
        land = high + meta[pl.ds(first + tiles, tiles), :].astype(jnp.float32)
    scale[pl.ds(0, tiles), :] = 1.0 - land
    scale[pl.ds(tiles, tiles), :] = land
    scale[pl.ds(2 * tiles, 8), :] = jnp.zeros((8, cells), jnp.float32)
    acc[...] = jnp.zeros_like(acc)
    for at, (part, size) in enumerate(zip(parts, part_slots)):
        first = where[1 + at]
        for s in range(size):
            slot = first + s
            weight = part[0, s] if own else part[pl.ds(s * cells, cells), :]
            dense = jnp.dot(
                fields[table[0, slot]], weight, preferred_element_type=jnp.float32
            )
            span = pl.ds(pl.multiple_of(table[1, slot] * rows, rows), rows)
            acc[span, :] += dense * scale[pl.ds(table[2, slot], 1), :]
    local_vars = rows // steps
    half_vars = local_vars // 2
    for v in range(local_vars):
        for q in range(2):
            column = (v % half_vars * 2 + q) * cells
            pieces = [
                acc[pl.ds(q * rows + t * local_vars + v, tiles // 2, 2 * rows), :]
                for t in range(steps)
            ]
            out[0, v // half_vars, :, pl.ds(column, cells)] = jnp.concatenate(
                pieces, axis=0
            ).astype(out.dtype)


def regrid(table, where, fields, parts, part_slots, rest, own, meta_at, previous, bands, steps, tiles):
    rows, cells = fields.shape[1:]
    whole = lambda a: pl.BlockSpec(a.shape, lambda i, t, w, n=a.ndim: (0,) * n)
    in_specs = [whole(fields)]
    for part in parts:
        if own:
            in_specs.append(pl.BlockSpec((1,) + part.shape[1:], lambda i, t, w: (w[0], 0, 0, 0)))
        else:
            in_specs.append(whole(part))
    in_specs += [whole(a) for a in rest]
    operands = [fields] + list(parts) + list(rest)
    aliases = {}
    if previous is not None:
        aliases = {2 + len(operands): 0}
        in_specs.append(pl.BlockSpec(memory_space=pl.ANY))
        operands.append(previous)
    row_count, width = steps * tiles // 2, rows // steps // 2 * 2 * cells
    return pl.pallas_call(
        functools.partial(regrid_kernel, own, steps, meta_at, tuple(part_slots)),
        out_shape=jax.ShapeDtypeStruct((bands, 2, row_count, width), jnp.bfloat16),
        grid_spec=pltpu.PrefetchScalarGridSpec(
            num_scalar_prefetch=2,
            grid=(1,),
            in_specs=in_specs,
            out_specs=pl.BlockSpec((1, 2, row_count, width), lambda i, t, w: (w[0], 0, 0, 0)),
            scratch_shapes=[
                pltpu.VMEM((tiles * rows, cells), jnp.float32),
                pltpu.VMEM((2 * tiles + 8, cells), jnp.float32),
            ],
        ),
        input_output_aliases=aliases,
        cost_estimate=pl.CostEstimate(
            flops=2 * sum(part_slots) * rows * cells * cells,
            bytes_accessed=4 << 20,
            transcendentals=0,
        ),
        compiler_params=pltpu.CompilerParams(vmem_limit_bytes=20 << 20),
    )(table, where, *operands)


def embed_kernel(steps, halves, rows_x, mine, theirs, out, total):
    at = pl.program_id(0)
    sub = lax.axis_index("sub")
    bands, _, row_count, width = rows_x.shape

    @pl.when(at == 0)
    def _():
        total[...] = jnp.zeros_like(total)

    left = rows_x[:, sub].reshape(bands * row_count, width)
    right = rows_x[:, 1 - sub].reshape(bands * row_count, width)
    total[...] += jnp.dot(left, mine[...], preferred_element_type=jnp.float32) + jnp.dot(
        right, theirs[...], preferred_element_type=jnp.float32
    )

    @pl.when(at == pl.num_programs(0) - 1)
    def _():
        if out.ndim == 2:
            out[...] = total[...].astype(out.dtype)
        else:
            share = row_count // (steps * halves)
            for chunk in range(steps * halves):
                pieces = [
                    total[pl.ds(b * row_count + chunk * share, share), :] for b in range(bands)
                ]
                out[chunk] = jnp.concatenate(pieces, axis=0).astype(out.dtype)


def embed(rows_x, mine, theirs, steps, halves):
    bands, _, row_count, half_width = rows_x.shape
    width = mine.shape[-1]
    grid = 6 if half_width % (6 * 256) == 0 else 3
    step_rows = half_width // grid
    rows = bands * row_count
    share = row_count // (steps * halves)
    if share % 4 == 0:
        shape = (steps * halves, bands * share, width)
    else:
        shape = (rows, width)
    weight_spec = pl.BlockSpec((step_rows, width), lambda i: (i, 0))
    out = pl.pallas_call(
        functools.partial(embed_kernel, steps, halves),
        out_shape=jax.ShapeDtypeStruct(shape, jnp.bfloat16),
        grid=(grid,),
        in_specs=[
            pl.BlockSpec((bands, 2, row_count, step_rows), lambda i: (0, 0, 0, i)),
            weight_spec,
            weight_spec,
        ],
        out_specs=pl.BlockSpec(shape, lambda i: (0,) * len(shape)),
        scratch_shapes=[pltpu.VMEM((rows, width), jnp.float32)],
        cost_estimate=pl.CostEstimate(
            flops=4 * rows * mine.shape[0] * width,
            bytes_accessed=4 * mine.shape[0] * width,
            transcendentals=0,
        ),
        compiler_params=pltpu.CompilerParams(
            vmem_limit_bytes=(48 if rows > 1024 else 16) << 20
        ),
    )(rows_x, mine, theirs)
    if share % 4:
        out = out.reshape(bands, steps * halves, share, width).transpose(1, 0, 2, 3)
        out = out.reshape(steps * halves, bands * share, width)
    return out


def swap(x, axis):
    return lax.ppermute(x, axis, [(0, 1), (1, 0)])


def per_device(
    ocean_fields,
    ocean_dest,
    ocean_weights,
    ocean_tiles,
    atmos_fields,
    atmos_dest,
    atmos_weights,
    atmos_tiles,
    land_fraction,
    embed_weight,
    embed_bias,
    embed_gain,
):
    nb = lax.axis_size("band")
    nv = lax.axis_size("var")
    ng = lax.axis_size("grp")
    rep = nv * ng
    cap = ocean_weights.shape[3]
    cells = ocean_weights.shape[-1]
    block_count, steps, local_vars, _ = ocean_fields.shape
    patches = land_fraction.shape[2]
    tiles = 2 * patches
    slots = 2 * cap
    share = patches // nv
    me = lax.axis_index("band")
    x, y = lax.axis_index("var"), lax.axis_index("grp")
    quarter = y * nv + x

    embed_other = swap(embed_weight, "sub")

    ocean_w = ocean_weights.reshape(nb, cap, cells, cells)
    atmos_w = atmos_weights.reshape(nb, cap, cells, cells)
    ocean_ids, atmos_ids = ocean_tiles.reshape(nb, cap), atmos_tiles.reshape(nb, cap)
    land = land_fraction.reshape(tiles, cells)
    order = ([1, nb - 1] + list(range(2, nb - 1)))[: nb - 1]
    paired = ng == 2 and nv == 2 and cap % 2 == 0
    each = cap // 2
    head = (each + 1) // 2
    if paired:
        flat = (nb, cap * cells, cells)
        pieces = pack(
            order, head, each, ocean_w.reshape(flat), atmos_w.reshape(flat), ocean_ids, atmos_ids, land
        )

    def slots_of(ocean_dest, atmos_dest):
        ocean_block, ocean_used = slot_tables(ocean_dest, nb, cap)
        atmos_block, atmos_used = slot_tables(atmos_dest, nb, cap)
        return (
            jnp.concatenate([ocean_block, atmos_block + block_count], axis=1),
            jnp.concatenate([ocean_used, atmos_used], axis=1),
        )

    block_all, used_all = slots_of(ocean_dest, atmos_dest)
    grid_row = jnp.where(jnp.arange(slots) < cap, 0, tiles)
    fields = jnp.concatenate([ocean_fields, atmos_fields], axis=0).reshape(
        2 * block_count, steps * local_vars, cells
    )

    def table_of(band, tile):
        block = lax.dynamic_index_in_dim(block_all, band, 0, keepdims=False)
        used = lax.dynamic_index_in_dim(used_all, band, 0, keepdims=False)
        scale = jnp.where(used, tile + grid_row, 2 * tiles)
        return jnp.stack([block, tile, scale]).astype(jnp.int32)

    tile_ids = jnp.concatenate([ocean_ids, atmos_ids], axis=1)
    own_tile = lax.dynamic_index_in_dim(tile_ids, me, 0, keepdims=False)
    where = jnp.stack([me, jnp.int32(0), jnp.int32(cap)])
    call = functools.partial(regrid, bands=nb, steps=steps, tiles=tiles)
    rows_x = call(
        table_of(me, own_tile), where, fields, [ocean_w, atmos_w], [cap, cap], [land], True, 0, None
    )

    if paired:
        sent = []
        for at, piece in enumerate(pieces):
            shift = order[at // 2]
            if at >= 2:
                piece, sent[at - 2] = lax.optimization_barrier((piece, sent[at - 2]))
            sent.append(lax.ppermute(piece, "band", [(b, (b + shift) % nb) for b in range(nb)]))
        for at, shift in enumerate(order):
            parts, sizes, firsts = [], [], []
            for half, (first, size) in enumerate(((0, head), (head, each - head))):
                piece = sent[2 * at + half]
                axes = ("var", "grp") if (half + at) % 2 == 0 else ("grp", "var")
                one, two = swap(piece, axes[0]), swap(piece, axes[1])
                both = swap(one, axes[1])
                by_x, by_y = (one, two) if axes[0] == "var" else (two, one)
                parts += [piece, by_x, by_y, both]
                sizes += [size] * 4
                firsts += [
                    (qy * 2 + qx) * each + first
                    for qx, qy in ((x, y), (1 - x, y), (x, 1 - y), (1 - x, 1 - y))
                ]
            band = (me - shift) % nb
            tail = parts[0][head * cells + 2 * tiles :]
            tile = jnp.concatenate([tail[0, :cap], tail[16, :cap]]).astype(jnp.int32)
            where = jnp.stack([band] + firsts).astype(jnp.int32)
            rows_x = call(
                table_of(band, tile), where, fields, parts, sizes, [], False, head * cells, rows_x
            )
    else:
        both = jnp.concatenate([ocean_w, atmos_w], axis=1).reshape(nb, slots * cells, cells)
        share_rows = slots * cells // rep
        high = lax.reduce_precision(land, 8, 7)
        low = (land - high).astype(jnp.bfloat16)
        tile_rows = jnp.pad(tile_ids.astype(jnp.bfloat16), ((0, 0), (0, cells - slots)))
        for shift in order:
            target, band = (me + shift) % nb, (me - shift) % nb
            piece = lax.dynamic_slice(
                both, (target, quarter * share_rows, 0), (1, share_rows, cells)
            )[0]
            row = lax.dynamic_slice(tile_rows, (target, 0), (1, cells))
            row = jnp.broadcast_to(row, (16, cells))
            piece = jnp.concatenate([piece, high.astype(jnp.bfloat16), low, row], axis=0)
            piece = lax.ppermute(piece, "band", [(b, (b + shift) % nb) for b in range(nb)])
            parts = lax.all_gather(piece, REPL, axis=0)
            meta = parts[0, share_rows:]
            tile = meta[2 * tiles, :slots].astype(jnp.int32)
            parts = parts[:, :share_rows].reshape(slots * cells, cells)
            where = jnp.stack([band, jnp.int32(0)]).astype(jnp.int32)
            rows_x = call(
                table_of(band, tile), where, fields, [parts], [slots], [meta], False, 0, rows_x
            )

    sent = embed(rows_x, embed_weight, embed_other, steps, nv)
    got = lax.all_to_all(sent, ("band", "var"), split_axis=0, concat_axis=0, tiled=True)
    shifted = jnp.sum(got.astype(jnp.float32), axis=0) + embed_bias
    inverse = lax.rsqrt(jnp.mean(shifted * shifted, axis=-1, keepdims=True) + 1e-05)
    finished = (shifted * inverse * embed_gain).astype(jnp.bfloat16)
    width = finished.shape[-1]
    finished = finished.reshape(nb, share, steps // nb, width).transpose(1, 0, 2, 3)
    return finished[None]


def solution(mesh):
    in_specs = (
        P(("grp", "band", "sub"), None, "var", None),
        P(("band", "sub"), None),
        P("band", "sub", None, None, None, None),
        P("band", "sub", None, None),
        P(("grp", "band", "sub"), None, "var", None),
        P(("band", "sub"), None),
        P("band", "sub", None, None, None, None),
        P("band", "sub", None, None),
        P("band", "sub", None, None, None),
        P(("var", "sub"), None),
        P(),
        P(),
    )
    out_specs = P("sub", "var", None, ("grp", "band"), None)
    return jax.shard_map(
        per_device, mesh=mesh, in_specs=in_specs, out_specs=out_specs, check_vma=False
    )
```

```python
import functools

import jax
import jax.numpy as jnp
from jax import lax
from jax.experimental import pallas as pl
from jax.experimental.pallas import tpu as pltpu
from jax.sharding import PartitionSpec as P

REPL = ("grp", "var")


def slot_tables(dest, band_count, cap):
    count = dest.shape[0]
    serial = jnp.arange(count, dtype=jnp.int32)
    band_of = dest[:, 0]
    earlier = (band_of[:, None] == band_of[None, :]) & (serial[None, :] < serial[:, None])
    position = jnp.sum(earlier.astype(jnp.int32), axis=1)
    slot = band_of * cap + position
    hit = slot[None, :] == jnp.arange(band_count * cap, dtype=jnp.int32)[:, None]
    block = jnp.sum(jnp.where(hit, serial[None, :], 0), axis=1)
    used = jnp.any(hit, axis=1)
    return block.reshape(band_count, cap), used.reshape(band_count, cap)


def pack_kernel(pieces, ocean, atmos, weights, tiles_of, land, *refs):
    (ocean_w, atmos_w), (ocean_ids, atmos_ids) = weights, tiles_of
    keep, send, own, outs, sem = refs[0], refs[1], refs[2], refs[3:-1], refs[-1]
    me, bands = lax.axis_index("band"), ocean_w.shape[0]
    x, y = lax.axis_index("var"), lax.axis_index("grp")
    cells, tiles = land.shape[-1], land.shape[0]
    cap = ocean_ids.shape[-1]
    each = cap // 2

    def copies(mine, other, weights):
        pairs = []
        for out, (shift, first, size) in zip(outs, pieces):
            start = pl.multiple_of((x * each + first) * cells, cells)
            target = lax.rem(me + shift, bands)
            pairs.append(
                (
                    weights.at[target, pl.ds(start, size * cells), :],
                    out.at[pl.ds(0, size * cells), :],
                )
            )
        pairs += [(other, send), (mine, keep), (weights.at[me], own)]
        return [pltpu.make_async_copy(a, b, sem.at[i]) for i, (a, b) in enumerate(pairs)]

    @pl.when(y == 0)
    def _():
        for copy in copies(ocean, atmos, ocean_w):
            copy.start()

    @pl.when(y == 1)
    def _():
        for copy in copies(atmos, ocean, atmos_w):
            copy.start()

    fraction = land[...]
    high = fraction.astype(jnp.bfloat16)
    low = (fraction - high.astype(jnp.float32)).astype(jnp.bfloat16)
    for out, (shift, first, size) in zip(outs, pieces):
        if first:
            continue
        target, base = lax.rem(me + shift, bands), size * cells
        out[pl.ds(base, tiles), :] = high
        out[pl.ds(base + tiles, tiles), :] = low
        row = jnp.where(y == 0, ocean_ids[pl.ds(target, 1), :], atmos_ids[pl.ds(target, 1), :])
        row = jnp.broadcast_to(row.astype(jnp.float32), (16, cap)).astype(jnp.bfloat16)
        out[pl.ds(base + 2 * tiles, 16), :] = jnp.zeros((16, cells), jnp.bfloat16)
        out[pl.ds(base + 2 * tiles, 16), pl.ds(0, cap)] = row
    for copy in copies(ocean, atmos, ocean_w):
        copy.wait()


def pack(pieces, ocean, atmos, ocean_w, atmos_w, ocean_ids, atmos_ids, land):
    cells, tiles = land.shape[-1], land.shape[0]
    any_spec = pl.BlockSpec(memory_space=pl.ANY)
    vmem = pl.BlockSpec(memory_space=pltpu.VMEM)
    sizes = [size * cells + (0 if first else 2 * tiles + 16) for _, first, size in pieces]
    shapes = [ocean.shape, ocean.shape, ocean_w.shape[1:]] + [(n, cells) for n in sizes]

    def body(o, a, ow, aw, oi, ai, land, *refs):
        pack_kernel(pieces, o, a, (ow, aw), (oi, ai), land, *refs)

    return pl.pallas_call(
        body,
        out_shape=[jax.ShapeDtypeStruct(shape, jnp.bfloat16) for shape in shapes],
        in_specs=[any_spec] * 4 + [vmem] * 3,
        out_specs=[vmem] * len(shapes),
        scratch_shapes=[pltpu.SemaphoreType.DMA((len(shapes),))],
        cost_estimate=pl.CostEstimate(flops=0, bytes_accessed=6 << 20, transcendentals=0),
        compiler_params=pltpu.CompilerParams(vmem_limit_bytes=60 << 20),
    )(ocean, atmos, ocean_w, atmos_w, ocean_ids, atmos_ids, land)


def regrid_kernel(groups, steps, meta_at, part_slots, table, where, *refs):
    out, acc, scale = refs[-3:]
    fields, refs = refs[:groups], refs[groups:]
    parts, rest = refs[: len(part_slots)], refs[len(part_slots) :]
    rows, cells = fields[0].shape[1:]
    tiles = acc.shape[1] // rows
    if meta_at is None:
        land = rest[0][...]
    else:
        meta = rest[0] if meta_at < 0 else parts[0]
        first = max(meta_at, 0)
        high = meta[pl.ds(first, tiles), :].astype(jnp.float32)
        land = high + meta[pl.ds(first + tiles, tiles), :].astype(jnp.float32)
    scale[pl.ds(0, tiles), :] = 1.0 - land
    scale[pl.ds(tiles, tiles), :] = land
    scale[pl.ds(2 * tiles, 8), :] = jnp.zeros((8, cells), jnp.float32)
    acc[...] = jnp.zeros_like(acc)
    for at, (part, size) in enumerate(zip(parts, part_slots)):
        first = where[1 + at]
        for s in range(size):
            slot = first + s
            block = table[0, slot]
            moved = [f[block] for f in fields]
            moved = moved[0] if groups == 1 else jnp.concatenate(moved, axis=0)
            dense = jnp.dot(
                moved, part[pl.ds(s * cells, cells), :], preferred_element_type=jnp.float32
            )
            dense = dense * scale[pl.ds(table[2, slot], 1), :]
            span = pl.ds(pl.multiple_of(table[1, slot] * rows, rows), rows)
            for g in range(groups):
                acc[g, span, :] += dense[g * rows : (g + 1) * rows]
    local_vars = rows // steps
    half_vars = local_vars // 2
    for g in range(groups):
        for v in range(local_vars):
            for q in range(2):
                column = (v % half_vars * 2 + q) * cells
                pieces = [
                    acc[g, pl.ds(q * rows + t * local_vars + v, tiles // 2, 2 * rows), :]
                    for t in range(steps)
                ]
                out[0, g, v // half_vars, :, pl.ds(column, cells)] = jnp.concatenate(
                    pieces, axis=0
                ).astype(out.dtype)


def regrid(table, where, fields, parts, part_slots, rest, meta_at, previous, bands, steps, tiles):
    groups = len(fields)
    rows, cells = fields[0].shape[1:]
    whole = lambda a: pl.BlockSpec(a.shape, lambda i, t, w, n=a.ndim: (0,) * n)
    operands = list(fields) + list(parts) + list(rest)
    in_specs = [whole(a) for a in operands]
    aliases = {}
    if previous is not None:
        aliases = {2 + len(operands): 0}
        in_specs.append(pl.BlockSpec(memory_space=pl.ANY))
        operands.append(previous)
    row_count, width = steps * tiles // 2, rows // steps // 2 * 2 * cells
    block = (groups, 2, row_count, width)
    return pl.pallas_call(
        functools.partial(regrid_kernel, groups, steps, meta_at, tuple(part_slots)),
        out_shape=jax.ShapeDtypeStruct((bands,) + block, jnp.bfloat16),
        grid_spec=pltpu.PrefetchScalarGridSpec(
            num_scalar_prefetch=2,
            grid=(1,),
            in_specs=in_specs,
            out_specs=pl.BlockSpec((1,) + block, lambda i, t, w: (w[0], 0, 0, 0, 0)),
            scratch_shapes=[
                pltpu.VMEM((groups, tiles * rows, cells), jnp.float32),
                pltpu.VMEM((2 * tiles + 8, cells), jnp.float32),
            ],
        ),
        input_output_aliases=aliases,
        cost_estimate=pl.CostEstimate(
            flops=2 * sum(part_slots) * groups * rows * cells * cells,
            bytes_accessed=4 << 20,
            transcendentals=0,
        ),
        compiler_params=pltpu.CompilerParams(vmem_limit_bytes=20 << 20),
    )(table, where, *operands)


def embed_kernel(steps, halves, rows_x, mine, theirs, out, total):
    at = pl.program_id(0)
    sub, mine_group = lax.axis_index("sub"), lax.axis_index("grp")
    bands, groups, _, row_count, width = rows_x.shape
    rows = bands * groups * row_count

    @pl.when(at == 0)
    def _():
        total[...] = jnp.zeros_like(total)

    left = rows_x[:, :, sub].reshape(rows, width)
    right = rows_x[:, :, 1 - sub].reshape(rows, width)
    total[...] += jnp.dot(left, mine[...], preferred_element_type=jnp.float32) + jnp.dot(
        right, theirs[...], preferred_element_type=jnp.float32
    )

    @pl.when(at == pl.num_programs(0) - 1)
    def _():
        if out.ndim == 2:
            out[...] = total[...].astype(out.dtype)
        else:
            count = steps * halves
            share = row_count // count
            for g in range(groups):
                base = (mine_group if g == 0 else 1 - mine_group) * count if groups > 1 else 0
                for chunk in range(count):
                    pieces = [
                        total[pl.ds((b * groups + g) * row_count + chunk * share, share), :]
                        for b in range(bands)
                    ]
                    out[base + chunk] = jnp.concatenate(pieces, axis=0).astype(out.dtype)


def embed(rows_x, mine, theirs, steps, halves):
    bands, groups, _, row_count, half_width = rows_x.shape
    width = mine.shape[-1]
    grid = 6 if half_width % (6 * 256) == 0 else 3
    step_rows = half_width // grid
    rows = bands * groups * row_count
    chunks = groups * steps * halves
    share = row_count // (steps * halves)
    shape = (chunks, bands * share, width) if share % 4 == 0 else (rows, width)
    weight_spec = pl.BlockSpec((step_rows, width), lambda i: (i, 0))
    out = pl.pallas_call(
        functools.partial(embed_kernel, steps, halves),
        out_shape=jax.ShapeDtypeStruct(shape, jnp.bfloat16),
        grid=(grid,),
        in_specs=[
            pl.BlockSpec((bands, groups, 2, row_count, step_rows), lambda i: (0, 0, 0, 0, i)),
            weight_spec,
            weight_spec,
        ],
        out_specs=pl.BlockSpec(shape, lambda i: (0,) * len(shape)),
        scratch_shapes=[pltpu.VMEM((rows, width), jnp.float32)],
        cost_estimate=pl.CostEstimate(
            flops=4 * rows * mine.shape[0] * width,
            bytes_accessed=4 * mine.shape[0] * width,
            transcendentals=0,
        ),
        compiler_params=pltpu.CompilerParams(
            vmem_limit_bytes=(48 if rows > 1024 else 16) << 20
        ),
    )(rows_x, mine, theirs)
    if share % 4:
        out = out.reshape(bands, chunks, share, width).transpose(1, 0, 2, 3)
        out = out.reshape(chunks, bands * share, width)
    return out


def swap(x, axis):
    return lax.ppermute(x, axis, [(0, 1), (1, 0)])


def per_device(
    ocean_fields,
    ocean_dest,
    ocean_weights,
    ocean_tiles,
    atmos_fields,
    atmos_dest,
    atmos_weights,
    atmos_tiles,
    land_fraction,
    embed_weight,
    embed_bias,
    embed_gain,
):
    nb = lax.axis_size("band")
    nv = lax.axis_size("var")
    ng = lax.axis_size("grp")
    rep = nv * ng
    cap = ocean_weights.shape[3]
    cells = ocean_weights.shape[-1]
    block_count, steps, local_vars, _ = ocean_fields.shape
    patches = land_fraction.shape[2]
    tiles = 2 * patches
    slots = 2 * cap
    share = patches // nv
    me = lax.axis_index("band")
    x, y = lax.axis_index("var"), lax.axis_index("grp")
    quarter = y * nv + x

    embed_other = swap(embed_weight, "sub")

    flat = (nb, cap * cells, cells)
    ocean_w, atmos_w = ocean_weights.reshape(flat), atmos_weights.reshape(flat)
    ocean_ids, atmos_ids = ocean_tiles.reshape(nb, cap), atmos_tiles.reshape(nb, cap)
    land = land_fraction.reshape(tiles, cells)
    blocks = (block_count, steps * local_vars, cells)
    ocean_f, atmos_f = ocean_fields.reshape(blocks), atmos_fields.reshape(blocks)
    order = ([1, nb - 1] + list(range(2, nb - 1)))[: nb - 1]
    call = functools.partial(regrid, bands=nb, steps=steps, tiles=tiles)
    along = lambda shift: [(b, (b + shift) % nb) for b in range(nb)]

    if ng == 2 and nv == 2 and cap % 2 == 0:
        each = cap // 2
        head = (each + 1) // 2
        pieces = []
        for shift in order:
            if 2 * shift == nb:
                pieces += [(shift, 0, head), (shift, head, each - head)]
            else:
                pieces.append((shift, 0, each))
        keep, send, own_w, *packed = pack(
            pieces, ocean_f, atmos_f, ocean_w, atmos_w, ocean_ids, atmos_ids, land
        )
        fields = [keep, swap(send, "grp")]
        dest = jnp.where(y == 0, ocean_dest, atmos_dest)
        block_all, used_all = slot_tables(dest, nb, cap)

        def table_of(band, tile):
            block = lax.dynamic_index_in_dim(block_all, band, 0, keepdims=False)
            used = lax.dynamic_index_in_dim(used_all, band, 0, keepdims=False)
            scale = jnp.where(used, tile + y * tiles, 2 * tiles)
            return jnp.stack([block, tile, scale]).astype(jnp.int32)

        sent = []
        for at, (piece, (shift, _, _)) in enumerate(zip(packed, pieces)):
            if at >= 2:
                piece, sent[at - 2] = lax.optimization_barrier((piece, sent[at - 2]))
            sent.append(lax.ppermute(piece, "band", along(shift)))
        crossed = [swap(piece, "var") for piece in sent]

        ids = jnp.where(y == 0, ocean_ids, atmos_ids)
        own_tile = lax.dynamic_index_in_dim(ids, me, 0, keepdims=False)
        where = jnp.stack([me, jnp.int32(0)])
        rows_x = call(table_of(me, own_tile), where, fields, [own_w], [cap], [land], None, None)
        for shift in order:
            band = (me - shift) % nb
            parts, sizes, firsts = [], [], []
            for piece, across, (of, first, size) in zip(sent, crossed, pieces):
                if of == shift:
                    parts += [piece, across]
                    sizes += [size, size]
                    firsts += [x * each + first, (1 - x) * each + first]
            meta_at = sizes[0] * cells
            tile = parts[0][meta_at + 2 * tiles, :cap].astype(jnp.int32)
            where = jnp.stack([band] + firsts).astype(jnp.int32)
            rows_x = call(table_of(band, tile), where, fields, parts, sizes, [], meta_at, rows_x)
        sent = embed(rows_x, embed_weight, embed_other, steps, nv)
        got = lax.all_to_all(sent, ("grp", "band", "var"), split_axis=0, concat_axis=0, tiled=True)
    else:
        both = jnp.concatenate([ocean_w, atmos_w], axis=1)
        fields = [jnp.concatenate([ocean_f, atmos_f], axis=0)]
        ocean_block, ocean_used = slot_tables(ocean_dest, nb, cap)
        atmos_block, atmos_used = slot_tables(atmos_dest, nb, cap)
        block_all = jnp.concatenate([ocean_block, atmos_block + block_count], axis=1)
        used_all = jnp.concatenate([ocean_used, atmos_used], axis=1)
        grid_row = jnp.where(jnp.arange(slots) < cap, 0, tiles)

        def table_of(band, tile):
            block = lax.dynamic_index_in_dim(block_all, band, 0, keepdims=False)
            used = lax.dynamic_index_in_dim(used_all, band, 0, keepdims=False)
            scale = jnp.where(used, tile + grid_row, 2 * tiles)
            return jnp.stack([block, tile, scale]).astype(jnp.int32)

        tile_ids = jnp.concatenate([ocean_ids, atmos_ids], axis=1)
        own_tile = lax.dynamic_index_in_dim(tile_ids, me, 0, keepdims=False)
        own_w = lax.dynamic_index_in_dim(both, me, 0, keepdims=False)
        where = jnp.stack([me, jnp.int32(0)])
        rows_x = call(table_of(me, own_tile), where, fields, [own_w], [slots], [land], None, None)
        share_rows = slots * cells // rep
        high = lax.reduce_precision(land, 8, 7)
        low = (land - high).astype(jnp.bfloat16)
        tile_rows = jnp.pad(tile_ids.astype(jnp.bfloat16), ((0, 0), (0, cells - slots)))
        for shift in order:
            target, band = (me + shift) % nb, (me - shift) % nb
            piece = lax.dynamic_slice(
                both, (target, quarter * share_rows, 0), (1, share_rows, cells)
            )[0]
            row = lax.dynamic_slice(tile_rows, (target, 0), (1, cells))
            row = jnp.broadcast_to(row, (16, cells))
            piece = jnp.concatenate([piece, high.astype(jnp.bfloat16), low, row], axis=0)
            parts = lax.all_gather(lax.ppermute(piece, "band", along(shift)), REPL, axis=0)
            meta = parts[0, share_rows:]
            tile = meta[2 * tiles, :slots].astype(jnp.int32)
            parts = parts[:, :share_rows].reshape(slots * cells, cells)
            where = jnp.stack([band, jnp.int32(0)])
            rows_x = call(
                table_of(band, tile), where, fields, [parts], [slots], [meta], -1, rows_x
            )
        sent = embed(rows_x, embed_weight, embed_other, steps, nv)
        got = lax.all_to_all(sent, ("band", "var"), split_axis=0, concat_axis=0, tiled=True)
    shifted = jnp.sum(got.astype(jnp.float32), axis=0) + embed_bias
    inverse = lax.rsqrt(jnp.mean(shifted * shifted, axis=-1, keepdims=True) + 1e-05)
    finished = (shifted * inverse * embed_gain).astype(jnp.bfloat16)
    width = finished.shape[-1]
    finished = finished.reshape(nb, share, steps // nb, width).transpose(1, 0, 2, 3)
    return finished[None]


def solution(mesh):
    in_specs = (
        P(("grp", "band", "sub"), None, "var", None),
        P(("band", "sub"), None),
        P("band", "sub", None, None, None, None),
        P("band", "sub", None, None),
        P(("grp", "band", "sub"), None, "var", None),
        P(("band", "sub"), None),
        P("band", "sub", None, None, None, None),
        P("band", "sub", None, None),
        P("band", "sub", None, None, None),
        P(("var", "sub"), None),
        P(),
        P(),
    )
    out_specs = P("sub", "var", None, ("grp", "band"), None)
    return jax.shard_map(
        per_device, mesh=mesh, in_specs=in_specs, out_specs=out_specs, check_vma=False
    )
```

```python
import functools

import jax
import jax.numpy as jnp
from jax import lax
from jax.experimental import pallas as pl
from jax.experimental.pallas import tpu as pltpu
from jax.sharding import PartitionSpec as P

REPL = ("grp", "var")


def slot_tables(dest, band_count, cap):
    count = dest.shape[0]
    serial = jnp.arange(count, dtype=jnp.int32)
    band_of = dest[:, 0]
    earlier = (band_of[:, None] == band_of[None, :]) & (serial[None, :] < serial[:, None])
    position = jnp.sum(earlier.astype(jnp.int32), axis=1)
    slot = band_of * cap + position
    hit = slot[None, :] == jnp.arange(band_count * cap, dtype=jnp.int32)[:, None]
    block = jnp.sum(jnp.where(hit, serial[None, :], 0), axis=1)
    used = jnp.any(hit, axis=1)
    return block.reshape(band_count, cap), used.reshape(band_count, cap)


def pack_kernel(pieces, *refs):
    ocean, atmos, ocean_w, atmos_w, ocean_ids, atmos_ids, land, send = refs[:8]
    outs, metas, sem = refs[8:-2], refs[-2], refs[-1]
    me, bands = lax.axis_index("band"), ocean_w.shape[0]
    x, y = lax.axis_index("var"), lax.axis_index("grp")
    cells, tiles = land.shape[-1], land.shape[0]
    cap = ocean_ids.shape[-1]
    each = cap // 2

    def copies(weights, fields):
        found = []
        for at, (out, (shift, first, size)) in enumerate(zip(outs, pieces)):
            start = pl.multiple_of((x * each + first) * cells, cells)
            target = lax.rem(me + shift, bands)
            found.append(
                pltpu.make_async_copy(
                    weights.at[target, pl.ds(start, size * cells), :],
                    out.at[pl.ds(0, size * cells), :],
                    sem.at[at],
                )
            )
        return found + [pltpu.make_async_copy(fields, send, sem.at[len(pieces)])]

    @pl.when(y == 0)
    def _():
        for copy in copies(ocean_w, atmos):
            copy.start()

    @pl.when(y == 1)
    def _():
        for copy in copies(atmos_w, ocean):
            copy.start()

    fraction = land[...]
    high = fraction.astype(jnp.bfloat16)
    low = (fraction - high.astype(jnp.float32)).astype(jnp.bfloat16)
    done = copies(ocean_w, atmos)
    for at, (out, (shift, first, size)) in enumerate(zip(outs, pieces)):
        if first:
            continue
        target = lax.rem(me + shift, bands)
        metas[at, pl.ds(0, tiles), :] = high
        metas[at, pl.ds(tiles, tiles), :] = low
        row = jnp.where(y == 0, ocean_ids[pl.ds(target, 1), :], atmos_ids[pl.ds(target, 1), :])
        row = jnp.broadcast_to(row.astype(jnp.float32), (16, cap)).astype(jnp.bfloat16)
        metas[at, pl.ds(2 * tiles, 16), :] = jnp.zeros((16, cells), jnp.bfloat16)
        metas[at, pl.ds(2 * tiles, 16), pl.ds(0, cap)] = row
        copy = pltpu.make_async_copy(
            metas.at[at],
            out.at[pl.ds(size * cells, metas.shape[1]), :],
            sem.at[len(pieces) + 1 + at],
        )
        copy.start()
        done.append(copy)
    for copy in done:
        copy.wait()


def pack(pieces, ocean, atmos, ocean_w, atmos_w, ocean_ids, atmos_ids, land):
    cells, tiles = land.shape[-1], land.shape[0]
    any_spec = pl.BlockSpec(memory_space=pl.ANY)
    vmem = pl.BlockSpec(memory_space=pltpu.VMEM)
    meta = 2 * tiles + 16
    sizes = [size * cells + (0 if first else meta) for _, first, size in pieces]
    shapes = [ocean.shape] + [(n, cells) for n in sizes]
    return pl.pallas_call(
        functools.partial(pack_kernel, pieces),
        out_shape=[jax.ShapeDtypeStruct(shape, jnp.bfloat16) for shape in shapes],
        in_specs=[any_spec] * 4 + [vmem] * 3,
        out_specs=[any_spec] * len(shapes),
        scratch_shapes=[
            pltpu.VMEM((len(pieces), meta, cells), jnp.bfloat16),
            pltpu.SemaphoreType.DMA((2 * len(pieces) + 1,)),
        ],
        cost_estimate=pl.CostEstimate(flops=0, bytes_accessed=4 << 20, transcendentals=0),
        compiler_params=pltpu.CompilerParams(vmem_limit_bytes=60 << 20),
    )(ocean, atmos, ocean_w, atmos_w, ocean_ids, atmos_ids, land)


def keep_kernel(ocean, atmos, ocean_w, atmos_w, keep, own, sem):
    me, y = lax.axis_index("band"), lax.axis_index("grp")

    def copies(fields, weights):
        return [
            pltpu.make_async_copy(fields, keep, sem.at[0]),
            pltpu.make_async_copy(weights.at[me], own, sem.at[1]),
        ]

    @pl.when(y == 0)
    def _():
        for copy in copies(ocean, ocean_w):
            copy.start()

    @pl.when(y == 1)
    def _():
        for copy in copies(atmos, atmos_w):
            copy.start()

    for copy in copies(ocean, ocean_w):
        copy.wait()


def keep_own(ocean, atmos, ocean_w, atmos_w):
    any_spec = pl.BlockSpec(memory_space=pl.ANY)
    shapes = [ocean.shape, ocean_w.shape[1:]]
    return pl.pallas_call(
        keep_kernel,
        out_shape=[jax.ShapeDtypeStruct(shape, jnp.bfloat16) for shape in shapes],
        in_specs=[any_spec] * 4,
        out_specs=[any_spec] * 2,
        scratch_shapes=[pltpu.SemaphoreType.DMA((2,))],
        cost_estimate=pl.CostEstimate(flops=0, bytes_accessed=3 << 20, transcendentals=0),
        compiler_params=pltpu.CompilerParams(vmem_limit_bytes=60 << 20),
    )(ocean, atmos, ocean_w, atmos_w)


def regrid_kernel(groups, steps, meta_at, part_slots, table, where, *refs):
    out, acc, scale = refs[-3:]
    fields, refs = refs[:groups], refs[groups:]
    parts, rest = refs[: len(part_slots)], refs[len(part_slots) :]
    rows, cells = fields[0].shape[1:]
    tiles = acc.shape[1] // rows
    if meta_at is None:
        land = rest[0][...]
    else:
        meta = rest[0] if meta_at < 0 else parts[0]
        first = max(meta_at, 0)
        high = meta[pl.ds(first, tiles), :].astype(jnp.float32)
        land = high + meta[pl.ds(first + tiles, tiles), :].astype(jnp.float32)
    scale[pl.ds(0, tiles), :] = 1.0 - land
    scale[pl.ds(tiles, tiles), :] = land
    scale[pl.ds(2 * tiles, 8), :] = jnp.zeros((8, cells), jnp.float32)
    acc[...] = jnp.zeros_like(acc)
    for at, (part, size) in enumerate(zip(parts, part_slots)):
        first = where[1 + at]
        for s in range(size):
            slot = first + s
            block = table[0, slot]
            moved = [f[block] for f in fields]
            moved = moved[0] if groups == 1 else jnp.concatenate(moved, axis=0)
            dense = jnp.dot(
                moved, part[pl.ds(s * cells, cells), :], preferred_element_type=jnp.float32
            )
            dense = dense * scale[pl.ds(table[2, slot], 1), :]
            span = pl.ds(pl.multiple_of(table[1, slot] * rows, rows), rows)
            for g in range(groups):
                acc[g, span, :] += dense[g * rows : (g + 1) * rows]
    local_vars = rows // steps
    half_vars = local_vars // 2
    for g in range(groups):
        for v in range(local_vars):
            for q in range(2):
                column = (v % half_vars * 2 + q) * cells
                pieces = [
                    acc[g, pl.ds(q * rows + t * local_vars + v, tiles // 2, 2 * rows), :]
                    for t in range(steps)
                ]
                out[0, g, v // half_vars, :, pl.ds(column, cells)] = jnp.concatenate(
                    pieces, axis=0
                ).astype(out.dtype)


def regrid(
    table, where, fields, parts, part_slots, rest, meta_at, previous, bands, steps, tiles, total, at=0
):
    groups = len(fields)
    rows, cells = fields[0].shape[1:]
    whole = lambda a: pl.BlockSpec(a.shape, lambda i, t, w, n=a.ndim: (0,) * n)
    operands = list(fields) + list(parts) + list(rest)
    in_specs = [whole(a) for a in operands]
    aliases = {}
    if previous is not None:
        aliases = {2 + len(operands): 0}
        in_specs.append(pl.BlockSpec(memory_space=pl.ANY))
        operands.append(previous)
    row_count, width = steps * tiles // 2, rows // steps // 2 * 2 * cells
    block = (2, row_count, width)
    return pl.pallas_call(
        functools.partial(regrid_kernel, groups, steps, meta_at, tuple(part_slots)),
        out_shape=jax.ShapeDtypeStruct((bands, total) + block, jnp.bfloat16),
        grid_spec=pltpu.PrefetchScalarGridSpec(
            num_scalar_prefetch=2,
            grid=(1,),
            in_specs=in_specs,
            out_specs=pl.BlockSpec((1, groups) + block, lambda i, t, w: (w[0], at, 0, 0, 0)),
            scratch_shapes=[
                pltpu.VMEM((groups, tiles * rows, cells), jnp.float32),
                pltpu.VMEM((2 * tiles + 8, cells), jnp.float32),
            ],
        ),
        input_output_aliases=aliases,
        cost_estimate=pl.CostEstimate(
            flops=2 * sum(part_slots) * groups * rows * cells * cells,
            bytes_accessed=4 << 20,
            transcendentals=0,
        ),
        compiler_params=pltpu.CompilerParams(vmem_limit_bytes=20 << 20),
    )(table, where, *operands)


def embed_kernel(steps, halves, rows_x, mine, theirs, out, total):
    at = pl.program_id(0)
    sub, mine_group = lax.axis_index("sub"), lax.axis_index("grp")
    bands, groups, _, row_count, width = rows_x.shape
    rows = bands * groups * row_count

    @pl.when(at == 0)
    def _():
        total[...] = jnp.zeros_like(total)

    left = rows_x[:, :, sub].reshape(rows, width)
    right = rows_x[:, :, 1 - sub].reshape(rows, width)
    total[...] += jnp.dot(left, mine[...], preferred_element_type=jnp.float32) + jnp.dot(
        right, theirs[...], preferred_element_type=jnp.float32
    )

    @pl.when(at == pl.num_programs(0) - 1)
    def _():
        if out.ndim == 2:
            out[...] = total[...].astype(out.dtype)
        else:
            count = steps * halves
            share = row_count // count
            for g in range(groups):
                base = (mine_group if g == 0 else 1 - mine_group) * count if groups > 1 else 0
                for chunk in range(count):
                    pieces = [
                        total[pl.ds((b * groups + g) * row_count + chunk * share, share), :]
                        for b in range(bands)
                    ]
                    out[base + chunk] = jnp.concatenate(pieces, axis=0).astype(out.dtype)


def embed(rows_x, mine, theirs, steps, halves):
    bands, groups, _, row_count, half_width = rows_x.shape
    width = mine.shape[-1]
    grid = 6 if half_width % (6 * 256) == 0 else 3
    step_rows = half_width // grid
    rows = bands * groups * row_count
    chunks = groups * steps * halves
    share = row_count // (steps * halves)
    shape = (chunks, bands * share, width) if share % 4 == 0 else (rows, width)
    weight_spec = pl.BlockSpec((step_rows, width), lambda i: (i, 0))
    out = pl.pallas_call(
        functools.partial(embed_kernel, steps, halves),
        out_shape=jax.ShapeDtypeStruct(shape, jnp.bfloat16),
        grid=(grid,),
        in_specs=[
            pl.BlockSpec((bands, groups, 2, row_count, step_rows), lambda i: (0, 0, 0, 0, i)),
            weight_spec,
            weight_spec,
        ],
        out_specs=pl.BlockSpec(shape, lambda i: (0,) * len(shape)),
        scratch_shapes=[pltpu.VMEM((rows, width), jnp.float32)],
        cost_estimate=pl.CostEstimate(
            flops=4 * rows * mine.shape[0] * width,
            bytes_accessed=4 * mine.shape[0] * width,
            transcendentals=0,
        ),
        compiler_params=pltpu.CompilerParams(
            vmem_limit_bytes=(48 if rows > 1024 else 16) << 20
        ),
    )(rows_x, mine, theirs)
    if share % 4:
        out = out.reshape(bands, chunks, share, width).transpose(1, 0, 2, 3)
        out = out.reshape(chunks, bands * share, width)
    return out


def swap(x, axis):
    return lax.ppermute(x, axis, [(0, 1), (1, 0)])


def per_device(
    ocean_fields,
    ocean_dest,
    ocean_weights,
    ocean_tiles,
    atmos_fields,
    atmos_dest,
    atmos_weights,
    atmos_tiles,
    land_fraction,
    embed_weight,
    embed_bias,
    embed_gain,
):
    nb = lax.axis_size("band")
    nv = lax.axis_size("var")
    ng = lax.axis_size("grp")
    rep = nv * ng
    cap = ocean_weights.shape[3]
    cells = ocean_weights.shape[-1]
    block_count, steps, local_vars, _ = ocean_fields.shape
    patches = land_fraction.shape[2]
    tiles = 2 * patches
    slots = 2 * cap
    share = patches // nv
    me = lax.axis_index("band")
    x, y = lax.axis_index("var"), lax.axis_index("grp")
    quarter = y * nv + x

    flat = (nb, cap * cells, cells)
    ocean_w, atmos_w = ocean_weights.reshape(flat), atmos_weights.reshape(flat)
    ocean_ids, atmos_ids = ocean_tiles.reshape(nb, cap), atmos_tiles.reshape(nb, cap)
    land = land_fraction.reshape(tiles, cells)
    blocks = (block_count, steps * local_vars, cells)
    ocean_f, atmos_f = ocean_fields.reshape(blocks), atmos_fields.reshape(blocks)
    order = ([1, nb - 1] + list(range(2, nb - 1)))[: nb - 1]
    call = functools.partial(regrid, bands=nb, steps=steps, tiles=tiles, total=1)
    along = lambda shift: [(b, (b + shift) % nb) for b in range(nb)]

    if ng == 2 and nv == 2 and cap % 2 == 0:
        each = cap // 2
        head = (each + 1) // 2
        pieces = []
        for shift in order:
            if 2 * shift == nb:
                pieces += [(shift, 0, head), (shift, head, each - head)]
            else:
                pieces.append((shift, 0, each))
        send, *packed = pack(
            pieces, ocean_f, atmos_f, ocean_w, atmos_w, ocean_ids, atmos_ids, land
        )
        theirs = swap(send, "grp")
        embed_other, packed[0] = lax.optimization_barrier((embed_weight, packed[0]))
        embed_other = swap(embed_other, "sub")
        keep, own_w = keep_own(ocean_f, atmos_f, ocean_w, atmos_w)
        dest = jnp.where(y == 0, ocean_dest, atmos_dest)
        block_all, used_all = slot_tables(dest, nb, cap)

        def table_of(band, tile):
            block = lax.dynamic_index_in_dim(block_all, band, 0, keepdims=False)
            used = lax.dynamic_index_in_dim(used_all, band, 0, keepdims=False)
            scale = jnp.where(used, tile + y * tiles, 2 * tiles)
            return jnp.stack([block, tile, scale]).astype(jnp.int32)

        sent = []
        for at, (piece, (shift, _, _)) in enumerate(zip(packed, pieces)):
            if at >= 2:
                piece, sent[at - 2] = lax.optimization_barrier((piece, sent[at - 2]))
            sent.append(lax.ppermute(piece, "band", along(shift)))

        ids = jnp.where(y == 0, ocean_ids, atmos_ids)
        own_tile = lax.dynamic_index_in_dim(ids, me, 0, keepdims=False)
        def call_of(shift):
            band = (me - shift) % nb
            parts, sizes, firsts = [], [], []
            for piece, across, (of, first, size) in zip(sent, crossed, pieces):
                if of == shift:
                    parts += [piece, across]
                    sizes += [size, size]
                    firsts += [x * each + first, (1 - x) * each + first]
            meta_at = sizes[0] * cells
            tile = parts[0][meta_at + 2 * tiles, :cap].astype(jnp.int32)
            where = jnp.stack([band] + firsts).astype(jnp.int32)
            return table_of(band, tile), where, parts, sizes, [], meta_at

        def add(previous, which, fields, at=0):
            table, where, *rest = which
            return call(table, where, fields, *rest, previous, total=2, at=at)

        where = jnp.stack([me, jnp.int32(0)])
        calls = [(table_of(me, own_tile), where, [own_w], [cap], [land], None)]
        rows_x = add(None, calls[0], [keep])
        crossed = [swap(piece, "var") for piece in sent[:2]]
        for at, piece in enumerate(sent[2:]):
            if at == 1:
                calls.append(call_of(order[0]))
                rows_x = add(rows_x, calls[1], [keep])
            piece, rows_x = lax.optimization_barrier((piece, rows_x))
            crossed.append(swap(piece, "var"))
        calls += [call_of(shift) for shift in order[len(calls) - 1 :]]
        for which in calls[2:-1]:
            rows_x = add(rows_x, which, [keep])
        for which in calls[:-1]:
            rows_x = add(rows_x, which, [theirs], 1)
        rows_x = add(rows_x, calls[-1], [keep, theirs])
        sent = embed(rows_x, embed_weight, embed_other, steps, nv)
        got = lax.all_to_all(sent, ("grp", "band", "var"), split_axis=0, concat_axis=0, tiled=True)
    else:
        embed_other = swap(embed_weight, "sub")
        both = jnp.concatenate([ocean_w, atmos_w], axis=1)
        fields = [jnp.concatenate([ocean_f, atmos_f], axis=0)]
        ocean_block, ocean_used = slot_tables(ocean_dest, nb, cap)
        atmos_block, atmos_used = slot_tables(atmos_dest, nb, cap)
        block_all = jnp.concatenate([ocean_block, atmos_block + block_count], axis=1)
        used_all = jnp.concatenate([ocean_used, atmos_used], axis=1)
        grid_row = jnp.where(jnp.arange(slots) < cap, 0, tiles)

        def table_of(band, tile):
            block = lax.dynamic_index_in_dim(block_all, band, 0, keepdims=False)
            used = lax.dynamic_index_in_dim(used_all, band, 0, keepdims=False)
            scale = jnp.where(used, tile + grid_row, 2 * tiles)
            return jnp.stack([block, tile, scale]).astype(jnp.int32)

        tile_ids = jnp.concatenate([ocean_ids, atmos_ids], axis=1)
        own_tile = lax.dynamic_index_in_dim(tile_ids, me, 0, keepdims=False)
        own_w = lax.dynamic_index_in_dim(both, me, 0, keepdims=False)
        where = jnp.stack([me, jnp.int32(0)])
        rows_x = call(table_of(me, own_tile), where, fields, [own_w], [slots], [land], None, None)
        share_rows = slots * cells // rep
        high = lax.reduce_precision(land, 8, 7)
        low = (land - high).astype(jnp.bfloat16)
        tile_rows = jnp.pad(tile_ids.astype(jnp.bfloat16), ((0, 0), (0, cells - slots)))
        for shift in order:
            target, band = (me + shift) % nb, (me - shift) % nb
            piece = lax.dynamic_slice(
                both, (target, quarter * share_rows, 0), (1, share_rows, cells)
            )[0]
            row = lax.dynamic_slice(tile_rows, (target, 0), (1, cells))
            row = jnp.broadcast_to(row, (16, cells))
            piece = jnp.concatenate([piece, high.astype(jnp.bfloat16), low, row], axis=0)
            parts = lax.all_gather(lax.ppermute(piece, "band", along(shift)), REPL, axis=0)
            meta = parts[0, share_rows:]
            tile = meta[2 * tiles, :slots].astype(jnp.int32)
            parts = parts[:, :share_rows].reshape(slots * cells, cells)
            where = jnp.stack([band, jnp.int32(0)])
            rows_x = call(
                table_of(band, tile), where, fields, [parts], [slots], [meta], -1, rows_x
            )
        sent = embed(rows_x, embed_weight, embed_other, steps, nv)
        got = lax.all_to_all(sent, ("band", "var"), split_axis=0, concat_axis=0, tiled=True)
    shifted = jnp.sum(got.astype(jnp.float32), axis=0) + embed_bias
    inverse = lax.rsqrt(jnp.mean(shifted * shifted, axis=-1, keepdims=True) + 1e-05)
    finished = (shifted * inverse * embed_gain).astype(jnp.bfloat16)
    width = finished.shape[-1]
    finished = finished.reshape(nb, share, steps // nb, width).transpose(1, 0, 2, 3)
    return finished[None]


def solution(mesh):
    in_specs = (
        P(("grp", "band", "sub"), None, "var", None),
        P(("band", "sub"), None),
        P("band", "sub", None, None, None, None),
        P("band", "sub", None, None),
        P(("grp", "band", "sub"), None, "var", None),
        P(("band", "sub"), None),
        P("band", "sub", None, None, None, None),
        P("band", "sub", None, None),
        P("band", "sub", None, None, None),
        P(("var", "sub"), None),
        P(),
        P(),
    )
    out_specs = P("sub", "var", None, ("grp", "band"), None)
    return jax.shard_map(
        per_device, mesh=mesh, in_specs=in_specs, out_specs=out_specs, check_vma=False
    )
```

```python
import functools

import jax
import jax.numpy as jnp
from jax import lax
from jax.experimental import pallas as pl
from jax.experimental.pallas import tpu as pltpu
from jax.sharding import PartitionSpec as P

REPL = ("grp", "var")


def slot_tables(dest, band_count, cap):
    count = dest.shape[0]
    serial = jnp.arange(count, dtype=jnp.int32)
    band_of = dest[:, 0]
    earlier = (band_of[:, None] == band_of[None, :]) & (serial[None, :] < serial[:, None])
    position = jnp.sum(earlier.astype(jnp.int32), axis=1)
    slot = band_of * cap + position
    hit = slot[None, :] == jnp.arange(band_count * cap, dtype=jnp.int32)[:, None]
    block = jnp.sum(jnp.where(hit, serial[None, :], 0), axis=1)
    used = jnp.any(hit, axis=1)
    return block.reshape(band_count, cap), used.reshape(band_count, cap)


def pack_kernel(pieces, *refs):
    count = len(pieces) + 1
    ocean, atmos, ocean_w, atmos_w, ocean_ids, atmos_ids, land = refs[:7]
    outs, stages, sem = refs[7 : 7 + count], refs[7 + count : -1], refs[-1]
    me, bands = lax.axis_index("band"), ocean_w.shape[0]
    x, y = lax.axis_index("var"), lax.axis_index("grp")
    cells, tiles = land.shape[-1], land.shape[0]
    cap = ocean_ids.shape[-1]
    each = cap // 2

    def loads(weights, fields):
        found = []
        for at, (stage, (shift, first, size)) in enumerate(zip(stages, pieces)):
            start = pl.multiple_of((x * each + first) * cells, cells)
            target = lax.rem(me + shift, bands)
            found.append(
                pltpu.make_async_copy(
                    weights.at[target, pl.ds(start, size * cells), :],
                    stage.at[pl.ds(0, size * cells), :],
                    sem.at[0, at],
                )
            )
        return found + [pltpu.make_async_copy(fields, stages[-1], sem.at[0, count - 1])]

    @pl.when(y == 0)
    def _():
        for copy in loads(ocean_w, atmos):
            copy.start()

    @pl.when(y == 1)
    def _():
        for copy in loads(atmos_w, ocean):
            copy.start()

    fraction = land[...]
    high = fraction.astype(jnp.bfloat16)
    low = (fraction - high.astype(jnp.float32)).astype(jnp.bfloat16)
    for stage, (shift, first, size) in zip(stages, pieces):
        if first:
            continue
        target, base = lax.rem(me + shift, bands), size * cells
        stage[pl.ds(base, tiles), :] = high
        stage[pl.ds(base + tiles, tiles), :] = low
        row = jnp.where(y == 0, ocean_ids[pl.ds(target, 1), :], atmos_ids[pl.ds(target, 1), :])
        row = jnp.broadcast_to(row.astype(jnp.float32), (16, cap)).astype(jnp.bfloat16)
        stage[pl.ds(base + 2 * tiles, 16), :] = jnp.zeros((16, cells), jnp.bfloat16)
        stage[pl.ds(base + 2 * tiles, 16), pl.ds(0, cap)] = row
    stores = []
    for at, load in enumerate(loads(ocean_w, atmos)):
        load.wait()
        stores.append(pltpu.make_async_copy(stages[at], outs[at], sem.at[1, at]))
        stores[-1].start()
    for store in stores:
        store.wait()


def pack(pieces, ocean, atmos, ocean_w, atmos_w, ocean_ids, atmos_ids, land):
    cells, tiles = land.shape[-1], land.shape[0]
    any_spec = pl.BlockSpec(memory_space=pl.ANY)
    vmem = pl.BlockSpec(memory_space=pltpu.VMEM)
    sizes = [size * cells + (0 if first else 2 * tiles + 16) for _, first, size in pieces]
    shapes = [(n, cells) for n in sizes] + [ocean.shape]
    return pl.pallas_call(
        functools.partial(pack_kernel, pieces),
        out_shape=[jax.ShapeDtypeStruct(shape, jnp.bfloat16) for shape in shapes],
        in_specs=[any_spec] * 4 + [vmem] * 3,
        out_specs=[any_spec] * len(shapes),
        scratch_shapes=[pltpu.VMEM(shape, jnp.bfloat16) for shape in shapes]
        + [pltpu.SemaphoreType.DMA((2, len(shapes)))],
        cost_estimate=pl.CostEstimate(flops=0, bytes_accessed=4 << 20, transcendentals=0),
        compiler_params=pltpu.CompilerParams(vmem_limit_bytes=60 << 20),
    )(ocean, atmos, ocean_w, atmos_w, ocean_ids, atmos_ids, land)


def keep_kernel(ocean, atmos, ocean_w, atmos_w, keep, own, keep_stage, own_stage, sem):
    me, y = lax.axis_index("band"), lax.axis_index("grp")

    def loads(fields, weights):
        return [
            pltpu.make_async_copy(fields, keep_stage, sem.at[0, 0]),
            pltpu.make_async_copy(weights.at[me], own_stage, sem.at[0, 1]),
        ]

    @pl.when(y == 0)
    def _():
        for copy in loads(ocean, ocean_w):
            copy.start()

    @pl.when(y == 1)
    def _():
        for copy in loads(atmos, atmos_w):
            copy.start()

    stores = [
        pltpu.make_async_copy(keep_stage, keep, sem.at[1, 0]),
        pltpu.make_async_copy(own_stage, own, sem.at[1, 1]),
    ]
    for load, store in zip(loads(ocean, ocean_w), stores):
        load.wait()
        store.start()
    for store in stores:
        store.wait()


def keep_own(ocean, atmos, ocean_w, atmos_w):
    any_spec = pl.BlockSpec(memory_space=pl.ANY)
    shapes = [ocean.shape, ocean_w.shape[1:]]
    return pl.pallas_call(
        keep_kernel,
        out_shape=[jax.ShapeDtypeStruct(shape, jnp.bfloat16) for shape in shapes],
        in_specs=[any_spec] * 4,
        out_specs=[any_spec] * 2,
        scratch_shapes=[pltpu.VMEM(shape, jnp.bfloat16) for shape in shapes]
        + [pltpu.SemaphoreType.DMA((2, 2))],
        cost_estimate=pl.CostEstimate(flops=0, bytes_accessed=3 << 20, transcendentals=0),
        compiler_params=pltpu.CompilerParams(vmem_limit_bytes=60 << 20),
    )(ocean, atmos, ocean_w, atmos_w)


def regrid_kernel(groups, steps, meta_at, part_slots, table, where, *refs):
    out, acc, scale = refs[-3:]
    fields, refs = refs[:groups], refs[groups:]
    parts, rest = refs[: len(part_slots)], refs[len(part_slots) :]
    rows, cells = fields[0].shape[1:]
    tiles = acc.shape[1] // rows
    if meta_at is None:
        land = rest[0][...]
    else:
        meta = rest[0] if meta_at < 0 else parts[0]
        first = max(meta_at, 0)
        high = meta[pl.ds(first, tiles), :].astype(jnp.float32)
        land = high + meta[pl.ds(first + tiles, tiles), :].astype(jnp.float32)
    scale[pl.ds(0, tiles), :] = 1.0 - land
    scale[pl.ds(tiles, tiles), :] = land
    scale[pl.ds(2 * tiles, 8), :] = jnp.zeros((8, cells), jnp.float32)
    acc[...] = jnp.zeros_like(acc)
    for at, (part, size) in enumerate(zip(parts, part_slots)):
        first = where[1 + at]
        for s in range(size):
            slot = first + s
            block = table[0, slot]
            moved = [f[block] for f in fields]
            moved = moved[0] if groups == 1 else jnp.concatenate(moved, axis=0)
            dense = jnp.dot(
                moved, part[pl.ds(s * cells, cells), :], preferred_element_type=jnp.float32
            )
            dense = dense * scale[pl.ds(table[2, slot], 1), :]
            span = pl.ds(pl.multiple_of(table[1, slot] * rows, rows), rows)
            for g in range(groups):
                acc[g, span, :] += dense[g * rows : (g + 1) * rows]
    local_vars = rows // steps
    half_vars = local_vars // 2
    for g in range(groups):
        for v in range(local_vars):
            for q in range(2):
                column = (v % half_vars * 2 + q) * cells
                pieces = [
                    acc[g, pl.ds(q * rows + t * local_vars + v, tiles // 2, 2 * rows), :]
                    for t in range(steps)
                ]
                out[0, g, v // half_vars, :, pl.ds(column, cells)] = jnp.concatenate(
                    pieces, axis=0
                ).astype(out.dtype)


def regrid(
    table, where, fields, parts, part_slots, rest, meta_at, previous, bands, steps, tiles, total, at=0
):
    groups = len(fields)
    rows, cells = fields[0].shape[1:]
    whole = lambda a: pl.BlockSpec(a.shape, lambda i, t, w, n=a.ndim: (0,) * n)
    operands = list(fields) + list(parts) + list(rest)
    in_specs = [whole(a) for a in operands]
    aliases = {}
    if previous is not None:
        aliases = {2 + len(operands): 0}
        in_specs.append(pl.BlockSpec(memory_space=pl.ANY))
        operands.append(previous)
    row_count, width = steps * tiles // 2, rows // steps // 2 * 2 * cells
    block = (2, row_count, width)
    return pl.pallas_call(
        functools.partial(regrid_kernel, groups, steps, meta_at, tuple(part_slots)),
        out_shape=jax.ShapeDtypeStruct((bands, total) + block, jnp.bfloat16),
        grid_spec=pltpu.PrefetchScalarGridSpec(
            num_scalar_prefetch=2,
            grid=(1,),
            in_specs=in_specs,
            out_specs=pl.BlockSpec((1, groups) + block, lambda i, t, w: (w[0], at, 0, 0, 0)),
            scratch_shapes=[
                pltpu.VMEM((groups, tiles * rows, cells), jnp.float32),
                pltpu.VMEM((2 * tiles + 8, cells), jnp.float32),
            ],
        ),
        input_output_aliases=aliases,
        cost_estimate=pl.CostEstimate(
            flops=2 * sum(part_slots) * groups * rows * cells * cells,
            bytes_accessed=4 << 20,
            transcendentals=0,
        ),
        compiler_params=pltpu.CompilerParams(vmem_limit_bytes=20 << 20),
    )(table, where, *operands)


def embed_kernel(steps, halves, rows_x, mine, theirs, out, total):
    at = pl.program_id(0)
    sub, mine_group = lax.axis_index("sub"), lax.axis_index("grp")
    bands, groups, _, row_count, width = rows_x.shape
    rows = bands * groups * row_count

    @pl.when(at == 0)
    def _():
        total[...] = jnp.zeros_like(total)

    left = rows_x[:, :, sub].reshape(rows, width)
    right = rows_x[:, :, 1 - sub].reshape(rows, width)
    total[...] += jnp.dot(left, mine[...], preferred_element_type=jnp.float32) + jnp.dot(
        right, theirs[...], preferred_element_type=jnp.float32
    )

    @pl.when(at == pl.num_programs(0) - 1)
    def _():
        if out.ndim == 2:
            out[...] = total[...].astype(out.dtype)
        else:
            count = steps * halves
            share = row_count // count
            for g in range(groups):
                base = (mine_group if g == 0 else 1 - mine_group) * count if groups > 1 else 0
                for chunk in range(count):
                    pieces = [
                        total[pl.ds((b * groups + g) * row_count + chunk * share, share), :]
                        for b in range(bands)
                    ]
                    out[base + chunk] = jnp.concatenate(pieces, axis=0).astype(out.dtype)


def embed(rows_x, mine, theirs, steps, halves):
    bands, groups, _, row_count, half_width = rows_x.shape
    width = mine.shape[-1]
    grid = 6 if half_width % (6 * 256) == 0 else 3
    step_rows = half_width // grid
    rows = bands * groups * row_count
    chunks = groups * steps * halves
    share = row_count // (steps * halves)
    shape = (chunks, bands * share, width) if share % 4 == 0 else (rows, width)
    weight_spec = pl.BlockSpec((step_rows, width), lambda i: (i, 0))
    out = pl.pallas_call(
        functools.partial(embed_kernel, steps, halves),
        out_shape=jax.ShapeDtypeStruct(shape, jnp.bfloat16),
        grid=(grid,),
        in_specs=[
            pl.BlockSpec((bands, groups, 2, row_count, step_rows), lambda i: (0, 0, 0, 0, i)),
            weight_spec,
            weight_spec,
        ],
        out_specs=pl.BlockSpec(shape, lambda i: (0,) * len(shape)),
        scratch_shapes=[pltpu.VMEM((rows, width), jnp.float32)],
        cost_estimate=pl.CostEstimate(
            flops=4 * rows * mine.shape[0] * width,
            bytes_accessed=4 * mine.shape[0] * width,
            transcendentals=0,
        ),
        compiler_params=pltpu.CompilerParams(
            vmem_limit_bytes=(48 if rows > 1024 else 16) << 20
        ),
    )(rows_x, mine, theirs)
    if share % 4:
        out = out.reshape(bands, chunks, share, width).transpose(1, 0, 2, 3)
        out = out.reshape(chunks, bands * share, width)
    return out


def swap(x, axis):
    return lax.ppermute(x, axis, [(0, 1), (1, 0)])


def per_device(
    ocean_fields,
    ocean_dest,
    ocean_weights,
    ocean_tiles,
    atmos_fields,
    atmos_dest,
    atmos_weights,
    atmos_tiles,
    land_fraction,
    embed_weight,
    embed_bias,
    embed_gain,
):
    nb = lax.axis_size("band")
    nv = lax.axis_size("var")
    ng = lax.axis_size("grp")
    rep = nv * ng
    cap = ocean_weights.shape[3]
    cells = ocean_weights.shape[-1]
    block_count, steps, local_vars, _ = ocean_fields.shape
    patches = land_fraction.shape[2]
    tiles = 2 * patches
    slots = 2 * cap
    share = patches // nv
    me = lax.axis_index("band")
    x, y = lax.axis_index("var"), lax.axis_index("grp")
    quarter = y * nv + x

    flat = (nb, cap * cells, cells)
    ocean_w, atmos_w = ocean_weights.reshape(flat), atmos_weights.reshape(flat)
    ocean_ids, atmos_ids = ocean_tiles.reshape(nb, cap), atmos_tiles.reshape(nb, cap)
    land = land_fraction.reshape(tiles, cells)
    blocks = (block_count, steps * local_vars, cells)
    ocean_f, atmos_f = ocean_fields.reshape(blocks), atmos_fields.reshape(blocks)
    order = ([1, nb - 1] + list(range(2, nb - 1)))[: nb - 1]
    call = functools.partial(regrid, bands=nb, steps=steps, tiles=tiles, total=1)
    along = lambda shift: [(b, (b + shift) % nb) for b in range(nb)]

    if ng == 2 and nv == 2 and cap % 2 == 0:
        each = cap // 2
        head = (each + 1) // 2
        pieces = []
        for shift in order:
            if 2 * shift == nb:
                pieces += [(shift, 0, head), (shift, head, each - head)]
            else:
                pieces.append((shift, 0, each))
        *packed, send = pack(
            pieces, ocean_f, atmos_f, ocean_w, atmos_w, ocean_ids, atmos_ids, land
        )
        theirs = swap(send, "grp")
        embed_other, packed[0] = lax.optimization_barrier((embed_weight, packed[0]))
        embed_other = swap(embed_other, "sub")
        keep, own_w = keep_own(ocean_f, atmos_f, ocean_w, atmos_w)
        dest = jnp.where(y == 0, ocean_dest, atmos_dest)
        block_all, used_all = slot_tables(dest, nb, cap)

        def table_of(band, tile):
            block = lax.dynamic_index_in_dim(block_all, band, 0, keepdims=False)
            used = lax.dynamic_index_in_dim(used_all, band, 0, keepdims=False)
            scale = jnp.where(used, tile + y * tiles, 2 * tiles)
            return jnp.stack([block, tile, scale]).astype(jnp.int32)

        sent = []
        for at, (piece, (shift, _, _)) in enumerate(zip(packed, pieces)):
            if at >= 2:
                piece, sent[at - 2] = lax.optimization_barrier((piece, sent[at - 2]))
            sent.append(lax.ppermute(piece, "band", along(shift)))

        ids = jnp.where(y == 0, ocean_ids, atmos_ids)
        own_tile = lax.dynamic_index_in_dim(ids, me, 0, keepdims=False)
        def call_of(shift):
            band = (me - shift) % nb
            parts, sizes, firsts = [], [], []
            for piece, across, (of, first, size) in zip(sent, crossed, pieces):
                if of == shift:
                    parts += [piece, across]
                    sizes += [size, size]
                    firsts += [x * each + first, (1 - x) * each + first]
            meta_at = sizes[0] * cells
            tile = parts[0][meta_at + 2 * tiles, :cap].astype(jnp.int32)
            where = jnp.stack([band] + firsts).astype(jnp.int32)
            return table_of(band, tile), where, parts, sizes, [], meta_at

        def add(previous, which, fields, at=0):
            table, where, *rest = which
            return call(table, where, fields, *rest, previous, total=2, at=at)

        where = jnp.stack([me, jnp.int32(0)])
        calls = [(table_of(me, own_tile), where, [own_w], [cap], [land], None)]
        rows_x = add(None, calls[0], [keep])
        crossed = [swap(piece, "var") for piece in sent[:2]]
        for at, piece in enumerate(sent[2:]):
            if at == 1:
                calls.append(call_of(order[0]))
                rows_x = add(rows_x, calls[1], [keep])
            piece, rows_x = lax.optimization_barrier((piece, rows_x))
            crossed.append(swap(piece, "var"))
        calls += [call_of(shift) for shift in order[len(calls) - 1 :]]
        for which in calls[2:-1]:
            rows_x = add(rows_x, which, [keep])
        for which in calls[:-1]:
            rows_x = add(rows_x, which, [theirs], 1)
        rows_x = add(rows_x, calls[-1], [keep, theirs])
        sent = embed(rows_x, embed_weight, embed_other, steps, nv)
        got = lax.all_to_all(sent, ("grp", "band", "var"), split_axis=0, concat_axis=0, tiled=True)
    else:
        embed_other = swap(embed_weight, "sub")
        both = jnp.concatenate([ocean_w, atmos_w], axis=1)
        fields = [jnp.concatenate([ocean_f, atmos_f], axis=0)]
        ocean_block, ocean_used = slot_tables(ocean_dest, nb, cap)
        atmos_block, atmos_used = slot_tables(atmos_dest, nb, cap)
        block_all = jnp.concatenate([ocean_block, atmos_block + block_count], axis=1)
        used_all = jnp.concatenate([ocean_used, atmos_used], axis=1)
        grid_row = jnp.where(jnp.arange(slots) < cap, 0, tiles)

        def table_of(band, tile):
            block = lax.dynamic_index_in_dim(block_all, band, 0, keepdims=False)
            used = lax.dynamic_index_in_dim(used_all, band, 0, keepdims=False)
            scale = jnp.where(used, tile + grid_row, 2 * tiles)
            return jnp.stack([block, tile, scale]).astype(jnp.int32)

        tile_ids = jnp.concatenate([ocean_ids, atmos_ids], axis=1)
        own_tile = lax.dynamic_index_in_dim(tile_ids, me, 0, keepdims=False)
        own_w = lax.dynamic_index_in_dim(both, me, 0, keepdims=False)
        where = jnp.stack([me, jnp.int32(0)])
        rows_x = call(table_of(me, own_tile), where, fields, [own_w], [slots], [land], None, None)
        share_rows = slots * cells // rep
        high = lax.reduce_precision(land, 8, 7)
        low = (land - high).astype(jnp.bfloat16)
        tile_rows = jnp.pad(tile_ids.astype(jnp.bfloat16), ((0, 0), (0, cells - slots)))
        for shift in order:
            target, band = (me + shift) % nb, (me - shift) % nb
            piece = lax.dynamic_slice(
                both, (target, quarter * share_rows, 0), (1, share_rows, cells)
            )[0]
            row = lax.dynamic_slice(tile_rows, (target, 0), (1, cells))
            row = jnp.broadcast_to(row, (16, cells))
            piece = jnp.concatenate([piece, high.astype(jnp.bfloat16), low, row], axis=0)
            parts = lax.all_gather(lax.ppermute(piece, "band", along(shift)), REPL, axis=0)
            meta = parts[0, share_rows:]
            tile = meta[2 * tiles, :slots].astype(jnp.int32)
            parts = parts[:, :share_rows].reshape(slots * cells, cells)
            where = jnp.stack([band, jnp.int32(0)])
            rows_x = call(
                table_of(band, tile), where, fields, [parts], [slots], [meta], -1, rows_x
            )
        sent = embed(rows_x, embed_weight, embed_other, steps, nv)
        got = lax.all_to_all(sent, ("band", "var"), split_axis=0, concat_axis=0, tiled=True)
    shifted = jnp.sum(got.astype(jnp.float32), axis=0) + embed_bias
    inverse = lax.rsqrt(jnp.mean(shifted * shifted, axis=-1, keepdims=True) + 1e-05)
    finished = (shifted * inverse * embed_gain).astype(jnp.bfloat16)
    width = finished.shape[-1]
    finished = finished.reshape(nb, share, steps // nb, width).transpose(1, 0, 2, 3)
    return finished[None]


def solution(mesh):
    in_specs = (
        P(("grp", "band", "sub"), None, "var", None),
        P(("band", "sub"), None),
        P("band", "sub", None, None, None, None),
        P("band", "sub", None, None),
        P(("grp", "band", "sub"), None, "var", None),
        P(("band", "sub"), None),
        P("band", "sub", None, None, None, None),
        P("band", "sub", None, None),
        P("band", "sub", None, None, None),
        P(("var", "sub"), None),
        P(),
        P(),
    )
    out_specs = P("sub", "var", None, ("grp", "band"), None)
    return jax.shard_map(
        per_device, mesh=mesh, in_specs=in_specs, out_specs=out_specs, check_vma=False
    )
```

```python
import functools

import jax
import jax.numpy as jnp
from jax import lax
from jax.experimental import pallas as pl
from jax.experimental.pallas import tpu as pltpu
from jax.sharding import PartitionSpec as P

REPL = ("grp", "var")
PACK_LIMIT = 60 << 20


def slot_tables(dest, band_count, cap):
    count = dest.shape[0]
    serial = jnp.arange(count, dtype=jnp.int32)
    band_of = dest[:, 0]
    earlier = (band_of[:, None] == band_of[None, :]) & (serial[None, :] < serial[:, None])
    position = jnp.sum(earlier.astype(jnp.int32), axis=1)
    slot = band_of * cap + position
    hit = slot[None, :] == jnp.arange(band_count * cap, dtype=jnp.int32)[:, None]
    block = jnp.sum(jnp.where(hit, serial[None, :], 0), axis=1)
    used = jnp.any(hit, axis=1)
    return block.reshape(band_count, cap), used.reshape(band_count, cap)


def pack_kernel(pieces, moved, *refs):
    ocean_w, atmos_w, ocean_ids, atmos_ids, land = refs[:5]
    fields, refs = refs[5 : 5 + 2 * moved], refs[5 + 2 * moved :]
    count = len(pieces) + moved
    stages, sem = refs[:count], refs[-1]
    me, bands = lax.axis_index("band"), ocean_w.shape[0]
    x, y = lax.axis_index("var"), lax.axis_index("grp")
    cells, tiles = land.shape[-1], land.shape[0]
    cap = ocean_ids.shape[-1]

    def loads(weights, other):
        found = []
        for at, (stage, (shift, first, size, split)) in enumerate(zip(stages, pieces)):
            start = first if split is None else x * split + first
            found.append(
                pltpu.make_async_copy(
                    weights.at[
                        lax.rem(me + shift, bands),
                        pl.ds(pl.multiple_of(start * cells, cells), size * cells),
                        :,
                    ],
                    stage.at[pl.ds(0, size * cells), :],
                    sem.at[at],
                )
            )
        if moved:
            found.append(pltpu.make_async_copy(fields[other], stages[-1], sem.at[count - 1]))
        return found

    @pl.when(y == 0)
    def _():
        for copy in loads(ocean_w, 1):
            copy.start()

    @pl.when(y == 1)
    def _():
        for copy in loads(atmos_w, 0):
            copy.start()

    fraction = land[...]
    high = fraction.astype(jnp.bfloat16)
    low = (fraction - high.astype(jnp.float32)).astype(jnp.bfloat16)
    for stage, (shift, first, size, split) in zip(stages, pieces):
        if first:
            continue
        target, base = lax.rem(me + shift, bands), size * cells
        stage[pl.ds(base, tiles), :] = high
        stage[pl.ds(base + tiles, tiles), :] = low
        row = jnp.where(y == 0, ocean_ids[pl.ds(target, 1), :], atmos_ids[pl.ds(target, 1), :])
        row = jnp.broadcast_to(row.astype(jnp.float32), (16, cap)).astype(jnp.bfloat16)
        stage[pl.ds(base + 2 * tiles, 16), :] = jnp.zeros((16, cells), jnp.bfloat16)
        stage[pl.ds(base + 2 * tiles, 16), pl.ds(0, cap)] = row
    for load in loads(ocean_w, 1):
        load.wait()


def pack(pieces, ocean_w, atmos_w, ocean_ids, atmos_ids, land, *fields):
    cells, tiles = land.shape[-1], land.shape[0]
    any_spec = pl.BlockSpec(memory_space=pl.ANY)
    vmem = pl.BlockSpec(memory_space=pltpu.VMEM)
    sizes = [size * cells + (0 if first else 2 * tiles + 16) for _, first, size, _ in pieces]
    shapes = [(n, cells) for n in sizes] + [f.shape for f in fields[:1]]
    return pl.pallas_call(
        functools.partial(pack_kernel, pieces, len(fields) // 2),
        out_shape=[jax.ShapeDtypeStruct(shape, jnp.bfloat16) for shape in shapes],
        in_specs=[any_spec] * 2 + [vmem] * 3 + [any_spec] * len(fields),
        out_specs=[vmem] * len(shapes),
        scratch_shapes=[pltpu.SemaphoreType.DMA((len(shapes),))],
        cost_estimate=pl.CostEstimate(flops=0, bytes_accessed=2 << 20, transcendentals=0),
        compiler_params=pltpu.CompilerParams(vmem_limit_bytes=PACK_LIMIT),
    )(ocean_w, atmos_w, ocean_ids, atmos_ids, land, *fields)


def regrid_kernel(steps, jobs, count, *refs):
    out, acc, scale = refs[-3:]
    local_rows, cells = acc.shape[1] // (scale.shape[0] // 2 - 4), acc.shape[2]
    tiles = acc.shape[1] // local_rows
    local_vars = local_rows // steps
    half_vars = local_vars // 2
    for table, where, meta, meta_at, parts, groups in jobs:
        table, where, meta = refs[table], refs[where], refs[meta]
        if meta.dtype == jnp.float32:
            land = meta[...]
        else:
            high = meta[pl.ds(meta_at, tiles), :].astype(jnp.float32)
            land = high + meta[pl.ds(meta_at + tiles, tiles), :].astype(jnp.float32)
        scale[pl.ds(0, tiles), :] = 1.0 - land
        scale[pl.ds(tiles, tiles), :] = land
        scale[pl.ds(2 * tiles, 8), :] = jnp.zeros((8, cells), jnp.float32)
        acc[pl.ds(0, len(groups))] = jnp.zeros((len(groups),) + acc.shape[1:], jnp.float32)
        for at, (part, size) in enumerate(parts):
            first = where[1 + at]
            for s in range(size):
                slot = first + s
                block = table[0, slot]
                moved = []
                for _, fields in groups:
                    piece = refs[fields[0]][block]
                    if len(fields) > 1:
                        piece = jnp.where(
                            lax.axis_index("grp") == 0, piece, refs[fields[1]][block]
                        )
                    moved.append(piece)
                moved = moved[0] if len(moved) == 1 else jnp.concatenate(moved, axis=0)
                dense = jnp.dot(
                    moved,
                    refs[part][pl.ds(s * cells, cells), :],
                    preferred_element_type=jnp.float32,
                )
                dense = dense * scale[pl.ds(table[2, slot], 1), :]
                span = pl.ds(pl.multiple_of(table[1, slot] * local_rows, local_rows), local_rows)
                for g in range(len(groups)):
                    acc[g, span, :] += dense[g * local_rows : (g + 1) * local_rows]
        for g, (to, _) in enumerate(groups):
            for v in range(local_vars):
                for q in range(2):
                    column = (v % half_vars * 2 + q) * cells
                    rows = [
                        acc[g, pl.ds(q * local_rows + t * local_vars + v, tiles // 2, 2 * local_rows), :]
                        for t in range(steps)
                    ]
                    out[where[0], to, v // half_vars, :, pl.ds(column, cells)] = jnp.concatenate(
                        rows, axis=0
                    ).astype(out.dtype)


def regrid(jobs, previous, bands, groups, steps, tiles, rows, cells):
    operands, specs, places = [], [], {}

    def place(array, space):
        if id(array) not in places:
            places[id(array)] = len(operands)
            operands.append(array)
            specs.append(pl.BlockSpec(memory_space=space))
        return places[id(array)]

    listed, flops, most = [], 0, 1
    for table, where, meta, meta_at, parts, sizes, fields in jobs:
        listed.append(
            (
                place(table, pltpu.SMEM),
                place(where, pltpu.SMEM),
                place(meta, pltpu.VMEM),
                meta_at,
                [(place(part, pltpu.VMEM), size) for part, size in zip(parts, sizes)],
                [(to, [place(f, pltpu.VMEM) for f in pair]) for to, pair in fields],
            )
        )
        flops += 2 * sum(sizes) * len(fields) * rows * cells * cells
        most = max(most, len(fields))
    aliases = {}
    if previous is not None:
        aliases = {len(operands): 0}
        operands.append(previous)
        specs.append(pl.BlockSpec(memory_space=pltpu.VMEM))
    shape = (bands, groups, 2, steps * tiles // 2, rows // steps // 2 * 2 * cells)
    return pl.pallas_call(
        functools.partial(regrid_kernel, steps, listed, len(operands)),
        out_shape=jax.ShapeDtypeStruct(shape, jnp.bfloat16),
        in_specs=specs,
        out_specs=pl.BlockSpec(memory_space=pltpu.VMEM),
        scratch_shapes=[
            pltpu.VMEM((most, tiles * rows, cells), jnp.float32),
            pltpu.VMEM((2 * tiles + 8, cells), jnp.float32),
        ],
        input_output_aliases=aliases,
        cost_estimate=pl.CostEstimate(
            flops=flops, bytes_accessed=len(jobs) * 3 << 20, transcendentals=0
        ),
        compiler_params=pltpu.CompilerParams(vmem_limit_bytes=28 << 20),
    )(*operands)


def embed_kernel(steps, halves, rows_x, mine, theirs, out, total):
    at = pl.program_id(0)
    sub, mine_group = lax.axis_index("sub"), lax.axis_index("grp")
    bands, groups, _, row_count, width = rows_x.shape
    rows = bands * groups * row_count

    @pl.when(at == 0)
    def _():
        total[...] = jnp.zeros_like(total)

    left = rows_x[:, :, sub].reshape(rows, width)
    right = rows_x[:, :, 1 - sub].reshape(rows, width)
    total[...] += jnp.dot(left, mine[...], preferred_element_type=jnp.float32) + jnp.dot(
        right, theirs[...], preferred_element_type=jnp.float32
    )

    @pl.when(at == pl.num_programs(0) - 1)
    def _():
        if out.ndim == 2:
            out[...] = total[...].astype(out.dtype)
        else:
            count = steps * halves
            share = row_count // count
            for g in range(groups):
                base = (mine_group if g == 0 else 1 - mine_group) * count if groups > 1 else 0
                for chunk in range(count):
                    pieces = [
                        total[pl.ds((b * groups + g) * row_count + chunk * share, share), :]
                        for b in range(bands)
                    ]
                    out[base + chunk] = jnp.concatenate(pieces, axis=0).astype(out.dtype)


def embed(rows_x, mine, theirs, steps, halves):
    bands, groups, _, row_count, half_width = rows_x.shape
    width = mine.shape[-1]
    grid = 6 if half_width % (6 * 256) == 0 else 3
    step_rows = half_width // grid
    rows = bands * groups * row_count
    chunks = groups * steps * halves
    share = row_count // (steps * halves)
    shape = (chunks, bands * share, width) if share % 4 == 0 else (rows, width)
    weight_spec = pl.BlockSpec((step_rows, width), lambda i: (i, 0))
    out = pl.pallas_call(
        functools.partial(embed_kernel, steps, halves),
        out_shape=jax.ShapeDtypeStruct(shape, jnp.bfloat16),
        grid=(grid,),
        in_specs=[
            pl.BlockSpec((bands, groups, 2, row_count, step_rows), lambda i: (0, 0, 0, 0, i)),
            weight_spec,
            weight_spec,
        ],
        out_specs=pl.BlockSpec(shape, lambda i: (0,) * len(shape)),
        scratch_shapes=[pltpu.VMEM((rows, width), jnp.float32)],
        cost_estimate=pl.CostEstimate(
            flops=4 * rows * mine.shape[0] * width,
            bytes_accessed=4 * mine.shape[0] * width,
            transcendentals=0,
        ),
        compiler_params=pltpu.CompilerParams(
            vmem_limit_bytes=(48 if rows > 1024 else 16) << 20
        ),
    )(rows_x, mine, theirs)
    if share % 4:
        out = out.reshape(bands, chunks, share, width).transpose(1, 0, 2, 3)
        out = out.reshape(chunks, bands * share, width)
    return out


def swap(x, axis):
    return lax.ppermute(x, axis, [(0, 1), (1, 0)])


def per_device(
    ocean_fields,
    ocean_dest,
    ocean_weights,
    ocean_tiles,
    atmos_fields,
    atmos_dest,
    atmos_weights,
    atmos_tiles,
    land_fraction,
    embed_weight,
    embed_bias,
    embed_gain,
):
    nb = lax.axis_size("band")
    nv = lax.axis_size("var")
    ng = lax.axis_size("grp")
    rep = nv * ng
    cap = ocean_weights.shape[3]
    cells = ocean_weights.shape[-1]
    block_count, steps, local_vars, _ = ocean_fields.shape
    patches = land_fraction.shape[2]
    tiles = 2 * patches
    slots = 2 * cap
    share = patches // nv
    me = lax.axis_index("band")
    x, y = lax.axis_index("var"), lax.axis_index("grp")
    quarter = y * nv + x

    flat = (nb, cap * cells, cells)
    ocean_w, atmos_w = ocean_weights.reshape(flat), atmos_weights.reshape(flat)
    ocean_ids, atmos_ids = ocean_tiles.reshape(nb, cap), atmos_tiles.reshape(nb, cap)
    land = land_fraction.reshape(tiles, cells)
    blocks = (block_count, steps * local_vars, cells)
    ocean_f, atmos_f = ocean_fields.reshape(blocks), atmos_fields.reshape(blocks)
    order = ([1, nb - 1] + list(range(2, nb - 1)))[: nb - 1]
    along = lambda shift: [(b, (b + shift) % nb) for b in range(nb)]
    call = functools.partial(
        regrid, bands=nb, steps=steps, tiles=tiles, rows=steps * local_vars, cells=cells
    )

    if ng == 2 and nv == 2 and cap % 2 == 0:
        each = cap // 2
        pieces = []
        for shift in order:
            pieces.append((shift, 0, each, each))
        *packed, own_w, send = pack(
            pieces + [(0, 0, cap, None)], ocean_w, atmos_w, ocean_ids, atmos_ids, land, ocean_f, atmos_f
        )
        sent = [
            lax.ppermute(piece, "band", along(shift))
            for piece, (shift, _, _, _) in zip(packed, pieces)
        ]
        embed_other, send = lax.optimization_barrier((embed_weight, send))
        embed_other = swap(embed_other, "sub")
        keep, theirs = (ocean_f, atmos_f), (swap(send, "grp"),)
        dest = jnp.where(y == 0, ocean_dest, atmos_dest)
        block_all, used_all = slot_tables(dest, nb, cap)

        def job_of(band, parts, sizes, firsts, fields):
            meta_at = sizes[0] * cells
            tile = parts[0][meta_at + 2 * tiles, :cap].astype(jnp.int32)
            block = lax.dynamic_index_in_dim(block_all, band, 0, keepdims=False)
            used = lax.dynamic_index_in_dim(used_all, band, 0, keepdims=False)
            scale = jnp.where(used, tile + y * tiles, 2 * tiles)
            table = jnp.stack([block, tile, scale]).astype(jnp.int32)
            where = jnp.stack([band] + firsts).astype(jnp.int32)
            return table, where, parts[0], meta_at, parts, sizes, fields

        def with_fields(job, fields):
            return job[:-1] + (fields,)

        def job_at(shift, fields):
            parts, sizes, firsts = [], [], []
            for piece, across, (of, first, size, _) in zip(sent, crossed, pieces):
                if of == shift:
                    parts += [piece, across]
                    sizes += [size, size]
                    firsts += [x * each + first, (1 - x) * each + first]
            return job_of((me - shift) % nb, parts, sizes, firsts, fields)

        ours, others = [(0, keep)], [(1, theirs)]
        own_w, sent[0] = lax.optimization_barrier((own_w, sent[0]))
        jobs = [job_of(me, [own_w], [cap], [jnp.int32(0)], ours)]
        rows_x = call(jobs[:1], None, groups=2)
        crossed = [swap(sent[0], "var")]
        for at in range(1, len(sent)):
            if at > 1:
                jobs.append(job_at(order[at - 2], ours))
                rows_x = call(jobs[-1:], rows_x, groups=2)
            sent[at], rows_x = lax.optimization_barrier((sent[at], rows_x))
            crossed.append(swap(sent[at], "var"))
        done = len(jobs)
        jobs += [job_at(shift, ours) for shift in order[done - 1 :]]
        rows_x = call(
            jobs[done:-1] + [with_fields(job, others) for job in jobs[:-1]], rows_x, groups=2
        )
        rows_x = call([with_fields(jobs[-1], ours + others)], rows_x, groups=2)
        sent = embed(rows_x, embed_weight, embed_other, steps, nv)
        got = lax.all_to_all(sent, ("grp", "band", "var"), split_axis=0, concat_axis=0, tiled=True)
    else:
        embed_other = swap(embed_weight, "sub")
        both = jnp.concatenate([ocean_w, atmos_w], axis=1)
        fields = [(0, (jnp.concatenate([ocean_f, atmos_f], axis=0),))]
        ocean_block, ocean_used = slot_tables(ocean_dest, nb, cap)
        atmos_block, atmos_used = slot_tables(atmos_dest, nb, cap)
        block_all = jnp.concatenate([ocean_block, atmos_block + block_count], axis=1)
        used_all = jnp.concatenate([ocean_used, atmos_used], axis=1)
        grid_row = jnp.where(jnp.arange(slots) < cap, 0, tiles)

        def job_of(band, tile, meta, parts):
            block = lax.dynamic_index_in_dim(block_all, band, 0, keepdims=False)
            used = lax.dynamic_index_in_dim(used_all, band, 0, keepdims=False)
            scale = jnp.where(used, tile + grid_row, 2 * tiles)
            table = jnp.stack([block, tile, scale]).astype(jnp.int32)
            where = jnp.stack([band, jnp.int32(0)])
            return table, where, meta, 0, [parts], [slots], fields

        tile_ids = jnp.concatenate([ocean_ids, atmos_ids], axis=1)
        own_tile = lax.dynamic_index_in_dim(tile_ids, me, 0, keepdims=False)
        own_w = lax.dynamic_index_in_dim(both, me, 0, keepdims=False)
        rows_x = call([job_of(me, own_tile, land, own_w)], None, groups=1)
        share_rows = slots * cells // rep
        high = lax.reduce_precision(land, 8, 7)
        low = (land - high).astype(jnp.bfloat16)
        tile_rows = jnp.pad(tile_ids.astype(jnp.bfloat16), ((0, 0), (0, cells - slots)))
        for shift in order:
            target, band = (me + shift) % nb, (me - shift) % nb
            piece = lax.dynamic_slice(
                both, (target, quarter * share_rows, 0), (1, share_rows, cells)
            )[0]
            row = lax.dynamic_slice(tile_rows, (target, 0), (1, cells))
            row = jnp.broadcast_to(row, (16, cells))
            piece = jnp.concatenate([piece, high.astype(jnp.bfloat16), low, row], axis=0)
            parts = lax.all_gather(lax.ppermute(piece, "band", along(shift)), REPL, axis=0)
            meta = parts[0, share_rows:]
            tile = meta[2 * tiles, :slots].astype(jnp.int32)
            parts = parts[:, :share_rows].reshape(slots * cells, cells)
            rows_x = call([job_of(band, tile, meta, parts)], rows_x, groups=1)
        sent = embed(rows_x, embed_weight, embed_other, steps, nv)
        got = lax.all_to_all(sent, ("band", "var"), split_axis=0, concat_axis=0, tiled=True)
    shifted = jnp.sum(got.astype(jnp.float32), axis=0) + embed_bias
    inverse = lax.rsqrt(jnp.mean(shifted * shifted, axis=-1, keepdims=True) + 1e-05)
    finished = (shifted * inverse * embed_gain).astype(jnp.bfloat16)
    width = finished.shape[-1]
    finished = finished.reshape(nb, share, steps // nb, width).transpose(1, 0, 2, 3)
    return finished[None]


def solution(mesh):
    in_specs = (
        P(("grp", "band", "sub"), None, "var", None),
        P(("band", "sub"), None),
        P("band", "sub", None, None, None, None),
        P("band", "sub", None, None),
        P(("grp", "band", "sub"), None, "var", None),
        P(("band", "sub"), None),
        P("band", "sub", None, None, None, None),
        P("band", "sub", None, None),
        P("band", "sub", None, None, None),
        P(("var", "sub"), None),
        P(),
        P(),
    )
    out_specs = P("sub", "var", None, ("grp", "band"), None)
    return jax.shard_map(
        per_device, mesh=mesh, in_specs=in_specs, out_specs=out_specs, check_vma=False
    )
```

```python
import functools

import jax
import jax.numpy as jnp
from jax import lax
from jax.experimental import pallas as pl
from jax.experimental.pallas import tpu as pltpu
from jax.sharding import PartitionSpec as P

REPL = ("grp", "var")
PACK_LIMIT = 60 << 20


def slot_tables(dest, band_count, cap):
    count = dest.shape[0]
    serial = jnp.arange(count, dtype=jnp.int32)
    band_of = dest[:, 0]
    earlier = (band_of[:, None] == band_of[None, :]) & (serial[None, :] < serial[:, None])
    position = jnp.sum(earlier.astype(jnp.int32), axis=1)
    slot = band_of * cap + position
    hit = slot[None, :] == jnp.arange(band_count * cap, dtype=jnp.int32)[:, None]
    block = jnp.sum(jnp.where(hit, serial[None, :], 0), axis=1)
    used = jnp.any(hit, axis=1)
    return block.reshape(band_count, cap), used.reshape(band_count, cap)


def pack_kernel(pieces, moved, *refs):
    ocean_w, atmos_w, ocean_ids, atmos_ids, land = refs[:5]
    fields, refs = refs[5 : 5 + 2 * moved], refs[5 + 2 * moved :]
    count = len(pieces) + moved
    stages, sem = refs[:count], refs[-1]
    me, bands = lax.axis_index("band"), ocean_w.shape[0]
    x, y = lax.axis_index("var"), lax.axis_index("grp")
    cells, tiles = land.shape[-1], land.shape[0]
    cap = ocean_ids.shape[-1]

    def loads(weights, other):
        found = []
        for at, (stage, (shift, first, size, split)) in enumerate(zip(stages, pieces)):
            start = first if split is None else x * split + first
            found.append(
                pltpu.make_async_copy(
                    weights.at[
                        lax.rem(me + shift, bands),
                        pl.ds(pl.multiple_of(start * cells, cells), size * cells),
                        :,
                    ],
                    stage.at[pl.ds(0, size * cells), :],
                    sem.at[at],
                )
            )
        if moved:
            found.append(pltpu.make_async_copy(fields[other], stages[-1], sem.at[count - 1]))
        return found

    @pl.when(y == 0)
    def _():
        for copy in loads(ocean_w, 1):
            copy.start()

    @pl.when(y == 1)
    def _():
        for copy in loads(atmos_w, 0):
            copy.start()

    fraction = land[...]
    high = fraction.astype(jnp.bfloat16)
    low = (fraction - high.astype(jnp.float32)).astype(jnp.bfloat16)
    for stage, (shift, first, size, split) in zip(stages, pieces):
        if first:
            continue
        target, base = lax.rem(me + shift, bands), size * cells
        stage[pl.ds(base, tiles), :] = high
        stage[pl.ds(base + tiles, tiles), :] = low
        row = jnp.where(y == 0, ocean_ids[pl.ds(target, 1), :], atmos_ids[pl.ds(target, 1), :])
        row = jnp.broadcast_to(row.astype(jnp.float32), (16, cap)).astype(jnp.bfloat16)
        stage[pl.ds(base + 2 * tiles, 16), :] = jnp.zeros((16, cells), jnp.bfloat16)
        stage[pl.ds(base + 2 * tiles, 16), pl.ds(0, cap)] = row
    for load in loads(ocean_w, 1):
        load.wait()


def pack(pieces, ocean_w, atmos_w, ocean_ids, atmos_ids, land, *fields):
    cells, tiles = land.shape[-1], land.shape[0]
    any_spec = pl.BlockSpec(memory_space=pl.ANY)
    vmem = pl.BlockSpec(memory_space=pltpu.VMEM)
    sizes = [size * cells + (0 if first else 2 * tiles + 16) for _, first, size, _ in pieces]
    shapes = [(n, cells) for n in sizes] + [f.shape for f in fields[:1]]
    return pl.pallas_call(
        functools.partial(pack_kernel, pieces, len(fields) // 2),
        out_shape=[jax.ShapeDtypeStruct(shape, jnp.bfloat16) for shape in shapes],
        in_specs=[any_spec] * 2 + [vmem] * 3 + [any_spec] * len(fields),
        out_specs=[vmem] * len(shapes),
        scratch_shapes=[pltpu.SemaphoreType.DMA((len(shapes),))],
        cost_estimate=pl.CostEstimate(flops=0, bytes_accessed=2 << 20, transcendentals=0),
        compiler_params=pltpu.CompilerParams(vmem_limit_bytes=PACK_LIMIT),
    )(ocean_w, atmos_w, ocean_ids, atmos_ids, land, *fields)


def regrid_kernel(steps, jobs, count, *refs):
    out, acc, scale = refs[-3:]
    local_rows, cells = acc.shape[1] // (scale.shape[0] // 2 - 4), acc.shape[2]
    tiles = acc.shape[1] // local_rows
    local_vars = local_rows // steps
    half_vars = local_vars // 2
    for table, where, meta, meta_at, parts, groups in jobs:
        table, where, meta = refs[table], refs[where], refs[meta]
        if meta.dtype == jnp.float32:
            land = meta[...]
        else:
            high = meta[pl.ds(meta_at, tiles), :].astype(jnp.float32)
            land = high + meta[pl.ds(meta_at + tiles, tiles), :].astype(jnp.float32)
        scale[pl.ds(0, tiles), :] = 1.0 - land
        scale[pl.ds(tiles, tiles), :] = land
        scale[pl.ds(2 * tiles, 8), :] = jnp.zeros((8, cells), jnp.float32)
        acc[pl.ds(0, len(groups))] = jnp.zeros((len(groups),) + acc.shape[1:], jnp.float32)
        for at, (part, size) in enumerate(parts):
            first = where[1 + at]
            for s in range(size):
                slot = first + s
                block = table[0, slot]
                moved = []
                for _, fields in groups:
                    piece = refs[fields[0]][block]
                    if len(fields) > 1:
                        piece = jnp.where(
                            lax.axis_index("grp") == 0, piece, refs[fields[1]][block]
                        )
                    moved.append(piece)
                moved = moved[0] if len(moved) == 1 else jnp.concatenate(moved, axis=0)
                dense = jnp.dot(
                    moved,
                    refs[part][pl.ds(s * cells, cells), :],
                    preferred_element_type=jnp.float32,
                )
                dense = dense * scale[pl.ds(table[2, slot], 1), :]
                span = pl.ds(pl.multiple_of(table[1, slot] * local_rows, local_rows), local_rows)
                for g in range(len(groups)):
                    acc[g, span, :] += dense[g * local_rows : (g + 1) * local_rows]
        for g, (to, _) in enumerate(groups):
            for v in range(local_vars):
                for q in range(2):
                    column = (v % half_vars * 2 + q) * cells
                    rows = [
                        acc[g, pl.ds(q * local_rows + t * local_vars + v, tiles // 2, 2 * local_rows), :]
                        for t in range(steps)
                    ]
                    out[where[0], to, v // half_vars, :, pl.ds(column, cells)] = jnp.concatenate(
                        rows, axis=0
                    ).astype(out.dtype)


def regrid(jobs, previous, bands, groups, steps, tiles, rows, cells):
    operands, specs, places = [], [], {}

    def place(array, space):
        if id(array) not in places:
            places[id(array)] = len(operands)
            operands.append(array)
            specs.append(pl.BlockSpec(memory_space=space))
        return places[id(array)]

    listed, flops, most = [], 0, 1
    for table, where, meta, meta_at, parts, sizes, fields in jobs:
        listed.append(
            (
                place(table, pltpu.SMEM),
                place(where, pltpu.SMEM),
                place(meta, pltpu.VMEM),
                meta_at,
                [(place(part, pltpu.VMEM), size) for part, size in zip(parts, sizes)],
                [(to, [place(f, pltpu.VMEM) for f in pair]) for to, pair in fields],
            )
        )
        flops += 2 * sum(sizes) * len(fields) * rows * cells * cells
        most = max(most, len(fields))
    aliases = {}
    if previous is not None:
        aliases = {len(operands): 0}
        operands.append(previous)
        specs.append(pl.BlockSpec(memory_space=pltpu.VMEM))
    shape = (bands, groups, 2, steps * tiles // 2, rows // steps // 2 * 2 * cells)
    return pl.pallas_call(
        functools.partial(regrid_kernel, steps, listed, len(operands)),
        out_shape=jax.ShapeDtypeStruct(shape, jnp.bfloat16),
        in_specs=specs,
        out_specs=pl.BlockSpec(memory_space=pltpu.VMEM),
        scratch_shapes=[
            pltpu.VMEM((most, tiles * rows, cells), jnp.float32),
            pltpu.VMEM((2 * tiles + 8, cells), jnp.float32),
        ],
        input_output_aliases=aliases,
        cost_estimate=pl.CostEstimate(
            flops=flops, bytes_accessed=len(jobs) * 3 << 20, transcendentals=0
        ),
        compiler_params=pltpu.CompilerParams(vmem_limit_bytes=28 << 20),
    )(*operands)


def embed_kernel(steps, halves, rows_x, first, second, out, total):
    at = pl.program_id(0)
    mine_group = lax.axis_index("grp")
    bands, groups, _, row_count, width = rows_x.shape
    rows = bands * groups * row_count

    @pl.when(at == 0)
    def _():
        total[...] = jnp.zeros_like(total)

    left, right = (rows_x[:, :, half].reshape(rows, width) for half in range(2))
    total[...] += jnp.dot(left, first[...], preferred_element_type=jnp.float32) + jnp.dot(
        right, second[...], preferred_element_type=jnp.float32
    )

    @pl.when(at == pl.num_programs(0) - 1)
    def _():
        if out.ndim == 2:
            out[...] = total[...].astype(out.dtype)
        else:
            count = steps * halves
            share = row_count // count
            for g in range(groups):
                base = (mine_group if g == 0 else 1 - mine_group) * count if groups > 1 else 0
                for chunk in range(count):
                    pieces = [
                        total[pl.ds((b * groups + g) * row_count + chunk * share, share), :]
                        for b in range(bands)
                    ]
                    out[base + chunk] = jnp.concatenate(pieces, axis=0).astype(out.dtype)


def embed(rows_x, weight, steps, halves):
    bands, groups, _, row_count, half_width = rows_x.shape
    width = weight.shape[-1]
    grid = 6 if half_width % (6 * 256) == 0 else 3
    step_rows = half_width // grid
    rows = bands * groups * row_count
    chunks = groups * steps * halves
    share = row_count // (steps * halves)
    shape = (chunks, bands * share, width) if share % 4 == 0 else (rows, width)
    weight_specs = [
        pl.BlockSpec((step_rows, width), lambda i: (i, 0)),
        pl.BlockSpec((step_rows, width), lambda i: (i + grid, 0)),
    ]
    out = pl.pallas_call(
        functools.partial(embed_kernel, steps, halves),
        out_shape=jax.ShapeDtypeStruct(shape, jnp.bfloat16),
        grid=(grid,),
        in_specs=[
            pl.BlockSpec((bands, groups, 2, row_count, step_rows), lambda i: (0, 0, 0, 0, i)),
            *weight_specs,
        ],
        out_specs=pl.BlockSpec(shape, lambda i: (0,) * len(shape)),
        scratch_shapes=[pltpu.VMEM((rows, width), jnp.float32)],
        cost_estimate=pl.CostEstimate(
            flops=2 * rows * weight.shape[0] * width,
            bytes_accessed=2 * weight.shape[0] * width,
            transcendentals=0,
        ),
        compiler_params=pltpu.CompilerParams(
            vmem_limit_bytes=(48 if rows > 1024 else 16) << 20
        ),
    )(rows_x, weight, weight)
    if share % 4:
        out = out.reshape(bands, chunks, share, width).transpose(1, 0, 2, 3)
        out = out.reshape(chunks, bands * share, width)
    return out


def swap(x, axis):
    return lax.ppermute(x, axis, [(0, 1), (1, 0)])


def per_device(
    ocean_fields,
    ocean_dest,
    ocean_weights,
    ocean_tiles,
    atmos_fields,
    atmos_dest,
    atmos_weights,
    atmos_tiles,
    land_fraction,
    embed_weight,
    embed_bias,
    embed_gain,
):
    nb = lax.axis_size("band")
    nv = lax.axis_size("var")
    ng = lax.axis_size("grp")
    rep = nv * ng
    cap = ocean_weights.shape[3]
    cells = ocean_weights.shape[-1]
    block_count, steps, local_vars, _ = ocean_fields.shape
    patches = land_fraction.shape[2]
    tiles = 2 * patches
    slots = 2 * cap
    share = patches // nv
    me = lax.axis_index("band")
    x, y = lax.axis_index("var"), lax.axis_index("grp")
    quarter = y * nv + x

    embed_rows = lax.all_gather(embed_weight, "sub", axis=0, tiled=True)

    flat = (nb, cap * cells, cells)
    ocean_w, atmos_w = ocean_weights.reshape(flat), atmos_weights.reshape(flat)
    ocean_ids, atmos_ids = ocean_tiles.reshape(nb, cap), atmos_tiles.reshape(nb, cap)
    land = land_fraction.reshape(tiles, cells)
    blocks = (block_count, steps * local_vars, cells)
    ocean_f, atmos_f = ocean_fields.reshape(blocks), atmos_fields.reshape(blocks)
    order = ([1, nb - 1] + list(range(2, nb - 1)))[: nb - 1]
    along = lambda shift: [(b, (b + shift) % nb) for b in range(nb)]
    call = functools.partial(
        regrid, bands=nb, steps=steps, tiles=tiles, rows=steps * local_vars, cells=cells
    )

    if ng == 2 and nv == 2 and cap % 2 == 0:
        each = cap // 2
        head = (each + 1) // 2
        pieces = []
        for shift in order:
            if 2 * shift == nb:
                pieces += [(shift, 0, head, each), (shift, head, each - head, each)]
            else:
                pieces.append((shift, 0, each, each))
        *packed, own_w, send = pack(
            pieces + [(0, 0, cap, None)], ocean_w, atmos_w, ocean_ids, atmos_ids, land, ocean_f, atmos_f
        )
        sent = []
        for at, (piece, (shift, _, _, _)) in enumerate(zip(packed, pieces)):
            if at >= 2:
                piece, sent[at - 2] = lax.optimization_barrier((piece, sent[at - 2]))
            sent.append(lax.ppermute(piece, "band", along(shift)))
        keep, theirs = (ocean_f, atmos_f), (swap(send, "grp"),)
        dest = jnp.where(y == 0, ocean_dest, atmos_dest)
        block_all, used_all = slot_tables(dest, nb, cap)

        def job_of(band, parts, sizes, firsts, fields):
            meta_at = sizes[0] * cells
            tile = parts[0][meta_at + 2 * tiles, :cap].astype(jnp.int32)
            block = lax.dynamic_index_in_dim(block_all, band, 0, keepdims=False)
            used = lax.dynamic_index_in_dim(used_all, band, 0, keepdims=False)
            scale = jnp.where(used, tile + y * tiles, 2 * tiles)
            table = jnp.stack([block, tile, scale]).astype(jnp.int32)
            where = jnp.stack([band] + firsts).astype(jnp.int32)
            return table, where, parts[0], meta_at, parts, sizes, fields

        def with_fields(job, fields):
            return job[:-1] + (fields,)

        def job_at(shift, fields):
            parts, sizes, firsts = [], [], []
            for piece, across, (of, first, size, _) in zip(sent, crossed, pieces):
                if of == shift:
                    parts += [piece, across]
                    sizes += [size, size]
                    firsts += [x * each + first, (1 - x) * each + first]
            return job_of((me - shift) % nb, parts, sizes, firsts, fields)

        ours, others = [(0, keep)], [(1, theirs)]
        jobs = [job_of(me, [own_w], [cap], [jnp.int32(0)], ours)]
        rows_x = call(jobs[:1], None, groups=2)
        crossed = [swap(piece, "var") for piece in sent[:2]]
        for at in range(2, len(sent)):
            if at == 3:
                jobs.append(job_at(order[0], ours))
                rows_x = call(jobs[-1:], rows_x, groups=2)
            sent[at], rows_x = lax.optimization_barrier((sent[at], rows_x))
            crossed.append(swap(sent[at], "var"))
        done = len(jobs)
        jobs += [job_at(shift, ours) for shift in order[done - 1 :]]
        rows_x = call(
            jobs[done:-1] + [with_fields(job, others) for job in jobs[:-1]], rows_x, groups=2
        )
        rows_x = call([with_fields(jobs[-1], ours + others)], rows_x, groups=2)
        sent = embed(rows_x, embed_rows, steps, nv)
        got = lax.all_to_all(sent, ("grp", "band", "var"), split_axis=0, concat_axis=0, tiled=True)
    else:
        both = jnp.concatenate([ocean_w, atmos_w], axis=1)
        fields = [(0, (jnp.concatenate([ocean_f, atmos_f], axis=0),))]
        ocean_block, ocean_used = slot_tables(ocean_dest, nb, cap)
        atmos_block, atmos_used = slot_tables(atmos_dest, nb, cap)
        block_all = jnp.concatenate([ocean_block, atmos_block + block_count], axis=1)
        used_all = jnp.concatenate([ocean_used, atmos_used], axis=1)
        grid_row = jnp.where(jnp.arange(slots) < cap, 0, tiles)

        def job_of(band, tile, meta, parts):
            block = lax.dynamic_index_in_dim(block_all, band, 0, keepdims=False)
            used = lax.dynamic_index_in_dim(used_all, band, 0, keepdims=False)
            scale = jnp.where(used, tile + grid_row, 2 * tiles)
            table = jnp.stack([block, tile, scale]).astype(jnp.int32)
            where = jnp.stack([band, jnp.int32(0)])
            return table, where, meta, 0, [parts], [slots], fields

        tile_ids = jnp.concatenate([ocean_ids, atmos_ids], axis=1)
        own_tile = lax.dynamic_index_in_dim(tile_ids, me, 0, keepdims=False)
        own_w = lax.dynamic_index_in_dim(both, me, 0, keepdims=False)
        rows_x = call([job_of(me, own_tile, land, own_w)], None, groups=1)
        share_rows = slots * cells // rep
        high = lax.reduce_precision(land, 8, 7)
        low = (land - high).astype(jnp.bfloat16)
        tile_rows = jnp.pad(tile_ids.astype(jnp.bfloat16), ((0, 0), (0, cells - slots)))
        for shift in order:
            target, band = (me + shift) % nb, (me - shift) % nb
            piece = lax.dynamic_slice(
                both, (target, quarter * share_rows, 0), (1, share_rows, cells)
            )[0]
            row = lax.dynamic_slice(tile_rows, (target, 0), (1, cells))
            row = jnp.broadcast_to(row, (16, cells))
            piece = jnp.concatenate([piece, high.astype(jnp.bfloat16), low, row], axis=0)
            parts = lax.all_gather(lax.ppermute(piece, "band", along(shift)), REPL, axis=0)
            meta = parts[0, share_rows:]
            tile = meta[2 * tiles, :slots].astype(jnp.int32)
            parts = parts[:, :share_rows].reshape(slots * cells, cells)
            rows_x = call([job_of(band, tile, meta, parts)], rows_x, groups=1)
        sent = embed(rows_x, embed_rows, steps, nv)
        got = lax.all_to_all(sent, ("band", "var"), split_axis=0, concat_axis=0, tiled=True)
    shifted = jnp.sum(got.astype(jnp.float32), axis=0) + embed_bias
    inverse = lax.rsqrt(jnp.mean(shifted * shifted, axis=-1, keepdims=True) + 1e-05)
    finished = (shifted * inverse * embed_gain).astype(jnp.bfloat16)
    width = finished.shape[-1]
    finished = finished.reshape(nb, share, steps // nb, width).transpose(1, 0, 2, 3)
    return finished[None]


def solution(mesh):
    in_specs = (
        P(("grp", "band", "sub"), None, "var", None),
        P(("band", "sub"), None),
        P("band", "sub", None, None, None, None),
        P("band", "sub", None, None),
        P(("grp", "band", "sub"), None, "var", None),
        P(("band", "sub"), None),
        P("band", "sub", None, None, None, None),
        P("band", "sub", None, None),
        P("band", "sub", None, None, None),
        P(("var", "sub"), None),
        P(),
        P(),
    )
    out_specs = P("sub", "var", None, ("grp", "band"), None)
    return jax.shard_map(
        per_device, mesh=mesh, in_specs=in_specs, out_specs=out_specs, check_vma=False
    )
```

```python
import functools

import jax
import jax.numpy as jnp
from jax import lax
from jax.experimental import pallas as pl
from jax.experimental.pallas import tpu as pltpu
from jax.sharding import PartitionSpec as P

REPL = ("grp", "var")
PACK_LIMIT = 60 << 20
FINISH_LIMIT = 36 << 20


def slot_tables(dest, band_count, cap):
    count = dest.shape[0]
    serial = jnp.arange(count, dtype=jnp.int32)
    band_of = dest[:, 0]
    earlier = (band_of[:, None] == band_of[None, :]) & (serial[None, :] < serial[:, None])
    position = jnp.sum(earlier.astype(jnp.int32), axis=1)
    slot = band_of * cap + position
    hit = slot[None, :] == jnp.arange(band_count * cap, dtype=jnp.int32)[:, None]
    block = jnp.sum(jnp.where(hit, serial[None, :], 0), axis=1)
    used = jnp.any(hit, axis=1)
    return block.reshape(band_count, cap), used.reshape(band_count, cap)


def pack_kernel(pieces, moved, *refs):
    ocean_w, atmos_w, ocean_ids, atmos_ids, land = refs[:5]
    fields, refs = refs[5 : 5 + 2 * moved], refs[5 + 2 * moved :]
    count = len(pieces) + moved
    stages, sem = refs[:count], refs[-1]
    me, bands = lax.axis_index("band"), ocean_w.shape[0]
    x, y = lax.axis_index("var"), lax.axis_index("grp")
    cells, tiles = land.shape[-1], land.shape[0]
    cap = ocean_ids.shape[-1]

    def loads(weights, other):
        found = []
        for at, (stage, (shift, first, size, split)) in enumerate(zip(stages, pieces)):
            start = first if split is None else x * split + first
            found.append(
                pltpu.make_async_copy(
                    weights.at[
                        lax.rem(me + shift, bands),
                        pl.ds(pl.multiple_of(start * cells, cells), size * cells),
                        :,
                    ],
                    stage.at[pl.ds(0, size * cells), :],
                    sem.at[at],
                )
            )
        if moved:
            found.append(pltpu.make_async_copy(fields[other], stages[-1], sem.at[count - 1]))
        return found

    @pl.when(y == 0)
    def _():
        for copy in loads(ocean_w, 1):
            copy.start()

    @pl.when(y == 1)
    def _():
        for copy in loads(atmos_w, 0):
            copy.start()

    fraction = land[...]
    high = fraction.astype(jnp.bfloat16)
    low = (fraction - high.astype(jnp.float32)).astype(jnp.bfloat16)
    for stage, (shift, first, size, split) in zip(stages, pieces):
        if first:
            continue
        target, base = lax.rem(me + shift, bands), size * cells
        stage[pl.ds(base, tiles), :] = high
        stage[pl.ds(base + tiles, tiles), :] = low
        row = jnp.where(y == 0, ocean_ids[pl.ds(target, 1), :], atmos_ids[pl.ds(target, 1), :])
        row = jnp.broadcast_to(row.astype(jnp.float32), (16, cap)).astype(jnp.bfloat16)
        stage[pl.ds(base + 2 * tiles, 16), :] = jnp.zeros((16, cells), jnp.bfloat16)
        stage[pl.ds(base + 2 * tiles, 16), pl.ds(0, cap)] = row
    for load in loads(ocean_w, 1):
        load.wait()


def pack(pieces, ocean_w, atmos_w, ocean_ids, atmos_ids, land, *fields):
    cells, tiles = land.shape[-1], land.shape[0]
    any_spec = pl.BlockSpec(memory_space=pl.ANY)
    vmem = pl.BlockSpec(memory_space=pltpu.VMEM)
    sizes = [size * cells + (0 if first else 2 * tiles + 16) for _, first, size, _ in pieces]
    shapes = [(n, cells) for n in sizes] + [f.shape for f in fields[:1]]
    return pl.pallas_call(
        functools.partial(pack_kernel, pieces, len(fields) // 2),
        out_shape=[jax.ShapeDtypeStruct(shape, jnp.bfloat16) for shape in shapes],
        in_specs=[any_spec] * 2 + [vmem] * 3 + [any_spec] * len(fields),
        out_specs=[vmem] * len(shapes),
        scratch_shapes=[pltpu.SemaphoreType.DMA((len(shapes),))],
        cost_estimate=pl.CostEstimate(flops=0, bytes_accessed=2 << 20, transcendentals=0),
        compiler_params=pltpu.CompilerParams(vmem_limit_bytes=PACK_LIMIT),
    )(ocean_w, atmos_w, ocean_ids, atmos_ids, land, *fields)


def run_jobs(steps, jobs, refs, out, acc, scale):
    local_rows, cells = acc.shape[1] // (scale.shape[0] // 2 - 4), acc.shape[2]
    tiles = acc.shape[1] // local_rows
    local_vars = local_rows // steps
    half_vars = local_vars // 2
    for table, where, meta, meta_at, parts, groups in jobs:
        table, where, meta = refs[table], refs[where], refs[meta]
        if meta.dtype == jnp.float32:
            land = meta[...]
        else:
            high = meta[pl.ds(meta_at, tiles), :].astype(jnp.float32)
            land = high + meta[pl.ds(meta_at + tiles, tiles), :].astype(jnp.float32)
        scale[pl.ds(0, tiles), :] = 1.0 - land
        scale[pl.ds(tiles, tiles), :] = land
        scale[pl.ds(2 * tiles, 8), :] = jnp.zeros((8, cells), jnp.float32)
        acc[pl.ds(0, len(groups))] = jnp.zeros((len(groups),) + acc.shape[1:], jnp.float32)
        for at, (part, size) in enumerate(parts):
            first = where[1 + at]
            for s in range(size):
                slot = first + s
                block = table[0, slot]
                moved = []
                for _, fields in groups:
                    piece = refs[fields[0]][block]
                    if len(fields) > 1:
                        piece = jnp.where(
                            lax.axis_index("grp") == 0, piece, refs[fields[1]][block]
                        )
                    moved.append(piece)
                moved = moved[0] if len(moved) == 1 else jnp.concatenate(moved, axis=0)
                dense = jnp.dot(
                    moved,
                    refs[part][pl.ds(s * cells, cells), :],
                    preferred_element_type=jnp.float32,
                )
                dense = dense * scale[pl.ds(table[2, slot], 1), :]
                span = pl.ds(pl.multiple_of(table[1, slot] * local_rows, local_rows), local_rows)
                for g in range(len(groups)):
                    acc[g, span, :] += dense[g * local_rows : (g + 1) * local_rows]
        for g, (to, _) in enumerate(groups):
            for v in range(local_vars):
                for q in range(2):
                    column = (v % half_vars * 2 + q) * cells
                    rows = [
                        acc[g, pl.ds(q * local_rows + t * local_vars + v, tiles // 2, 2 * local_rows), :]
                        for t in range(steps)
                    ]
                    out[where[0], to, v // half_vars, :, pl.ds(column, cells)] = jnp.concatenate(
                        rows, axis=0
                    ).astype(out.dtype)


def regrid_kernel(steps, jobs, *refs):
    run_jobs(steps, jobs, refs, *refs[-3:])


def finish_kernel(steps, halves, jobs, count, *refs):
    theirs, mine, rows_x, out, acc, scale, weight, total, sem = refs[count:]
    sub, mine_group = lax.axis_index("sub"), lax.axis_index("grp")
    chunks = sem.shape[0]
    height = mine.shape[0] // chunks

    def span(chunk):
        return pl.ds(pl.multiple_of(chunk * height, height), height)

    def copy(chunk):
        return pltpu.make_async_copy(
            mine.at[span(chunk), :], weight.at[span(chunk), :], sem.at[chunk]
        )

    def add(chunk, place, source):
        left = rows_x[:, :, place, :, span(chunk)].reshape(total.shape[0], height)
        total[...] += jnp.dot(left, source[span(chunk), :], preferred_element_type=jnp.float32)

    for chunk in range(chunks):
        copy(chunk).start()
    run_jobs(steps, jobs, refs, rows_x, acc, scale)
    total[...] = jnp.zeros_like(total)

    @pl.loop(0, chunks)
    def _(chunk):
        add(chunk, 1 - sub, theirs)

    @pl.loop(0, chunks)
    def _(chunk):
        copy(chunk).wait()
        add(chunk, sub, weight)

    send_rows(steps, halves, rows_x.shape, mine_group, total, out)


def send_rows(steps, halves, shape, mine_group, total, out):
    bands, groups, _, row_count, _ = shape
    count = steps * halves
    share = row_count // count
    for g in range(groups):
        base = (mine_group if g == 0 else 1 - mine_group) * count if groups > 1 else 0
        for chunk in range(count):
            pieces = [
                total[pl.ds((b * groups + g) * row_count + chunk * share, share), :]
                for b in range(bands)
            ]
            out[base + chunk] = jnp.concatenate(pieces, axis=0).astype(out.dtype)


def regrid(jobs, previous, bands, groups, steps, tiles, rows, cells, last=None):
    operands, specs, places = [], [], {}

    def place(array, space):
        if id(array) not in places:
            places[id(array)] = len(operands)
            operands.append(array)
            specs.append(pl.BlockSpec(memory_space=space))
        return places[id(array)]

    listed, flops, most = [], 0, 1
    for table, where, meta, meta_at, parts, sizes, fields in jobs:
        listed.append(
            (
                place(table, pltpu.SMEM),
                place(where, pltpu.SMEM),
                place(meta, pltpu.VMEM),
                meta_at,
                [(place(part, pltpu.VMEM), size) for part, size in zip(parts, sizes)],
                [(to, [place(f, pltpu.VMEM) for f in pair]) for to, pair in fields],
            )
        )
        flops += 2 * sum(sizes) * len(fields) * rows * cells * cells
        most = max(most, len(fields))
    aliases = {}
    vmem = pl.BlockSpec(memory_space=pltpu.VMEM)
    if previous is not None:
        aliases = {len(operands): 0}
        operands.append(previous)
        specs.append(vmem)
    shape = (bands, groups, 2, steps * tiles // 2, rows // steps // 2 * 2 * cells)
    shapes = [jax.ShapeDtypeStruct(shape, jnp.bfloat16)]
    scratch = [
        pltpu.VMEM((most, tiles * rows, cells), jnp.float32),
        pltpu.VMEM((2 * tiles + 8, cells), jnp.float32),
    ]
    if last is None:
        body = functools.partial(regrid_kernel, steps, listed)
        limit, moved = 12 << 20, len(jobs) * 3 << 20
    else:
        mine, theirs, halves = last
        height, width = mine.shape
        total = bands * groups * shape[3]
        body = functools.partial(finish_kernel, steps, halves, listed, len(operands))
        operands += [theirs, mine]
        specs += [vmem, pl.BlockSpec(memory_space=pl.ANY)]
        count = groups * steps * halves
        shapes.append(jax.ShapeDtypeStruct((count, total // count, width), jnp.bfloat16))
        scratch += [
            pltpu.VMEM((height, width), jnp.bfloat16),
            pltpu.VMEM((total, width), jnp.float32),
            pltpu.SemaphoreType.DMA((6,)),
        ]
        limit, moved = FINISH_LIMIT, 4 * height * width
        flops += 4 * total * height * width
    done = pl.pallas_call(
        body,
        out_shape=shapes,
        in_specs=specs,
        out_specs=[vmem] * len(shapes),
        scratch_shapes=scratch,
        input_output_aliases=aliases,
        cost_estimate=pl.CostEstimate(flops=flops, bytes_accessed=moved, transcendentals=0),
        compiler_params=pltpu.CompilerParams(vmem_limit_bytes=limit),
    )(*operands)
    return done[-1]


def embed_kernel(steps, halves, rows_x, mine, theirs, out, total):
    at = pl.program_id(0)
    sub, mine_group = lax.axis_index("sub"), lax.axis_index("grp")
    bands, groups, _, row_count, width = rows_x.shape
    rows = bands * groups * row_count

    @pl.when(at == 0)
    def _():
        total[...] = jnp.zeros_like(total)

    left = rows_x[:, :, sub].reshape(rows, width)
    right = rows_x[:, :, 1 - sub].reshape(rows, width)
    total[...] += jnp.dot(left, mine[...], preferred_element_type=jnp.float32) + jnp.dot(
        right, theirs[...], preferred_element_type=jnp.float32
    )

    @pl.when(at == pl.num_programs(0) - 1)
    def _():
        if out.ndim == 2:
            out[...] = total[...].astype(out.dtype)
        else:
            send_rows(steps, halves, rows_x.shape, mine_group, total, out)


def embed(rows_x, mine, theirs, steps, halves):
    bands, groups, _, row_count, half_width = rows_x.shape
    width = mine.shape[-1]
    grid = 6 if half_width % (6 * 256) == 0 else 3
    step_rows = half_width // grid
    rows = bands * groups * row_count
    chunks = groups * steps * halves
    share = row_count // (steps * halves)
    shape = (chunks, bands * share, width) if share % 4 == 0 else (rows, width)
    weight_spec = pl.BlockSpec((step_rows, width), lambda i: (i, 0))
    out = pl.pallas_call(
        functools.partial(embed_kernel, steps, halves),
        out_shape=jax.ShapeDtypeStruct(shape, jnp.bfloat16),
        grid=(grid,),
        in_specs=[
            pl.BlockSpec((bands, groups, 2, row_count, step_rows), lambda i: (0, 0, 0, 0, i)),
            weight_spec,
            weight_spec,
        ],
        out_specs=pl.BlockSpec(shape, lambda i: (0,) * len(shape)),
        scratch_shapes=[pltpu.VMEM((rows, width), jnp.float32)],
        cost_estimate=pl.CostEstimate(
            flops=4 * rows * mine.shape[0] * width,
            bytes_accessed=4 * mine.shape[0] * width,
            transcendentals=0,
        ),
        compiler_params=pltpu.CompilerParams(
            vmem_limit_bytes=(48 if rows > 1024 else 16) << 20
        ),
    )(rows_x, mine, theirs)
    if share % 4:
        out = out.reshape(bands, chunks, share, width).transpose(1, 0, 2, 3)
        out = out.reshape(chunks, bands * share, width)
    return out


def swap(x, axis):
    return lax.ppermute(x, axis, [(0, 1), (1, 0)])


def per_device(
    ocean_fields,
    ocean_dest,
    ocean_weights,
    ocean_tiles,
    atmos_fields,
    atmos_dest,
    atmos_weights,
    atmos_tiles,
    land_fraction,
    embed_weight,
    embed_bias,
    embed_gain,
):
    nb = lax.axis_size("band")
    nv = lax.axis_size("var")
    ng = lax.axis_size("grp")
    rep = nv * ng
    cap = ocean_weights.shape[3]
    cells = ocean_weights.shape[-1]
    block_count, steps, local_vars, _ = ocean_fields.shape
    patches = land_fraction.shape[2]
    tiles = 2 * patches
    slots = 2 * cap
    share = patches // nv
    me = lax.axis_index("band")
    x, y = lax.axis_index("var"), lax.axis_index("grp")
    quarter = y * nv + x

    flat = (nb, cap * cells, cells)
    ocean_w, atmos_w = ocean_weights.reshape(flat), atmos_weights.reshape(flat)
    ocean_ids, atmos_ids = ocean_tiles.reshape(nb, cap), atmos_tiles.reshape(nb, cap)
    land = land_fraction.reshape(tiles, cells)
    blocks = (block_count, steps * local_vars, cells)
    ocean_f, atmos_f = ocean_fields.reshape(blocks), atmos_fields.reshape(blocks)
    order = ([1, nb - 1] + list(range(2, nb - 1)))[: nb - 1]
    along = lambda shift: [(b, (b + shift) % nb) for b in range(nb)]
    call = functools.partial(
        regrid, bands=nb, steps=steps, tiles=tiles, rows=steps * local_vars, cells=cells
    )

    if ng == 2 and nv == 2 and cap % 2 == 0:
        each = cap // 2
        pieces = []
        for shift in order:
            pieces.append((shift, 0, each, each))
        *packed, own_w, send = pack(
            pieces + [(0, 0, cap, None)], ocean_w, atmos_w, ocean_ids, atmos_ids, land, ocean_f, atmos_f
        )
        sent = []
        for at, (piece, (shift, _, _, _)) in enumerate(zip(packed, pieces)):
            if at >= 2:
                piece, sent[at - 2] = lax.optimization_barrier((piece, sent[at - 2]))
            sent.append(lax.ppermute(piece, "band", along(shift)))
        embed_other, send = lax.optimization_barrier((embed_weight, send))
        embed_other = swap(embed_other, "sub")
        keep, theirs = (ocean_f, atmos_f), (swap(send, "grp"),)
        dest = jnp.where(y == 0, ocean_dest, atmos_dest)
        block_all, used_all = slot_tables(dest, nb, cap)

        def job_of(band, parts, sizes, firsts, fields):
            meta_at = sizes[0] * cells
            tile = parts[0][meta_at + 2 * tiles, :cap].astype(jnp.int32)
            block = lax.dynamic_index_in_dim(block_all, band, 0, keepdims=False)
            used = lax.dynamic_index_in_dim(used_all, band, 0, keepdims=False)
            scale = jnp.where(used, tile + y * tiles, 2 * tiles)
            table = jnp.stack([block, tile, scale]).astype(jnp.int32)
            where = jnp.stack([band] + firsts).astype(jnp.int32)
            return table, where, parts[0], meta_at, parts, sizes, fields

        def with_fields(job, fields):
            return job[:-1] + (fields,)

        def job_at(shift, fields):
            parts, sizes, firsts = [], [], []
            for piece, across, (of, first, size, _) in zip(sent, crossed, pieces):
                if of == shift:
                    parts += [piece, across]
                    sizes += [size, size]
                    firsts += [x * each + first, (1 - x) * each + first]
            return job_of((me - shift) % nb, parts, sizes, firsts, fields)

        ours, others = [(0, keep)], [(1, theirs)]
        jobs = [job_of(me, [own_w], [cap], [jnp.int32(0)], ours)]
        rows_x = call(jobs[:1], None, groups=2)
        crossed = [swap(piece, "var") for piece in sent[:2]]
        for at in range(2, len(sent)):
            jobs.append(job_at(order[at - 2], ours))
            rows_x = call(jobs[-1:], rows_x, groups=2)
            sent[at], rows_x = lax.optimization_barrier((sent[at], rows_x))
            crossed.append(swap(sent[at], "var"))
        done = len(jobs)
        jobs += [job_at(shift, ours) for shift in order[done - 1 :]]
        rows_x = call(
            jobs[done:-1] + [with_fields(job, others) for job in jobs[:-1]], rows_x, groups=2
        )
        sent = call(
            [with_fields(jobs[-1], ours + others)],
            rows_x,
            groups=2,
            last=(embed_weight, embed_other, nv),
        )
        got = lax.all_to_all(sent, ("grp", "band", "var"), split_axis=0, concat_axis=0, tiled=True)
    else:
        embed_other = swap(embed_weight, "sub")
        both = jnp.concatenate([ocean_w, atmos_w], axis=1)
        fields = [(0, (jnp.concatenate([ocean_f, atmos_f], axis=0),))]
        ocean_block, ocean_used = slot_tables(ocean_dest, nb, cap)
        atmos_block, atmos_used = slot_tables(atmos_dest, nb, cap)
        block_all = jnp.concatenate([ocean_block, atmos_block + block_count], axis=1)
        used_all = jnp.concatenate([ocean_used, atmos_used], axis=1)
        grid_row = jnp.where(jnp.arange(slots) < cap, 0, tiles)

        def job_of(band, tile, meta, parts):
            block = lax.dynamic_index_in_dim(block_all, band, 0, keepdims=False)
            used = lax.dynamic_index_in_dim(used_all, band, 0, keepdims=False)
            scale = jnp.where(used, tile + grid_row, 2 * tiles)
            table = jnp.stack([block, tile, scale]).astype(jnp.int32)
            where = jnp.stack([band, jnp.int32(0)])
            return table, where, meta, 0, [parts], [slots], fields

        tile_ids = jnp.concatenate([ocean_ids, atmos_ids], axis=1)
        own_tile = lax.dynamic_index_in_dim(tile_ids, me, 0, keepdims=False)
        own_w = lax.dynamic_index_in_dim(both, me, 0, keepdims=False)
        rows_x = call([job_of(me, own_tile, land, own_w)], None, groups=1)
        share_rows = slots * cells // rep
        high = lax.reduce_precision(land, 8, 7)
        low = (land - high).astype(jnp.bfloat16)
        tile_rows = jnp.pad(tile_ids.astype(jnp.bfloat16), ((0, 0), (0, cells - slots)))
        for shift in order:
            target, band = (me + shift) % nb, (me - shift) % nb
            piece = lax.dynamic_slice(
                both, (target, quarter * share_rows, 0), (1, share_rows, cells)
            )[0]
            row = lax.dynamic_slice(tile_rows, (target, 0), (1, cells))
            row = jnp.broadcast_to(row, (16, cells))
            piece = jnp.concatenate([piece, high.astype(jnp.bfloat16), low, row], axis=0)
            parts = lax.all_gather(lax.ppermute(piece, "band", along(shift)), REPL, axis=0)
            meta = parts[0, share_rows:]
            tile = meta[2 * tiles, :slots].astype(jnp.int32)
            parts = parts[:, :share_rows].reshape(slots * cells, cells)
            rows_x = call([job_of(band, tile, meta, parts)], rows_x, groups=1)
        sent = embed(rows_x, embed_weight, embed_other, steps, nv)
        got = lax.all_to_all(sent, ("band", "var"), split_axis=0, concat_axis=0, tiled=True)
    shifted = jnp.sum(got.astype(jnp.float32), axis=0) + embed_bias
    inverse = lax.rsqrt(jnp.mean(shifted * shifted, axis=-1, keepdims=True) + 1e-05)
    finished = (shifted * inverse * embed_gain).astype(jnp.bfloat16)
    width = finished.shape[-1]
    finished = finished.reshape(nb, share, steps // nb, width).transpose(1, 0, 2, 3)
    return finished[None]


def solution(mesh):
    in_specs = (
        P(("grp", "band", "sub"), None, "var", None),
        P(("band", "sub"), None),
        P("band", "sub", None, None, None, None),
        P("band", "sub", None, None),
        P(("grp", "band", "sub"), None, "var", None),
        P(("band", "sub"), None),
        P("band", "sub", None, None, None, None),
        P("band", "sub", None, None),
        P("band", "sub", None, None, None),
        P(("var", "sub"), None),
        P(),
        P(),
    )
    out_specs = P("sub", "var", None, ("grp", "band"), None)
    return jax.shard_map(
        per_device, mesh=mesh, in_specs=in_specs, out_specs=out_specs, check_vma=False
    )
```

```python
import functools

import jax
import jax.numpy as jnp
from jax import lax
from jax.experimental import pallas as pl
from jax.experimental.pallas import tpu as pltpu
from jax.sharding import PartitionSpec as P

REPL = ("grp", "var")


def slot_tables(dest, band_count, cap):
    count = dest.shape[0]
    serial = jnp.arange(count, dtype=jnp.int32)
    band_of = dest[:, 0]
    earlier = (band_of[:, None] == band_of[None, :]) & (serial[None, :] < serial[:, None])
    position = jnp.sum(earlier.astype(jnp.int32), axis=1)
    slot = band_of * cap + position
    hit = slot[None, :] == jnp.arange(band_count * cap, dtype=jnp.int32)[:, None]
    block = jnp.sum(jnp.where(hit, serial[None, :], 0), axis=1)
    used = jnp.any(hit, axis=1)
    return block.reshape(band_count, cap), used.reshape(band_count, cap)


def pack_kernel(pieces, moved, *refs):
    ocean_w, atmos_w, ocean_ids, atmos_ids, land = refs[:5]
    fields, refs = refs[5 : 5 + 2 * moved], refs[5 + 2 * moved :]
    count = len(pieces) + moved
    stages, sem = refs[:count], refs[-1]
    me, bands = lax.axis_index("band"), ocean_w.shape[0]
    x, y = lax.axis_index("var"), lax.axis_index("grp")
    cells, tiles = land.shape[-1], land.shape[0]
    cap = ocean_ids.shape[-1]

    def loads(weights, other):
        found = []
        for at, (stage, (shift, first, size, split)) in enumerate(zip(stages, pieces)):
            start = first if split is None else x * split + first
            found.append(
                pltpu.make_async_copy(
                    weights.at[
                        lax.rem(me + shift, bands),
                        pl.ds(pl.multiple_of(start * cells, cells), size * cells),
                        :,
                    ],
                    stage.at[pl.ds(0, size * cells), :],
                    sem.at[at],
                )
            )
        if moved:
            found.append(pltpu.make_async_copy(fields[other], stages[-1], sem.at[count - 1]))
        return found

    @pl.when(y == 0)
    def _():
        for copy in loads(ocean_w, 1):
            copy.start()

    @pl.when(y == 1)
    def _():
        for copy in loads(atmos_w, 0):
            copy.start()

    fraction = land[...]
    high = fraction.astype(jnp.bfloat16)
    low = (fraction - high.astype(jnp.float32)).astype(jnp.bfloat16)
    for stage, (shift, first, size, split) in zip(stages, pieces):
        if first:
            continue
        target, base = lax.rem(me + shift, bands), size * cells
        stage[pl.ds(base, tiles), :] = high
        stage[pl.ds(base + tiles, tiles), :] = low
        row = jnp.where(y == 0, ocean_ids[pl.ds(target, 1), :], atmos_ids[pl.ds(target, 1), :])
        row = jnp.broadcast_to(row.astype(jnp.float32), (16, cap)).astype(jnp.bfloat16)
        stage[pl.ds(base + 2 * tiles, 16), :] = jnp.zeros((16, cells), jnp.bfloat16)
        stage[pl.ds(base + 2 * tiles, 16), pl.ds(0, cap)] = row
    for load in loads(ocean_w, 1):
        load.wait()


def pack(limit, pieces, ocean_w, atmos_w, ocean_ids, atmos_ids, land, *fields):
    cells, tiles = land.shape[-1], land.shape[0]
    any_spec = pl.BlockSpec(memory_space=pl.ANY)
    vmem = pl.BlockSpec(memory_space=pltpu.VMEM)
    sizes = [size * cells + (0 if first else 2 * tiles + 16) for _, first, size, _ in pieces]
    shapes = [(n, cells) for n in sizes] + [f.shape for f in fields[:1]]
    return pl.pallas_call(
        functools.partial(pack_kernel, pieces, len(fields) // 2),
        out_shape=[jax.ShapeDtypeStruct(shape, jnp.bfloat16) for shape in shapes],
        in_specs=[any_spec] * 2 + [vmem] * 3 + [any_spec] * len(fields),
        out_specs=[vmem] * len(shapes),
        scratch_shapes=[pltpu.SemaphoreType.DMA((len(shapes),))],
        cost_estimate=pl.CostEstimate(flops=0, bytes_accessed=2 << 20, transcendentals=0),
        compiler_params=pltpu.CompilerParams(vmem_limit_bytes=limit << 20),
    )(ocean_w, atmos_w, ocean_ids, atmos_ids, land, *fields)


def run_jobs(steps, jobs, refs, out, acc, scale):
    local_rows, cells = acc.shape[1] // (scale.shape[0] // 2 - 4), acc.shape[2]
    tiles = acc.shape[1] // local_rows
    local_vars = local_rows // steps
    half_vars = local_vars // 2
    for table, where, meta, meta_at, parts, groups in jobs:
        table, where, meta = refs[table], refs[where], refs[meta]
        if meta.dtype == jnp.float32:
            land = meta[...]
        else:
            high = meta[pl.ds(meta_at, tiles), :].astype(jnp.float32)
            land = high + meta[pl.ds(meta_at + tiles, tiles), :].astype(jnp.float32)
        scale[pl.ds(0, tiles), :] = 1.0 - land
        scale[pl.ds(tiles, tiles), :] = land
        scale[pl.ds(2 * tiles, 8), :] = jnp.zeros((8, cells), jnp.float32)
        acc[pl.ds(0, len(groups))] = jnp.zeros((len(groups),) + acc.shape[1:], jnp.float32)
        for at, (part, size) in enumerate(parts):
            first = where[1 + at]
            for s in range(size):
                slot = first + s
                block = table[0, slot]
                moved = []
                for _, fields in groups:
                    piece = refs[fields[0]][block]
                    if len(fields) > 1:
                        piece = jnp.where(
                            lax.axis_index("grp") == 0, piece, refs[fields[1]][block]
                        )
                    moved.append(piece)
                moved = moved[0] if len(moved) == 1 else jnp.concatenate(moved, axis=0)
                dense = jnp.dot(
                    moved,
                    refs[part][pl.ds(s * cells, cells), :],
                    preferred_element_type=jnp.float32,
                )
                dense = dense * scale[pl.ds(table[2, slot], 1), :]
                span = pl.ds(pl.multiple_of(table[1, slot] * local_rows, local_rows), local_rows)
                for g in range(len(groups)):
                    acc[g, span, :] += dense[g * local_rows : (g + 1) * local_rows]
        for g, (to, _) in enumerate(groups):
            for v in range(local_vars):
                for q in range(2):
                    column = (v % half_vars * 2 + q) * cells
                    rows = [
                        acc[g, pl.ds(q * local_rows + t * local_vars + v, tiles // 2, 2 * local_rows), :]
                        for t in range(steps)
                    ]
                    out[where[0], to, v // half_vars, :, pl.ds(column, cells)] = jnp.concatenate(
                        rows, axis=0
                    ).astype(out.dtype)


def regrid_kernel(steps, jobs, *refs):
    run_jobs(steps, jobs, refs, *refs[-3:])


def finish_kernel(steps, halves, jobs, count, *refs):
    theirs, mine, rows_x, out, acc, scale, weight, total, sem = refs[count:]
    sub, mine_group = lax.axis_index("sub"), lax.axis_index("grp")
    blocks = sem.shape[0]
    width = mine.shape[1] // blocks

    def copy(block):
        span = pl.ds(block * width, width)
        return pltpu.make_async_copy(mine.at[:, span], weight.at[:, span], sem.at[block])

    for block in range(blocks):
        copy(block).start()
    run_jobs(steps, jobs, refs, rows_x, acc, scale)
    for block in range(blocks):
        span = pl.ds(block * width, width)
        left, right = (
            rows_x[:, :, place].reshape(total.shape[0], mine.shape[0]) for place in (1 - sub, sub)
        )
        some = jnp.dot(left, theirs[:, span], preferred_element_type=jnp.float32)
        copy(block).wait()
        total[:, span] = some + jnp.dot(
            right, weight[:, span], preferred_element_type=jnp.float32
        )
    send_rows(steps, halves, rows_x.shape, mine_group, total, out)


def send_rows(steps, halves, shape, mine_group, total, out):
    bands, groups, _, row_count, _ = shape
    count = steps * halves
    share = row_count // count
    for g in range(groups):
        base = (mine_group if g == 0 else 1 - mine_group) * count if groups > 1 else 0
        for chunk in range(count):
            pieces = [
                total[pl.ds((b * groups + g) * row_count + chunk * share, share), :]
                for b in range(bands)
            ]
            out[base + chunk] = jnp.concatenate(pieces, axis=0).astype(out.dtype)


def regrid(jobs, previous, bands, groups, steps, tiles, rows, cells, last=None):
    operands, specs, places = [], [], {}

    def place(array, space):
        if id(array) not in places:
            places[id(array)] = len(operands)
            operands.append(array)
            specs.append(pl.BlockSpec(memory_space=space))
        return places[id(array)]

    listed, flops, most = [], 0, 1
    for table, where, meta, meta_at, parts, sizes, fields in jobs:
        listed.append(
            (
                place(table, pltpu.SMEM),
                place(where, pltpu.SMEM),
                place(meta, pltpu.VMEM),
                meta_at,
                [(place(part, pltpu.VMEM), size) for part, size in zip(parts, sizes)],
                [(to, [place(f, pltpu.VMEM) for f in pair]) for to, pair in fields],
            )
        )
        flops += 2 * sum(sizes) * len(fields) * rows * cells * cells
        most = max(most, len(fields))
    aliases = {}
    vmem = pl.BlockSpec(memory_space=pltpu.VMEM)
    if previous is not None:
        aliases = {len(operands): 0}
        operands.append(previous)
        specs.append(vmem)
    shape = (bands, groups, 2, steps * tiles // 2, rows // steps // 2 * 2 * cells)
    shapes = [jax.ShapeDtypeStruct(shape, jnp.bfloat16)]
    scratch = [
        pltpu.VMEM((most, tiles * rows, cells), jnp.float32),
        pltpu.VMEM((2 * tiles + 8, cells), jnp.float32),
    ]
    if last is None:
        body = functools.partial(regrid_kernel, steps, listed)
        limit, moved = 12 << 20, len(jobs) * 3 << 20
    else:
        mine, theirs, halves = last
        height, width = mine.shape
        total = bands * groups * shape[3]
        body = functools.partial(finish_kernel, steps, halves, listed, len(operands))
        operands += [theirs, mine]
        specs += [vmem, pl.BlockSpec(memory_space=pl.ANY)]
        count = groups * steps * halves
        shapes.append(jax.ShapeDtypeStruct((count, total // count, width), jnp.bfloat16))
        scratch += [
            pltpu.VMEM((height, width), jnp.bfloat16),
            pltpu.VMEM((total, width), jnp.float32),
            pltpu.SemaphoreType.DMA((4,)),
        ]
        limit, moved = 36 << 20, 4 * height * width
        flops += 4 * total * height * width
    done = pl.pallas_call(
        body,
        out_shape=shapes,
        in_specs=specs,
        out_specs=[vmem] * len(shapes),
        scratch_shapes=scratch,
        input_output_aliases=aliases,
        cost_estimate=pl.CostEstimate(flops=flops, bytes_accessed=moved, transcendentals=0),
        compiler_params=pltpu.CompilerParams(vmem_limit_bytes=limit),
    )(*operands)
    return done[-1]


def embed_kernel(steps, halves, rows_x, mine, theirs, out, total):
    at = pl.program_id(0)
    sub, mine_group = lax.axis_index("sub"), lax.axis_index("grp")
    bands, groups, _, row_count, width = rows_x.shape
    rows = bands * groups * row_count

    @pl.when(at == 0)
    def _():
        total[...] = jnp.zeros_like(total)

    left = rows_x[:, :, sub].reshape(rows, width)
    right = rows_x[:, :, 1 - sub].reshape(rows, width)
    total[...] += jnp.dot(left, mine[...], preferred_element_type=jnp.float32) + jnp.dot(
        right, theirs[...], preferred_element_type=jnp.float32
    )

    @pl.when(at == pl.num_programs(0) - 1)
    def _():
        if out.ndim == 2:
            out[...] = total[...].astype(out.dtype)
        else:
            send_rows(steps, halves, rows_x.shape, mine_group, total, out)


def embed(rows_x, mine, theirs, steps, halves):
    bands, groups, _, row_count, half_width = rows_x.shape
    width = mine.shape[-1]
    grid = 6 if half_width % (6 * 256) == 0 else 3
    step_rows = half_width // grid
    rows = bands * groups * row_count
    chunks = groups * steps * halves
    share = row_count // (steps * halves)
    shape = (chunks, bands * share, width) if share % 4 == 0 else (rows, width)
    weight_spec = pl.BlockSpec((step_rows, width), lambda i: (i, 0))
    out = pl.pallas_call(
        functools.partial(embed_kernel, steps, halves),
        out_shape=jax.ShapeDtypeStruct(shape, jnp.bfloat16),
        grid=(grid,),
        in_specs=[
            pl.BlockSpec((bands, groups, 2, row_count, step_rows), lambda i: (0, 0, 0, 0, i)),
            weight_spec,
            weight_spec,
        ],
        out_specs=pl.BlockSpec(shape, lambda i: (0,) * len(shape)),
        scratch_shapes=[pltpu.VMEM((rows, width), jnp.float32)],
        cost_estimate=pl.CostEstimate(
            flops=4 * rows * mine.shape[0] * width,
            bytes_accessed=4 * mine.shape[0] * width,
            transcendentals=0,
        ),
        compiler_params=pltpu.CompilerParams(
            vmem_limit_bytes=(48 if rows > 1024 else 16) << 20
        ),
    )(rows_x, mine, theirs)
    if share % 4:
        out = out.reshape(bands, chunks, share, width).transpose(1, 0, 2, 3)
        out = out.reshape(chunks, bands * share, width)
    return out


def swap(x, axis):
    return lax.ppermute(x, axis, [(0, 1), (1, 0)])


def per_device(
    ocean_fields,
    ocean_dest,
    ocean_weights,
    ocean_tiles,
    atmos_fields,
    atmos_dest,
    atmos_weights,
    atmos_tiles,
    land_fraction,
    embed_weight,
    embed_bias,
    embed_gain,
):
    nb = lax.axis_size("band")
    nv = lax.axis_size("var")
    ng = lax.axis_size("grp")
    rep = nv * ng
    cap = ocean_weights.shape[3]
    cells = ocean_weights.shape[-1]
    block_count, steps, local_vars, _ = ocean_fields.shape
    patches = land_fraction.shape[2]
    tiles = 2 * patches
    slots = 2 * cap
    share = patches // nv
    me = lax.axis_index("band")
    x, y = lax.axis_index("var"), lax.axis_index("grp")
    quarter = y * nv + x

    flat = (nb, cap * cells, cells)
    ocean_w, atmos_w = ocean_weights.reshape(flat), atmos_weights.reshape(flat)
    ocean_ids, atmos_ids = ocean_tiles.reshape(nb, cap), atmos_tiles.reshape(nb, cap)
    land = land_fraction.reshape(tiles, cells)
    blocks = (block_count, steps * local_vars, cells)
    ocean_f, atmos_f = ocean_fields.reshape(blocks), atmos_fields.reshape(blocks)
    order = ([1, nb - 1] + list(range(2, nb - 1)))[: nb - 1]
    along = lambda shift: [(b, (b + shift) % nb) for b in range(nb)]
    call = functools.partial(
        regrid, bands=nb, steps=steps, tiles=tiles, rows=steps * local_vars, cells=cells
    )

    if ng == 2 and nv == 2 and cap % 2 == 0:
        each = cap // 2
        pieces = []
        for shift in order:
            pieces.append((shift, 0, each, each))
        *packed, send = pack(
            60, pieces, ocean_w, atmos_w, ocean_ids, atmos_ids, land, ocean_f, atmos_f
        )
        sent = []
        for at, (piece, (shift, _, _, _)) in enumerate(zip(packed, pieces)):
            if at >= 2:
                piece, sent[at - 2] = lax.optimization_barrier((piece, sent[at - 2]))
            sent.append(lax.ppermute(piece, "band", along(shift)))
        embed_other, own_land, send = lax.optimization_barrier((embed_weight, land, send))
        own_w = pack(54, [(0, 0, cap, None)], ocean_w, atmos_w, ocean_ids, atmos_ids, own_land)[0]
        embed_other = swap(embed_other, "sub")
        keep, theirs = (ocean_f, atmos_f), (swap(send, "grp"),)
        dest = jnp.where(y == 0, ocean_dest, atmos_dest)
        block_all, used_all = slot_tables(dest, nb, cap)
        def job_of(band, parts, sizes, firsts, fields):
            meta_at = sizes[0] * cells
            tile = parts[0][meta_at + 2 * tiles, :cap].astype(jnp.int32)
            block = lax.dynamic_index_in_dim(block_all, band, 0, keepdims=False)
            used = lax.dynamic_index_in_dim(used_all, band, 0, keepdims=False)
            scale = jnp.where(used, tile + y * tiles, 2 * tiles)
            table = jnp.stack([block, tile, scale]).astype(jnp.int32)
            where = jnp.stack([band] + firsts).astype(jnp.int32)
            return table, where, parts[0], meta_at, parts, sizes, fields

        def with_fields(job, fields):
            return job[:-1] + (fields,)

        def job_at(shift, fields):
            parts, sizes, firsts = [], [], []
            for piece, across, (of, first, size, _) in zip(sent, crossed, pieces):
                if of == shift:
                    parts += [piece, across]
                    sizes += [size, size]
                    firsts += [x * each + first, (1 - x) * each + first]
            return job_of((me - shift) % nb, parts, sizes, firsts, fields)

        ours, others = [(0, keep)], [(1, theirs)]
        jobs = [job_of(me, [own_w], [cap], [jnp.int32(0)], ours)]
        rows_x = call(jobs[:1], None, groups=2)
        crossed = [swap(piece, "var") for piece in sent[:2]]
        for at in range(2, len(sent)):
            jobs.append(job_at(order[at - 2], ours))
            rows_x = call(jobs[-1:], rows_x, groups=2)
            sent[at], rows_x = lax.optimization_barrier((sent[at], rows_x))
            crossed.append(swap(sent[at], "var"))
        done = len(jobs)
        jobs += [job_at(shift, ours) for shift in order[done - 1 :]]
        rows_x = call(
            jobs[done:-1] + [with_fields(job, others) for job in jobs[:-1]], rows_x, groups=2
        )
        sent = call(
            [with_fields(jobs[-1], ours + others)],
            rows_x,
            groups=2,
            last=(embed_weight, embed_other, nv),
        )
        got = lax.all_to_all(sent, ("grp", "band", "var"), split_axis=0, concat_axis=0, tiled=True)
    else:
        embed_other = swap(embed_weight, "sub")
        both = jnp.concatenate([ocean_w, atmos_w], axis=1)
        fields = [(0, (jnp.concatenate([ocean_f, atmos_f], axis=0),))]
        ocean_block, ocean_used = slot_tables(ocean_dest, nb, cap)
        atmos_block, atmos_used = slot_tables(atmos_dest, nb, cap)
        block_all = jnp.concatenate([ocean_block, atmos_block + block_count], axis=1)
        used_all = jnp.concatenate([ocean_used, atmos_used], axis=1)
        grid_row = jnp.where(jnp.arange(slots) < cap, 0, tiles)

        def job_of(band, tile, meta, parts):
            block = lax.dynamic_index_in_dim(block_all, band, 0, keepdims=False)
            used = lax.dynamic_index_in_dim(used_all, band, 0, keepdims=False)
            scale = jnp.where(used, tile + grid_row, 2 * tiles)
            table = jnp.stack([block, tile, scale]).astype(jnp.int32)
            where = jnp.stack([band, jnp.int32(0)])
            return table, where, meta, 0, [parts], [slots], fields

        tile_ids = jnp.concatenate([ocean_ids, atmos_ids], axis=1)
        own_tile = lax.dynamic_index_in_dim(tile_ids, me, 0, keepdims=False)
        own_w = lax.dynamic_index_in_dim(both, me, 0, keepdims=False)
        rows_x = call([job_of(me, own_tile, land, own_w)], None, groups=1)
        share_rows = slots * cells // rep
        high = lax.reduce_precision(land, 8, 7)
        low = (land - high).astype(jnp.bfloat16)
        tile_rows = jnp.pad(tile_ids.astype(jnp.bfloat16), ((0, 0), (0, cells - slots)))
        for shift in order:
            target, band = (me + shift) % nb, (me - shift) % nb
            piece = lax.dynamic_slice(
                both, (target, quarter * share_rows, 0), (1, share_rows, cells)
            )[0]
            row = lax.dynamic_slice(tile_rows, (target, 0), (1, cells))
            row = jnp.broadcast_to(row, (16, cells))
            piece = jnp.concatenate([piece, high.astype(jnp.bfloat16), low, row], axis=0)
            parts = lax.all_gather(lax.ppermute(piece, "band", along(shift)), REPL, axis=0)
            meta = parts[0, share_rows:]
            tile = meta[2 * tiles, :slots].astype(jnp.int32)
            parts = parts[:, :share_rows].reshape(slots * cells, cells)
            rows_x = call([job_of(band, tile, meta, parts)], rows_x, groups=1)
        sent = embed(rows_x, embed_weight, embed_other, steps, nv)
        got = lax.all_to_all(sent, ("band", "var"), split_axis=0, concat_axis=0, tiled=True)
    shifted = jnp.sum(got.astype(jnp.float32), axis=0) + embed_bias
    inverse = lax.rsqrt(jnp.mean(shifted * shifted, axis=-1, keepdims=True) + 1e-05)
    finished = (shifted * inverse * embed_gain).astype(jnp.bfloat16)
    width = finished.shape[-1]
    finished = finished.reshape(nb, share, steps // nb, width).transpose(1, 0, 2, 3)
    return finished[None]


def solution(mesh):
    in_specs = (
        P(("grp", "band", "sub"), None, "var", None),
        P(("band", "sub"), None),
        P("band", "sub", None, None, None, None),
        P("band", "sub", None, None),
        P(("grp", "band", "sub"), None, "var", None),
        P(("band", "sub"), None),
        P("band", "sub", None, None, None, None),
        P("band", "sub", None, None),
        P("band", "sub", None, None, None),
        P(("var", "sub"), None),
        P(),
        P(),
    )
    out_specs = P("sub", "var", None, ("grp", "band"), None)
    return jax.shard_map(
        per_device, mesh=mesh, in_specs=in_specs, out_specs=out_specs, check_vma=False
    )
```

```python
import functools

import jax
import jax.numpy as jnp
from jax import lax
from jax.experimental import pallas as pl
from jax.experimental.pallas import tpu as pltpu
from jax.sharding import PartitionSpec as P

REPL = ("grp", "var")


def slot_tables(dest, band_count, cap):
    count = dest.shape[0]
    serial = jnp.arange(count, dtype=jnp.int32)
    band_of = dest[:, 0]
    earlier = (band_of[:, None] == band_of[None, :]) & (serial[None, :] < serial[:, None])
    position = jnp.sum(earlier.astype(jnp.int32), axis=1)
    slot = band_of * cap + position
    hit = slot[None, :] == jnp.arange(band_count * cap, dtype=jnp.int32)[:, None]
    block = jnp.sum(jnp.where(hit, serial[None, :], 0), axis=1)
    used = jnp.any(hit, axis=1)
    return block.reshape(band_count, cap), used.reshape(band_count, cap)


def pack_kernel(pieces, moved, *refs):
    ocean_w, atmos_w, ocean_ids, atmos_ids, land = refs[:5]
    fields, refs = refs[5 : 5 + 2 * moved], refs[5 + 2 * moved :]
    count = len(pieces) + moved
    stages, sem = refs[:count], refs[-1]
    me, bands = lax.axis_index("band"), ocean_w.shape[0]
    x, y = lax.axis_index("var"), lax.axis_index("grp")
    cells, tiles = land.shape[-1], land.shape[0]
    cap = ocean_ids.shape[-1]

    def loads(weights, other):
        found = []
        for at, (stage, (shift, first, size, split)) in enumerate(zip(stages, pieces)):
            start = first if split is None else x * split + first
            found.append(
                pltpu.make_async_copy(
                    weights.at[
                        lax.rem(me + shift, bands),
                        pl.ds(pl.multiple_of(start * cells, cells), size * cells),
                        :,
                    ],
                    stage.at[pl.ds(0, size * cells), :],
                    sem.at[at],
                )
            )
        if moved:
            found.append(pltpu.make_async_copy(fields[other], stages[-1], sem.at[count - 1]))
        return found

    @pl.when(y == 0)
    def _():
        for copy in loads(ocean_w, 1):
            copy.start()

    @pl.when(y == 1)
    def _():
        for copy in loads(atmos_w, 0):
            copy.start()

    fraction = land[...]
    high = fraction.astype(jnp.bfloat16)
    low = (fraction - high.astype(jnp.float32)).astype(jnp.bfloat16)
    for stage, (shift, first, size, split) in zip(stages, pieces):
        if first:
            continue
        target, base = lax.rem(me + shift, bands), size * cells
        stage[pl.ds(base, tiles), :] = high
        stage[pl.ds(base + tiles, tiles), :] = low
        row = jnp.where(y == 0, ocean_ids[pl.ds(target, 1), :], atmos_ids[pl.ds(target, 1), :])
        row = jnp.broadcast_to(row.astype(jnp.float32), (16, cap)).astype(jnp.bfloat16)
        stage[pl.ds(base + 2 * tiles, 16), :] = jnp.zeros((16, cells), jnp.bfloat16)
        stage[pl.ds(base + 2 * tiles, 16), pl.ds(0, cap)] = row
    for load in loads(ocean_w, 1):
        load.wait()


def pack(limit, pieces, ocean_w, atmos_w, ocean_ids, atmos_ids, land, *fields):
    cells, tiles = land.shape[-1], land.shape[0]
    any_spec = pl.BlockSpec(memory_space=pl.ANY)
    vmem = pl.BlockSpec(memory_space=pltpu.VMEM)
    sizes = [size * cells + (0 if first else 2 * tiles + 16) for _, first, size, _ in pieces]
    shapes = [(n, cells) for n in sizes] + [f.shape for f in fields[:1]]
    return pl.pallas_call(
        functools.partial(pack_kernel, pieces, len(fields) // 2),
        out_shape=[jax.ShapeDtypeStruct(shape, jnp.bfloat16) for shape in shapes],
        in_specs=[any_spec] * 2 + [vmem] * 3 + [any_spec] * len(fields),
        out_specs=[vmem] * len(shapes),
        scratch_shapes=[pltpu.SemaphoreType.DMA((len(shapes),))],
        cost_estimate=pl.CostEstimate(flops=0, bytes_accessed=2 << 20, transcendentals=0),
        compiler_params=pltpu.CompilerParams(vmem_limit_bytes=limit << 20),
    )(ocean_w, atmos_w, ocean_ids, atmos_ids, land, *fields)


def run_jobs(steps, jobs, refs, out, acc, scale):
    local_rows, cells = acc.shape[1] // (scale.shape[0] // 2 - 4), acc.shape[2]
    tiles = acc.shape[1] // local_rows
    local_vars = local_rows // steps
    half_vars = local_vars // 2
    for table, where, meta, meta_at, parts, groups in jobs:
        table, where, meta = refs[table], refs[where], refs[meta]
        if meta.dtype == jnp.float32:
            land = meta[...]
        else:
            high = meta[pl.ds(meta_at, tiles), :].astype(jnp.float32)
            land = high + meta[pl.ds(meta_at + tiles, tiles), :].astype(jnp.float32)
        scale[pl.ds(0, tiles), :] = 1.0 - land
        scale[pl.ds(tiles, tiles), :] = land
        scale[pl.ds(2 * tiles, 8), :] = jnp.zeros((8, cells), jnp.float32)
        acc[pl.ds(0, len(groups))] = jnp.zeros((len(groups),) + acc.shape[1:], jnp.float32)
        for at, (part, size) in enumerate(parts):
            first = where[1 + at]
            for s in range(size):
                slot = first + s
                block = table[0, slot]
                moved = []
                for _, fields in groups:
                    piece = refs[fields[0]][block]
                    if len(fields) > 1:
                        piece = jnp.where(
                            lax.axis_index("grp") == 0, piece, refs[fields[1]][block]
                        )
                    moved.append(piece)
                moved = moved[0] if len(moved) == 1 else jnp.concatenate(moved, axis=0)
                dense = jnp.dot(
                    moved,
                    refs[part][pl.ds(s * cells, cells), :],
                    preferred_element_type=jnp.float32,
                )
                dense = dense * scale[pl.ds(table[2, slot], 1), :]
                span = pl.ds(pl.multiple_of(table[1, slot] * local_rows, local_rows), local_rows)
                for g in range(len(groups)):
                    acc[g, span, :] += dense[g * local_rows : (g + 1) * local_rows]
        for g, (to, _) in enumerate(groups):
            for v in range(local_vars):
                for q in range(2):
                    column = (v % half_vars * 2 + q) * cells
                    rows = [
                        acc[g, pl.ds(q * local_rows + t * local_vars + v, tiles // 2, 2 * local_rows), :]
                        for t in range(steps)
                    ]
                    out[where[0], to, v // half_vars, :, pl.ds(column, cells)] = jnp.concatenate(
                        rows, axis=0
                    ).astype(out.dtype)


def regrid_kernel(steps, jobs, *refs):
    run_jobs(steps, jobs, refs, *refs[-3:])


def finish_kernel(steps, halves, jobs, count, *refs):
    theirs, mine, rows_x, out, acc, scale, weight, total, sem = refs[count:]
    sub, mine_group = lax.axis_index("sub"), lax.axis_index("grp")
    chunks = sem.shape[0]
    height = mine.shape[0] // chunks

    def copy(chunk):
        span = pl.ds(pl.multiple_of(chunk * height, height), height)
        return pltpu.make_async_copy(mine.at[span, :], weight.at[span, :], sem.at[chunk])

    for chunk in range(chunks):
        copy(chunk).start()
    run_jobs(steps, jobs, refs, rows_x, acc, scale)
    total[...] = jnp.zeros_like(total)

    @pl.loop(0, chunks)
    def _(chunk):
        span = pl.ds(pl.multiple_of(chunk * height, height), height)
        left, right = (
            rows_x[:, :, place, :, span].reshape(total.shape[0], height) for place in (sub, 1 - sub)
        )
        copy(chunk).wait()
        total[...] += jnp.dot(
            left, weight[span, :], preferred_element_type=jnp.float32
        ) + jnp.dot(right, theirs[span, :], preferred_element_type=jnp.float32)

    send_rows(steps, halves, rows_x.shape, mine_group, total, out)


def send_rows(steps, halves, shape, mine_group, total, out):
    bands, groups, _, row_count, _ = shape
    count = steps * halves
    share = row_count // count
    for g in range(groups):
        base = (mine_group if g == 0 else 1 - mine_group) * count if groups > 1 else 0
        for chunk in range(count):
            pieces = [
                total[pl.ds((b * groups + g) * row_count + chunk * share, share), :]
                for b in range(bands)
            ]
            out[base + chunk] = jnp.concatenate(pieces, axis=0).astype(out.dtype)


def regrid(jobs, previous, bands, groups, steps, tiles, rows, cells, last=None):
    operands, specs, places = [], [], {}

    def place(array, space):
        if id(array) not in places:
            places[id(array)] = len(operands)
            operands.append(array)
            specs.append(pl.BlockSpec(memory_space=space))
        return places[id(array)]

    listed, flops, most = [], 0, 1
    for table, where, meta, meta_at, parts, sizes, fields in jobs:
        listed.append(
            (
                place(table, pltpu.SMEM),
                place(where, pltpu.SMEM),
                place(meta, pltpu.VMEM),
                meta_at,
                [(place(part, pltpu.VMEM), size) for part, size in zip(parts, sizes)],
                [(to, [place(f, pltpu.VMEM) for f in pair]) for to, pair in fields],
            )
        )
        flops += 2 * sum(sizes) * len(fields) * rows * cells * cells
        most = max(most, len(fields))
    aliases = {}
    vmem = pl.BlockSpec(memory_space=pltpu.VMEM)
    if previous is not None:
        aliases = {len(operands): 0}
        operands.append(previous)
        specs.append(vmem)
    shape = (bands, groups, 2, steps * tiles // 2, rows // steps // 2 * 2 * cells)
    shapes = [jax.ShapeDtypeStruct(shape, jnp.bfloat16)]
    scratch = [
        pltpu.VMEM((most, tiles * rows, cells), jnp.float32),
        pltpu.VMEM((2 * tiles + 8, cells), jnp.float32),
    ]
    if last is None:
        body = functools.partial(regrid_kernel, steps, listed)
        limit, moved = 12 << 20, len(jobs) * 3 << 20
    else:
        mine, theirs, halves = last
        height, width = mine.shape
        total = bands * groups * shape[3]
        body = functools.partial(finish_kernel, steps, halves, listed, len(operands))
        operands += [theirs, mine]
        specs += [vmem, pl.BlockSpec(memory_space=pl.ANY)]
        count = groups * steps * halves
        shapes.append(jax.ShapeDtypeStruct((count, total // count, width), jnp.bfloat16))
        scratch += [
            pltpu.VMEM((height, width), jnp.bfloat16),
            pltpu.VMEM((total, width), jnp.float32),
            pltpu.SemaphoreType.DMA((6,)),
        ]
        limit, moved = 36 << 20, 4 * height * width
        flops += 4 * total * height * width
    done = pl.pallas_call(
        body,
        out_shape=shapes,
        in_specs=specs,
        out_specs=[vmem] * len(shapes),
        scratch_shapes=scratch,
        input_output_aliases=aliases,
        cost_estimate=pl.CostEstimate(flops=flops, bytes_accessed=moved, transcendentals=0),
        compiler_params=pltpu.CompilerParams(vmem_limit_bytes=limit),
    )(*operands)
    return done[-1]


def embed_kernel(steps, halves, rows_x, mine, theirs, out, total):
    at = pl.program_id(0)
    sub, mine_group = lax.axis_index("sub"), lax.axis_index("grp")
    bands, groups, _, row_count, width = rows_x.shape
    rows = bands * groups * row_count

    @pl.when(at == 0)
    def _():
        total[...] = jnp.zeros_like(total)

    left = rows_x[:, :, sub].reshape(rows, width)
    right = rows_x[:, :, 1 - sub].reshape(rows, width)
    total[...] += jnp.dot(left, mine[...], preferred_element_type=jnp.float32) + jnp.dot(
        right, theirs[...], preferred_element_type=jnp.float32
    )

    @pl.when(at == pl.num_programs(0) - 1)
    def _():
        if out.ndim == 2:
            out[...] = total[...].astype(out.dtype)
        else:
            send_rows(steps, halves, rows_x.shape, mine_group, total, out)


def embed(rows_x, mine, theirs, steps, halves):
    bands, groups, _, row_count, half_width = rows_x.shape
    width = mine.shape[-1]
    grid = 6 if half_width % (6 * 256) == 0 else 3
    step_rows = half_width // grid
    rows = bands * groups * row_count
    chunks = groups * steps * halves
    share = row_count // (steps * halves)
    shape = (chunks, bands * share, width) if share % 4 == 0 else (rows, width)
    weight_spec = pl.BlockSpec((step_rows, width), lambda i: (i, 0))
    out = pl.pallas_call(
        functools.partial(embed_kernel, steps, halves),
        out_shape=jax.ShapeDtypeStruct(shape, jnp.bfloat16),
        grid=(grid,),
        in_specs=[
            pl.BlockSpec((bands, groups, 2, row_count, step_rows), lambda i: (0, 0, 0, 0, i)),
            weight_spec,
            weight_spec,
        ],
        out_specs=pl.BlockSpec(shape, lambda i: (0,) * len(shape)),
        scratch_shapes=[pltpu.VMEM((rows, width), jnp.float32)],
        cost_estimate=pl.CostEstimate(
            flops=4 * rows * mine.shape[0] * width,
            bytes_accessed=4 * mine.shape[0] * width,
            transcendentals=0,
        ),
        compiler_params=pltpu.CompilerParams(
            vmem_limit_bytes=(48 if rows > 1024 else 16) << 20
        ),
    )(rows_x, mine, theirs)
    if share % 4:
        out = out.reshape(bands, chunks, share, width).transpose(1, 0, 2, 3)
        out = out.reshape(chunks, bands * share, width)
    return out


def swap(x, axis):
    return lax.ppermute(x, axis, [(0, 1), (1, 0)])


def per_device(
    ocean_fields,
    ocean_dest,
    ocean_weights,
    ocean_tiles,
    atmos_fields,
    atmos_dest,
    atmos_weights,
    atmos_tiles,
    land_fraction,
    embed_weight,
    embed_bias,
    embed_gain,
):
    nb = lax.axis_size("band")
    nv = lax.axis_size("var")
    ng = lax.axis_size("grp")
    rep = nv * ng
    cap = ocean_weights.shape[3]
    cells = ocean_weights.shape[-1]
    block_count, steps, local_vars, _ = ocean_fields.shape
    patches = land_fraction.shape[2]
    tiles = 2 * patches
    slots = 2 * cap
    share = patches // nv
    me = lax.axis_index("band")
    x, y = lax.axis_index("var"), lax.axis_index("grp")
    quarter = y * nv + x

    flat = (nb, cap * cells, cells)
    ocean_w, atmos_w = ocean_weights.reshape(flat), atmos_weights.reshape(flat)
    ocean_ids, atmos_ids = ocean_tiles.reshape(nb, cap), atmos_tiles.reshape(nb, cap)
    land = land_fraction.reshape(tiles, cells)
    blocks = (block_count, steps * local_vars, cells)
    ocean_f, atmos_f = ocean_fields.reshape(blocks), atmos_fields.reshape(blocks)
    order = ([1, nb - 1] + list(range(2, nb - 1)))[: nb - 1]
    along = lambda shift: [(b, (b + shift) % nb) for b in range(nb)]
    call = functools.partial(
        regrid, bands=nb, steps=steps, tiles=tiles, rows=steps * local_vars, cells=cells
    )

    if ng == 2 and nv == 2 and cap % 2 == 0:
        each = cap // 2
        pieces = []
        for shift in order:
            pieces.append((shift, 0, each, each))
        *packed, send = pack(
            60, pieces, ocean_w, atmos_w, ocean_ids, atmos_ids, land, ocean_f, atmos_f
        )
        sent = [
            lax.ppermute(piece, "band", along(shift))
            for piece, (shift, _, _, _) in zip(packed[:2], pieces)
        ]
        embed_other, own_land, send = lax.optimization_barrier((embed_weight, land, send))
        own_w = pack(54, [(0, 0, cap, None)], ocean_w, atmos_w, ocean_ids, atmos_ids, own_land)[0]
        embed_other = swap(embed_other, "sub")
        keep, theirs = (ocean_f, atmos_f), (swap(send, "grp"),)
        dest = jnp.where(y == 0, ocean_dest, atmos_dest)
        block_all, used_all = slot_tables(dest, nb, cap)
        def job_of(band, parts, sizes, firsts, fields):
            meta_at = sizes[0] * cells
            tile = parts[0][meta_at + 2 * tiles, :cap].astype(jnp.int32)
            block = lax.dynamic_index_in_dim(block_all, band, 0, keepdims=False)
            used = lax.dynamic_index_in_dim(used_all, band, 0, keepdims=False)
            scale = jnp.where(used, tile + y * tiles, 2 * tiles)
            table = jnp.stack([block, tile, scale]).astype(jnp.int32)
            where = jnp.stack([band] + firsts).astype(jnp.int32)
            return table, where, parts[0], meta_at, parts, sizes, fields

        def with_fields(job, fields):
            return job[:-1] + (fields,)

        def job_at(shift, fields):
            parts, sizes, firsts = [], [], []
            for piece, across, (of, first, size, _) in zip(sent, crossed, pieces):
                if of == shift:
                    parts += [piece, across]
                    sizes += [size, size]
                    firsts += [x * each + first, (1 - x) * each + first]
            return job_of((me - shift) % nb, parts, sizes, firsts, fields)

        ours, others = [(0, keep)], [(1, theirs)]
        jobs = [job_of(me, [own_w], [cap], [jnp.int32(0)], ours)]
        rows_x = call(jobs, None, groups=2)
        for at, (piece, (shift, _, _, _)) in enumerate(zip(packed[2:], pieces[2:])):
            piece, sent[at], rows_x = lax.optimization_barrier((piece, sent[at], rows_x))
            sent.append(lax.ppermute(piece, "band", along(shift)))
        crossed = [swap(piece, "var") for piece in sent]
        jobs += [job_at(shift, ours) for shift in order]
        rows_x = call(
            jobs[1:-1] + [with_fields(job, others) for job in jobs[:-1]], rows_x, groups=2
        )
        sent = call(
            [with_fields(jobs[-1], ours + others)],
            rows_x,
            groups=2,
            last=(embed_weight, embed_other, nv),
        )
        got = lax.all_to_all(sent, ("grp", "band", "var"), split_axis=0, concat_axis=0, tiled=True)
    else:
        embed_other = swap(embed_weight, "sub")
        both = jnp.concatenate([ocean_w, atmos_w], axis=1)
        fields = [(0, (jnp.concatenate([ocean_f, atmos_f], axis=0),))]
        ocean_block, ocean_used = slot_tables(ocean_dest, nb, cap)
        atmos_block, atmos_used = slot_tables(atmos_dest, nb, cap)
        block_all = jnp.concatenate([ocean_block, atmos_block + block_count], axis=1)
        used_all = jnp.concatenate([ocean_used, atmos_used], axis=1)
        grid_row = jnp.where(jnp.arange(slots) < cap, 0, tiles)

        def job_of(band, tile, meta, parts):
            block = lax.dynamic_index_in_dim(block_all, band, 0, keepdims=False)
            used = lax.dynamic_index_in_dim(used_all, band, 0, keepdims=False)
            scale = jnp.where(used, tile + grid_row, 2 * tiles)
            table = jnp.stack([block, tile, scale]).astype(jnp.int32)
            where = jnp.stack([band, jnp.int32(0)])
            return table, where, meta, 0, [parts], [slots], fields

        tile_ids = jnp.concatenate([ocean_ids, atmos_ids], axis=1)
        own_tile = lax.dynamic_index_in_dim(tile_ids, me, 0, keepdims=False)
        own_w = lax.dynamic_index_in_dim(both, me, 0, keepdims=False)
        rows_x = call([job_of(me, own_tile, land, own_w)], None, groups=1)
        share_rows = slots * cells // rep
        high = lax.reduce_precision(land, 8, 7)
        low = (land - high).astype(jnp.bfloat16)
        tile_rows = jnp.pad(tile_ids.astype(jnp.bfloat16), ((0, 0), (0, cells - slots)))
        for shift in order:
            target, band = (me + shift) % nb, (me - shift) % nb
            piece = lax.dynamic_slice(
                both, (target, quarter * share_rows, 0), (1, share_rows, cells)
            )[0]
            row = lax.dynamic_slice(tile_rows, (target, 0), (1, cells))
            row = jnp.broadcast_to(row, (16, cells))
            piece = jnp.concatenate([piece, high.astype(jnp.bfloat16), low, row], axis=0)
            parts = lax.all_gather(lax.ppermute(piece, "band", along(shift)), REPL, axis=0)
            meta = parts[0, share_rows:]
            tile = meta[2 * tiles, :slots].astype(jnp.int32)
            parts = parts[:, :share_rows].reshape(slots * cells, cells)
            rows_x = call([job_of(band, tile, meta, parts)], rows_x, groups=1)
        sent = embed(rows_x, embed_weight, embed_other, steps, nv)
        got = lax.all_to_all(sent, ("band", "var"), split_axis=0, concat_axis=0, tiled=True)
    shifted = jnp.sum(got.astype(jnp.float32), axis=0) + embed_bias
    inverse = lax.rsqrt(jnp.mean(shifted * shifted, axis=-1, keepdims=True) + 1e-05)
    finished = (shifted * inverse * embed_gain).astype(jnp.bfloat16)
    width = finished.shape[-1]
    finished = finished.reshape(nb, share, steps // nb, width).transpose(1, 0, 2, 3)
    return finished[None]


def solution(mesh):
    in_specs = (
        P(("grp", "band", "sub"), None, "var", None),
        P(("band", "sub"), None),
        P("band", "sub", None, None, None, None),
        P("band", "sub", None, None),
        P(("grp", "band", "sub"), None, "var", None),
        P(("band", "sub"), None),
        P("band", "sub", None, None, None, None),
        P("band", "sub", None, None),
        P("band", "sub", None, None, None),
        P(("var", "sub"), None),
        P(),
        P(),
    )
    out_specs = P("sub", "var", None, ("grp", "band"), None)
    return jax.shard_map(
        per_device, mesh=mesh, in_specs=in_specs, out_specs=out_specs, check_vma=False
    )
```

```python
import functools

import jax
import jax.numpy as jnp
from jax import lax
from jax.experimental import pallas as pl
from jax.experimental.pallas import tpu as pltpu
from jax.sharding import PartitionSpec as P

REPL = ("grp", "var")


def slot_tables(dest, band_count, cap):
    count = dest.shape[0]
    serial = jnp.arange(count, dtype=jnp.int32)
    band_of = dest[:, 0]
    earlier = (band_of[:, None] == band_of[None, :]) & (serial[None, :] < serial[:, None])
    position = jnp.sum(earlier.astype(jnp.int32), axis=1)
    slot = band_of * cap + position
    hit = slot[None, :] == jnp.arange(band_count * cap, dtype=jnp.int32)[:, None]
    block = jnp.sum(jnp.where(hit, serial[None, :], 0), axis=1)
    used = jnp.any(hit, axis=1)
    return block.reshape(band_count, cap), used.reshape(band_count, cap)


def pack_kernel(pieces, moved, *refs):
    ocean_w, atmos_w, ocean_ids, atmos_ids, land = refs[:5]
    fields, refs = refs[5 : 5 + 2 * moved], refs[5 + 2 * moved :]
    count = len(pieces) + moved
    stages, sem = refs[:count], refs[-1]
    me, bands = lax.axis_index("band"), ocean_w.shape[0]
    x, y = lax.axis_index("var"), lax.axis_index("grp")
    cells, tiles = land.shape[-1], land.shape[0]
    cap = ocean_ids.shape[-1]

    def loads(weights, other):
        found = []
        for at, (stage, (shift, first, size, split)) in enumerate(zip(stages, pieces)):
            start = first if split is None else x * split + first
            found.append(
                pltpu.make_async_copy(
                    weights.at[
                        lax.rem(me + shift, bands),
                        pl.ds(pl.multiple_of(start * cells, cells), size * cells),
                        :,
                    ],
                    stage.at[pl.ds(0, size * cells), :],
                    sem.at[at],
                )
            )
        if moved:
            found.append(pltpu.make_async_copy(fields[other], stages[-1], sem.at[count - 1]))
        return found

    @pl.when(y == 0)
    def _():
        for copy in loads(ocean_w, 1):
            copy.start()

    @pl.when(y == 1)
    def _():
        for copy in loads(atmos_w, 0):
            copy.start()

    fraction = land[...]
    high = fraction.astype(jnp.bfloat16)
    low = (fraction - high.astype(jnp.float32)).astype(jnp.bfloat16)
    for stage, (shift, first, size, split) in zip(stages, pieces):
        if first:
            continue
        target, base = lax.rem(me + shift, bands), size * cells
        stage[pl.ds(base, tiles), :] = high
        stage[pl.ds(base + tiles, tiles), :] = low
        row = jnp.where(y == 0, ocean_ids[pl.ds(target, 1), :], atmos_ids[pl.ds(target, 1), :])
        row = jnp.broadcast_to(row.astype(jnp.float32), (16, cap)).astype(jnp.bfloat16)
        stage[pl.ds(base + 2 * tiles, 16), :] = jnp.zeros((16, cells), jnp.bfloat16)
        stage[pl.ds(base + 2 * tiles, 16), pl.ds(0, cap)] = row
    for load in loads(ocean_w, 1):
        load.wait()


def pack(limit, pieces, ocean_w, atmos_w, ocean_ids, atmos_ids, land, *fields):
    cells, tiles = land.shape[-1], land.shape[0]
    any_spec = pl.BlockSpec(memory_space=pl.ANY)
    vmem = pl.BlockSpec(memory_space=pltpu.VMEM)
    sizes = [size * cells + (0 if first else 2 * tiles + 16) for _, first, size, _ in pieces]
    shapes = [(n, cells) for n in sizes] + [f.shape for f in fields[:1]]
    return pl.pallas_call(
        functools.partial(pack_kernel, pieces, len(fields) // 2),
        out_shape=[jax.ShapeDtypeStruct(shape, jnp.bfloat16) for shape in shapes],
        in_specs=[any_spec] * 2 + [vmem] * 3 + [any_spec] * len(fields),
        out_specs=[vmem] * len(shapes),
        scratch_shapes=[pltpu.SemaphoreType.DMA((len(shapes),))],
        cost_estimate=pl.CostEstimate(flops=0, bytes_accessed=2 << 20, transcendentals=0),
        compiler_params=pltpu.CompilerParams(vmem_limit_bytes=limit << 20),
    )(ocean_w, atmos_w, ocean_ids, atmos_ids, land, *fields)


def run_jobs(steps, jobs, refs, out, acc, scale):
    local_rows, cells = acc.shape[1] // (scale.shape[0] // 2 - 4), acc.shape[2]
    tiles = acc.shape[1] // local_rows
    local_vars = local_rows // steps
    half_vars = local_vars // 2
    for table, where, meta, meta_at, parts, groups in jobs:
        table, where, meta = refs[table], refs[where], refs[meta]
        if meta.dtype == jnp.float32:
            land = meta[...]
        else:
            high = meta[pl.ds(meta_at, tiles), :].astype(jnp.float32)
            land = high + meta[pl.ds(meta_at + tiles, tiles), :].astype(jnp.float32)
        scale[pl.ds(0, tiles), :] = 1.0 - land
        scale[pl.ds(tiles, tiles), :] = land
        scale[pl.ds(2 * tiles, 8), :] = jnp.zeros((8, cells), jnp.float32)
        acc[pl.ds(0, len(groups))] = jnp.zeros((len(groups),) + acc.shape[1:], jnp.float32)
        for at, (part, size) in enumerate(parts):
            first = where[1 + at]
            for s in range(size):
                slot = first + s
                block = table[0, slot]
                moved = []
                for _, fields in groups:
                    piece = refs[fields[0]][block]
                    if len(fields) > 1:
                        piece = jnp.where(
                            lax.axis_index("grp") == 0, piece, refs[fields[1]][block]
                        )
                    moved.append(piece)
                moved = moved[0] if len(moved) == 1 else jnp.concatenate(moved, axis=0)
                dense = jnp.dot(
                    moved,
                    refs[part][pl.ds(s * cells, cells), :],
                    preferred_element_type=jnp.float32,
                )
                dense = dense * scale[pl.ds(table[2, slot], 1), :]
                span = pl.ds(pl.multiple_of(table[1, slot] * local_rows, local_rows), local_rows)
                for g in range(len(groups)):
                    acc[g, span, :] += dense[g * local_rows : (g + 1) * local_rows]
        for g, (to, _) in enumerate(groups):
            for v in range(local_vars):
                for q in range(2):
                    column = (v % half_vars * 2 + q) * cells
                    rows = [
                        acc[g, pl.ds(q * local_rows + t * local_vars + v, tiles // 2, 2 * local_rows), :]
                        for t in range(steps)
                    ]
                    out[where[0], to, v // half_vars, :, pl.ds(column, cells)] = jnp.concatenate(
                        rows, axis=0
                    ).astype(out.dtype)


def regrid_kernel(steps, jobs, *refs):
    run_jobs(steps, jobs, refs, *refs[-3:])


def finish_kernel(steps, halves, jobs, count, *refs):
    sources, refs, outs = refs[count : count + 2], refs[:count], refs[count + 2 :]
    rows_x, keep_x, send_x, keep_y, send_y, acc, scale, weight, total, sem = outs
    sub = lax.axis_index("sub")
    chunks = sem.shape[1]
    height = weight.shape[1] // chunks

    def copy(half, chunk):
        span = pl.ds(pl.multiple_of(chunk * height, height), height)
        return pltpu.make_async_copy(
            sources[half].at[span, :], weight.at[half, span, :], sem.at[half, chunk]
        )

    for chunk in range(chunks):
        for half in range(2):
            copy(half, chunk).start()
    run_jobs(steps, jobs, refs, rows_x, acc, scale)
    total[...] = jnp.zeros_like(total)

    @pl.loop(0, chunks)
    def _(chunk):
        span = pl.ds(pl.multiple_of(chunk * height, height), height)
        terms = []
        for half, place in enumerate((sub, 1 - sub)):
            left = rows_x[:, :, place, :, span].reshape(total.shape[0], height)
            copy(half, chunk).wait()
            terms.append(
                jnp.dot(left, weight[half, span, :], preferred_element_type=jnp.float32)
            )
        total[...] += terms[0] + terms[1]

    x = lax.axis_index("var")
    bands, groups, _, row_count, _ = rows_x.shape
    share = row_count // (steps * halves)
    width = total.shape[1] // 2
    size = bands * share
    for g in range(groups):
        for t in range(steps):
            for h in range(halves):
                starts = [
                    (b * groups + g) * row_count + (t * halves + h) * share for b in range(bands)
                ]
                first, second = (
                    jnp.concatenate(
                        [total[pl.ds(at, share), pl.ds(c * width, width)] for at in starts], axis=0
                    )
                    for c in range(2)
                )
                place = pl.ds((g * steps + t) * size, size)

                @pl.when(x == h)
                def _(place=place, first=first):
                    keep_x[place, :] = first

                @pl.when(x != h)
                def _(place=place, first=first):
                    send_x[place, :] = first.astype(send_x.dtype)

                place = pl.multiple_of((lax.rem(x + h, 2) * steps + t) * size, size)
                if g == 0:
                    keep_y[pl.ds(place, size), :] = second
                else:
                    send_y[pl.ds(place, size), :] = second.astype(send_y.dtype)


def add_kernel(keep_x, got_x, keep_y, got_y, sum_x, send_x, sum_y, send_y):
    half = sum_x.shape[0]
    for keep, got, out, send in (
        (keep_x, got_x, sum_x, send_x),
        (keep_y, got_y, sum_y, send_y),
    ):
        out[...] = keep[:half, :] + got[:half, :].astype(jnp.float32)
        send[...] = (keep[half:, :] + got[half:, :].astype(jnp.float32)).astype(send.dtype)


def split_kernel(shifts, keep_x, got_x, keep_y, got_y, *outs):
    size, width = outs[0].shape[0], keep_x.shape[1]
    me, bands = lax.axis_index("band"), keep_x.shape[0] // size
    for out, shift in zip(outs, (0,) + tuple(shifts)):
        span = pl.ds(pl.multiple_of(lax.rem(me + shift, bands) * size, size), size)
        for c, (keep, got) in enumerate(((keep_x, got_x), (keep_y, got_y))):
            some = keep[span, :] + got[span, :].astype(jnp.float32)
            out[:, pl.ds(c * width, width)] = some.astype(out.dtype)


def norm_kernel(bands, own, *refs):
    parts, bias, gain, out = refs[:-3], refs[-3], refs[-2], refs[-1]
    summed = own[...] + bias[...]
    for part in parts:
        summed += part[...].astype(jnp.float32)
    inverse = lax.rsqrt(jnp.mean(summed * summed, axis=-1, keepdims=True) + 1e-05)
    done = summed * inverse * gain[...]
    share = done.shape[0] // bands
    rows = [done[b * share + p : b * share + p + 1] for p in range(share) for b in range(bands)]
    out[...] = jnp.concatenate(rows, axis=0).astype(out.dtype)


def small(body, shapes, *operands):
    vmem = pl.BlockSpec(memory_space=pltpu.VMEM)
    return pl.pallas_call(
        body,
        out_shape=[jax.ShapeDtypeStruct(shape, kind) for shape, kind in shapes],
        in_specs=[vmem] * len(operands),
        out_specs=[vmem] * len(shapes),
        cost_estimate=pl.CostEstimate(flops=1 << 18, bytes_accessed=1 << 20, transcendentals=0),
        compiler_params=pltpu.CompilerParams(vmem_limit_bytes=12 << 20),
    )(*operands)


def send_rows(steps, halves, shape, mine_group, total, out):
    bands, groups, _, row_count, _ = shape
    count = steps * halves
    share = row_count // count
    for g in range(groups):
        base = (mine_group if g == 0 else 1 - mine_group) * count if groups > 1 else 0
        for chunk in range(count):
            pieces = [
                total[pl.ds((b * groups + g) * row_count + chunk * share, share), :]
                for b in range(bands)
            ]
            out[base + chunk] = jnp.concatenate(pieces, axis=0).astype(out.dtype)


def regrid(jobs, previous, bands, groups, steps, tiles, rows, cells, last=None):
    operands, specs, places = [], [], {}

    def place(array, space):
        if id(array) not in places:
            places[id(array)] = len(operands)
            operands.append(array)
            specs.append(pl.BlockSpec(memory_space=space))
        return places[id(array)]

    listed, flops, most = [], 0, 1
    for table, where, meta, meta_at, parts, sizes, fields in jobs:
        listed.append(
            (
                place(table, pltpu.SMEM),
                place(where, pltpu.SMEM),
                place(meta, pltpu.VMEM),
                meta_at,
                [(place(part, pltpu.VMEM), size) for part, size in zip(parts, sizes)],
                [(to, [place(f, pltpu.VMEM) for f in pair]) for to, pair in fields],
            )
        )
        flops += 2 * sum(sizes) * len(fields) * rows * cells * cells
        most = max(most, len(fields))
    aliases = {}
    vmem = pl.BlockSpec(memory_space=pltpu.VMEM)
    if previous is not None:
        aliases = {len(operands): 0}
        operands.append(previous)
        specs.append(vmem)
    shape = (bands, groups, 2, steps * tiles // 2, rows // steps // 2 * 2 * cells)
    shapes = [jax.ShapeDtypeStruct(shape, jnp.bfloat16)]
    scratch = [
        pltpu.VMEM((most, tiles * rows, cells), jnp.float32),
        pltpu.VMEM((2 * tiles + 8, cells), jnp.float32),
    ]
    if last is None:
        body = functools.partial(regrid_kernel, steps, listed)
        limit, moved = 12 << 20, len(jobs) * 3 << 20
    else:
        mine, theirs, halves = last
        height, width = mine.shape
        total = bands * groups * shape[3]
        body = functools.partial(finish_kernel, steps, halves, listed, len(operands))
        operands += [mine, theirs]
        specs += [pl.BlockSpec(memory_space=pl.ANY)] * 2
        half = (total // 2, width // 2)
        shapes += [jax.ShapeDtypeStruct(half, kind) for kind in (jnp.float32, jnp.bfloat16) * 2]
        scratch += [
            pltpu.VMEM((2, height, width), jnp.bfloat16),
            pltpu.VMEM((total, width), jnp.float32),
            pltpu.SemaphoreType.DMA((2, 6)),
        ]
        limit, moved = 44 << 20, 4 * height * width
        flops += 4 * total * height * width
    done = pl.pallas_call(
        body,
        out_shape=shapes,
        in_specs=specs,
        out_specs=[vmem] * len(shapes),
        scratch_shapes=scratch,
        input_output_aliases=aliases,
        cost_estimate=pl.CostEstimate(flops=flops, bytes_accessed=moved, transcendentals=0),
        compiler_params=pltpu.CompilerParams(vmem_limit_bytes=limit),
    )(*operands)
    return done[0] if last is None else done[1:]


def embed_kernel(steps, halves, rows_x, mine, theirs, out, total):
    at = pl.program_id(0)
    sub, mine_group = lax.axis_index("sub"), lax.axis_index("grp")
    bands, groups, _, row_count, width = rows_x.shape
    rows = bands * groups * row_count

    @pl.when(at == 0)
    def _():
        total[...] = jnp.zeros_like(total)

    left = rows_x[:, :, sub].reshape(rows, width)
    right = rows_x[:, :, 1 - sub].reshape(rows, width)
    total[...] += jnp.dot(left, mine[...], preferred_element_type=jnp.float32) + jnp.dot(
        right, theirs[...], preferred_element_type=jnp.float32
    )

    @pl.when(at == pl.num_programs(0) - 1)
    def _():
        if out.ndim == 2:
            out[...] = total[...].astype(out.dtype)
        else:
            send_rows(steps, halves, rows_x.shape, mine_group, total, out)


def embed(rows_x, mine, theirs, steps, halves):
    bands, groups, _, row_count, half_width = rows_x.shape
    width = mine.shape[-1]
    grid = 6 if half_width % (6 * 256) == 0 else 3
    step_rows = half_width // grid
    rows = bands * groups * row_count
    chunks = groups * steps * halves
    share = row_count // (steps * halves)
    shape = (chunks, bands * share, width) if share % 4 == 0 else (rows, width)
    weight_spec = pl.BlockSpec((step_rows, width), lambda i: (i, 0))
    out = pl.pallas_call(
        functools.partial(embed_kernel, steps, halves),
        out_shape=jax.ShapeDtypeStruct(shape, jnp.bfloat16),
        grid=(grid,),
        in_specs=[
            pl.BlockSpec((bands, groups, 2, row_count, step_rows), lambda i: (0, 0, 0, 0, i)),
            weight_spec,
            weight_spec,
        ],
        out_specs=pl.BlockSpec(shape, lambda i: (0,) * len(shape)),
        scratch_shapes=[pltpu.VMEM((rows, width), jnp.float32)],
        cost_estimate=pl.CostEstimate(
            flops=4 * rows * mine.shape[0] * width,
            bytes_accessed=4 * mine.shape[0] * width,
            transcendentals=0,
        ),
        compiler_params=pltpu.CompilerParams(
            vmem_limit_bytes=(48 if rows > 1024 else 16) << 20
        ),
    )(rows_x, mine, theirs)
    if share % 4:
        out = out.reshape(bands, chunks, share, width).transpose(1, 0, 2, 3)
        out = out.reshape(chunks, bands * share, width)
    return out


def swap(x, axis):
    return lax.ppermute(x, axis, [(0, 1), (1, 0)])


def per_device(
    ocean_fields,
    ocean_dest,
    ocean_weights,
    ocean_tiles,
    atmos_fields,
    atmos_dest,
    atmos_weights,
    atmos_tiles,
    land_fraction,
    embed_weight,
    embed_bias,
    embed_gain,
):
    nb = lax.axis_size("band")
    nv = lax.axis_size("var")
    ng = lax.axis_size("grp")
    rep = nv * ng
    cap = ocean_weights.shape[3]
    cells = ocean_weights.shape[-1]
    block_count, steps, local_vars, _ = ocean_fields.shape
    patches = land_fraction.shape[2]
    tiles = 2 * patches
    slots = 2 * cap
    share = patches // nv
    me = lax.axis_index("band")
    x, y = lax.axis_index("var"), lax.axis_index("grp")
    quarter = y * nv + x

    flat = (nb, cap * cells, cells)
    ocean_w, atmos_w = ocean_weights.reshape(flat), atmos_weights.reshape(flat)
    ocean_ids, atmos_ids = ocean_tiles.reshape(nb, cap), atmos_tiles.reshape(nb, cap)
    land = land_fraction.reshape(tiles, cells)
    blocks = (block_count, steps * local_vars, cells)
    ocean_f, atmos_f = ocean_fields.reshape(blocks), atmos_fields.reshape(blocks)
    order = ([1, nb - 1] + list(range(2, nb - 1)))[: nb - 1]
    along = lambda shift: [(b, (b + shift) % nb) for b in range(nb)]
    call = functools.partial(
        regrid, bands=nb, steps=steps, tiles=tiles, rows=steps * local_vars, cells=cells
    )

    if ng == 2 and nv == 2 and cap % 2 == 0 and steps == nb:
        each = cap // 2
        pieces = []
        for shift in order:
            pieces.append((shift, 0, each, each))
        *packed, send = pack(
            60, pieces, ocean_w, atmos_w, ocean_ids, atmos_ids, land, ocean_f, atmos_f
        )
        sent = [
            lax.ppermute(piece, "band", along(shift))
            for piece, (shift, _, _, _) in zip(packed[:2], pieces)
        ]
        embed_other, own_land, send = lax.optimization_barrier((embed_weight, land, send))
        own_w = pack(60, [(0, 0, cap, None)], ocean_w, atmos_w, ocean_ids, atmos_ids, own_land)[0]
        embed_other = swap(embed_other, "sub")
        keep, theirs = (ocean_f, atmos_f), (swap(send, "grp"),)
        dest = jnp.where(y == 0, ocean_dest, atmos_dest)
        block_all, used_all = slot_tables(dest, nb, cap)
        def job_of(band, parts, sizes, firsts, fields):
            meta_at = sizes[0] * cells
            tile = parts[0][meta_at + 2 * tiles, :cap].astype(jnp.int32)
            block = lax.dynamic_index_in_dim(block_all, band, 0, keepdims=False)
            used = lax.dynamic_index_in_dim(used_all, band, 0, keepdims=False)
            scale = jnp.where(used, tile + y * tiles, 2 * tiles)
            table = jnp.stack([block, tile, scale]).astype(jnp.int32)
            where = jnp.stack([band] + firsts).astype(jnp.int32)
            return table, where, parts[0], meta_at, parts, sizes, fields

        def with_fields(job, fields):
            return job[:-1] + (fields,)

        def job_at(shift, fields):
            parts, sizes, firsts = [], [], []
            for piece, across, (of, first, size, _) in zip(sent, crossed, pieces):
                if of == shift:
                    parts += [piece, across]
                    sizes += [size, size]
                    firsts += [x * each + first, (1 - x) * each + first]
            return job_of((me - shift) % nb, parts, sizes, firsts, fields)

        ours, others = [(0, keep)], [(1, theirs)]
        jobs = [job_of(me, [own_w], [cap], [jnp.int32(0)], ours)]
        rows_x = call(jobs, None, groups=2)
        for at, (piece, (shift, _, _, _)) in enumerate(zip(packed[2:], pieces[2:])):
            piece, sent[at], rows_x = lax.optimization_barrier((piece, sent[at], rows_x))
            sent.append(lax.ppermute(piece, "band", along(shift)))
        crossed = [swap(piece, "var") for piece in sent]
        jobs += [job_at(shift, ours) for shift in order]
        rows_x = call(
            jobs[1:-1] + [with_fields(job, others) for job in jobs[:-1]], rows_x, groups=2
        )
        keep_x, send_x, keep_y, send_y = call(
            [with_fields(jobs[-1], ours + others)],
            rows_x,
            groups=2,
            last=(embed_weight, embed_other, nv),
        )
        whole, width = keep_x.shape
        part = ((whole // 2, width), jnp.float32), ((whole // 2, width), jnp.bfloat16)
        sum_x, send_x, sum_y, send_y = small(
            add_kernel, part * 2, keep_x, swap(send_x, "var"), keep_y, swap(send_y, "grp")
        )
        own = (whole // 2 // nb, 2 * width)
        own, *send = small(
            functools.partial(split_kernel, order),
            [(own, jnp.float32)] + [(own, jnp.bfloat16)] * len(order),
            sum_x,
            swap(send_x, "grp"),
            sum_y,
            swap(send_y, "var"),
        )
        got = [lax.ppermute(part, "band", along(shift)) for part, shift in zip(send, order)]
        finished = small(
            functools.partial(norm_kernel, nb),
            [(own.shape, jnp.bfloat16)],
            own,
            *got,
            embed_bias.reshape(1, -1),
            embed_gain.reshape(1, -1),
        )[0]
        return finished.reshape(1, share, nb, steps // nb, 2 * width)
    else:
        embed_other = swap(embed_weight, "sub")
        both = jnp.concatenate([ocean_w, atmos_w], axis=1)
        fields = [(0, (jnp.concatenate([ocean_f, atmos_f], axis=0),))]
        ocean_block, ocean_used = slot_tables(ocean_dest, nb, cap)
        atmos_block, atmos_used = slot_tables(atmos_dest, nb, cap)
        block_all = jnp.concatenate([ocean_block, atmos_block + block_count], axis=1)
        used_all = jnp.concatenate([ocean_used, atmos_used], axis=1)
        grid_row = jnp.where(jnp.arange(slots) < cap, 0, tiles)

        def job_of(band, tile, meta, parts):
            block = lax.dynamic_index_in_dim(block_all, band, 0, keepdims=False)
            used = lax.dynamic_index_in_dim(used_all, band, 0, keepdims=False)
            scale = jnp.where(used, tile + grid_row, 2 * tiles)
            table = jnp.stack([block, tile, scale]).astype(jnp.int32)
            where = jnp.stack([band, jnp.int32(0)])
            return table, where, meta, 0, [parts], [slots], fields

        tile_ids = jnp.concatenate([ocean_ids, atmos_ids], axis=1)
        own_tile = lax.dynamic_index_in_dim(tile_ids, me, 0, keepdims=False)
        own_w = lax.dynamic_index_in_dim(both, me, 0, keepdims=False)
        rows_x = call([job_of(me, own_tile, land, own_w)], None, groups=1)
        share_rows = slots * cells // rep
        high = lax.reduce_precision(land, 8, 7)
        low = (land - high).astype(jnp.bfloat16)
        tile_rows = jnp.pad(tile_ids.astype(jnp.bfloat16), ((0, 0), (0, cells - slots)))
        for shift in order:
            target, band = (me + shift) % nb, (me - shift) % nb
            piece = lax.dynamic_slice(
                both, (target, quarter * share_rows, 0), (1, share_rows, cells)
            )[0]
            row = lax.dynamic_slice(tile_rows, (target, 0), (1, cells))
            row = jnp.broadcast_to(row, (16, cells))
            piece = jnp.concatenate([piece, high.astype(jnp.bfloat16), low, row], axis=0)
            parts = lax.all_gather(lax.ppermute(piece, "band", along(shift)), REPL, axis=0)
            meta = parts[0, share_rows:]
            tile = meta[2 * tiles, :slots].astype(jnp.int32)
            parts = parts[:, :share_rows].reshape(slots * cells, cells)
            rows_x = call([job_of(band, tile, meta, parts)], rows_x, groups=1)
        sent = embed(rows_x, embed_weight, embed_other, steps, nv)
        got = lax.all_to_all(sent, ("band", "var"), split_axis=0, concat_axis=0, tiled=True)
    shifted = jnp.sum(got.astype(jnp.float32), axis=0) + embed_bias
    inverse = lax.rsqrt(jnp.mean(shifted * shifted, axis=-1, keepdims=True) + 1e-05)
    finished = (shifted * inverse * embed_gain).astype(jnp.bfloat16)
    width = finished.shape[-1]
    finished = finished.reshape(nb, share, steps // nb, width).transpose(1, 0, 2, 3)
    return finished[None]


def solution(mesh):
    in_specs = (
        P(("grp", "band", "sub"), None, "var", None),
        P(("band", "sub"), None),
        P("band", "sub", None, None, None, None),
        P("band", "sub", None, None),
        P(("grp", "band", "sub"), None, "var", None),
        P(("band", "sub"), None),
        P("band", "sub", None, None, None, None),
        P("band", "sub", None, None),
        P("band", "sub", None, None, None),
        P(("var", "sub"), None),
        P(),
        P(),
    )
    out_specs = P("sub", "var", None, ("grp", "band"), None)
    return jax.shard_map(
        per_device, mesh=mesh, in_specs=in_specs, out_specs=out_specs, check_vma=False
    )
```

```python
import functools

import jax
import jax.numpy as jnp
from jax import lax
from jax.experimental import pallas as pl
from jax.experimental.pallas import tpu as pltpu
from jax.sharding import PartitionSpec as P

REPL = ("grp", "var")


def slot_tables(dest, band_count, cap):
    count = dest.shape[0]
    serial = jnp.arange(count, dtype=jnp.int32)
    band_of = dest[:, 0]
    earlier = (band_of[:, None] == band_of[None, :]) & (serial[None, :] < serial[:, None])
    position = jnp.sum(earlier.astype(jnp.int32), axis=1)
    slot = band_of * cap + position
    hit = slot[None, :] == jnp.arange(band_count * cap, dtype=jnp.int32)[:, None]
    block = jnp.sum(jnp.where(hit, serial[None, :], 0), axis=1)
    used = jnp.any(hit, axis=1)
    return block.reshape(band_count, cap), used.reshape(band_count, cap)


def pack_kernel(pieces, moved, *refs):
    ocean_w, atmos_w, ocean_ids, atmos_ids, land = refs[:5]
    fields, refs = refs[5 : 5 + 2 * moved], refs[5 + 2 * moved :]
    count = len(pieces) + moved
    stages, sem = refs[:count], refs[-1]
    me, bands = lax.axis_index("band"), ocean_w.shape[0]
    x, y = lax.axis_index("var"), lax.axis_index("grp")
    cells, tiles = land.shape[-1], land.shape[0]
    cap = ocean_ids.shape[-1]

    def loads(weights, other):
        found = []
        for at, (stage, (shift, first, size, split)) in enumerate(zip(stages, pieces)):
            start = first if split is None else x * split + first
            found.append(
                pltpu.make_async_copy(
                    weights.at[
                        lax.rem(me + shift, bands),
                        pl.ds(pl.multiple_of(start * cells, cells), size * cells),
                        :,
                    ],
                    stage.at[pl.ds(0, size * cells), :],
                    sem.at[at],
                )
            )
        if moved:
            found.append(pltpu.make_async_copy(fields[other], stages[-1], sem.at[count - 1]))
        return found

    @pl.when(y == 0)
    def _():
        for copy in loads(ocean_w, 1):
            copy.start()

    @pl.when(y == 1)
    def _():
        for copy in loads(atmos_w, 0):
            copy.start()

    fraction = land[...]
    high = fraction.astype(jnp.bfloat16)
    low = (fraction - high.astype(jnp.float32)).astype(jnp.bfloat16)
    for stage, (shift, first, size, split) in zip(stages, pieces):
        if first:
            continue
        target, base = lax.rem(me + shift, bands), size * cells
        stage[pl.ds(base, tiles), :] = high
        stage[pl.ds(base + tiles, tiles), :] = low
        row = jnp.where(y == 0, ocean_ids[pl.ds(target, 1), :], atmos_ids[pl.ds(target, 1), :])
        row = jnp.broadcast_to(row.astype(jnp.float32), (16, cap)).astype(jnp.bfloat16)
        stage[pl.ds(base + 2 * tiles, 16), :] = jnp.zeros((16, cells), jnp.bfloat16)
        stage[pl.ds(base + 2 * tiles, 16), pl.ds(0, cap)] = row
    for load in loads(ocean_w, 1):
        load.wait()


def pack(limit, pieces, ocean_w, atmos_w, ocean_ids, atmos_ids, land, *fields):
    cells, tiles = land.shape[-1], land.shape[0]
    any_spec = pl.BlockSpec(memory_space=pl.ANY)
    vmem = pl.BlockSpec(memory_space=pltpu.VMEM)
    sizes = [size * cells + (0 if first else 2 * tiles + 16) for _, first, size, _ in pieces]
    shapes = [(n, cells) for n in sizes] + [f.shape for f in fields[:1]]
    return pl.pallas_call(
        functools.partial(pack_kernel, pieces, len(fields) // 2),
        out_shape=[jax.ShapeDtypeStruct(shape, jnp.bfloat16) for shape in shapes],
        in_specs=[any_spec] * 2 + [vmem] * 3 + [any_spec] * len(fields),
        out_specs=[vmem] * len(shapes),
        scratch_shapes=[pltpu.SemaphoreType.DMA((len(shapes),))],
        cost_estimate=pl.CostEstimate(flops=0, bytes_accessed=2 << 20, transcendentals=0),
        compiler_params=pltpu.CompilerParams(vmem_limit_bytes=limit << 20),
    )(ocean_w, atmos_w, ocean_ids, atmos_ids, land, *fields)


def run_jobs(steps, jobs, refs, out, acc, scale):
    local_rows, cells = acc.shape[1] // (scale.shape[0] // 2 - 4), acc.shape[2]
    tiles = acc.shape[1] // local_rows
    local_vars = local_rows // steps
    half_vars = local_vars // 2
    for table, where, meta, meta_at, parts, groups in jobs:
        table, where, meta = refs[table], refs[where], refs[meta]
        if meta.dtype == jnp.float32:
            land = meta[...]
        else:
            high = meta[pl.ds(meta_at, tiles), :].astype(jnp.float32)
            land = high + meta[pl.ds(meta_at + tiles, tiles), :].astype(jnp.float32)
        scale[pl.ds(0, tiles), :] = 1.0 - land
        scale[pl.ds(tiles, tiles), :] = land
        scale[pl.ds(2 * tiles, 8), :] = jnp.zeros((8, cells), jnp.float32)
        acc[pl.ds(0, len(groups))] = jnp.zeros((len(groups),) + acc.shape[1:], jnp.float32)
        for at, (part, size) in enumerate(parts):
            first = where[1 + at]
            for s in range(size):
                slot = first + s
                block = table[0, slot]
                moved = []
                for _, fields in groups:
                    piece = refs[fields[0]][block]
                    if len(fields) > 1:
                        piece = jnp.where(
                            lax.axis_index("grp") == 0, piece, refs[fields[1]][block]
                        )
                    moved.append(piece)
                moved = moved[0] if len(moved) == 1 else jnp.concatenate(moved, axis=0)
                dense = jnp.dot(
                    moved,
                    refs[part][pl.ds(s * cells, cells), :],
                    preferred_element_type=jnp.float32,
                )
                dense = dense * scale[pl.ds(table[2, slot], 1), :]
                span = pl.ds(pl.multiple_of(table[1, slot] * local_rows, local_rows), local_rows)
                for g in range(len(groups)):
                    acc[g, span, :] += dense[g * local_rows : (g + 1) * local_rows]
        for g, (to, _) in enumerate(groups):
            for v in range(local_vars):
                for q in range(2):
                    column = (v % half_vars * 2 + q) * cells
                    rows = [
                        acc[g, pl.ds(q * local_rows + t * local_vars + v, tiles // 2, 2 * local_rows), :]
                        for t in range(steps)
                    ]
                    out[where[0], to, v // half_vars, :, pl.ds(column, cells)] = jnp.concatenate(
                        rows, axis=0
                    ).astype(out.dtype)


def regrid_kernel(steps, jobs, *refs):
    run_jobs(steps, jobs, refs, *refs[-3:])


def finish_kernel(steps, halves, jobs, count, *refs):
    mine, theirs, rows_x, out, acc, scale, weight, total, sem = refs[count:]
    sub, mine_group = lax.axis_index("sub"), lax.axis_index("grp")
    chunks = sem.shape[0]
    height = mine.shape[0] // chunks

    def copy(chunk):
        span = pl.ds(pl.multiple_of(chunk * height, height), height)
        return pltpu.make_async_copy(theirs.at[span, :], weight.at[span, :], sem.at[chunk])

    for chunk in range(chunks):
        copy(chunk).start()
    run_jobs(steps, jobs, refs, rows_x, acc, scale)
    total[...] = jnp.zeros_like(total)

    @pl.loop(0, chunks)
    def _(chunk):
        span = pl.ds(pl.multiple_of(chunk * height, height), height)
        left, right = (
            rows_x[:, :, place, :, span].reshape(total.shape[0], height) for place in (sub, 1 - sub)
        )
        copy(chunk).wait()
        total[...] += jnp.dot(
            left, mine[span, :], preferred_element_type=jnp.float32
        ) + jnp.dot(right, weight[span, :], preferred_element_type=jnp.float32)

    send_rows(steps, halves, rows_x.shape, mine_group, total, out)


def send_rows(steps, halves, shape, mine_group, total, out):
    bands, groups, _, row_count, _ = shape
    count = steps * halves
    share = row_count // count
    for g in range(groups):
        base = (mine_group if g == 0 else 1 - mine_group) * count if groups > 1 else 0
        for chunk in range(count):
            pieces = [
                total[pl.ds((b * groups + g) * row_count + chunk * share, share), :]
                for b in range(bands)
            ]
            out[base + chunk] = jnp.concatenate(pieces, axis=0).astype(out.dtype)


def regrid(jobs, previous, bands, groups, steps, tiles, rows, cells, last=None):
    operands, specs, places = [], [], {}

    def place(array, space):
        if id(array) not in places:
            places[id(array)] = len(operands)
            operands.append(array)
            specs.append(pl.BlockSpec(memory_space=space))
        return places[id(array)]

    listed, flops, most = [], 0, 1
    for table, where, meta, meta_at, parts, sizes, fields in jobs:
        listed.append(
            (
                place(table, pltpu.SMEM),
                place(where, pltpu.SMEM),
                place(meta, pltpu.VMEM),
                meta_at,
                [(place(part, pltpu.VMEM), size) for part, size in zip(parts, sizes)],
                [(to, [place(f, pltpu.VMEM) for f in pair]) for to, pair in fields],
            )
        )
        flops += 2 * sum(sizes) * len(fields) * rows * cells * cells
        most = max(most, len(fields))
    aliases = {}
    vmem = pl.BlockSpec(memory_space=pltpu.VMEM)
    if previous is not None:
        aliases = {len(operands): 0}
        operands.append(previous)
        specs.append(vmem)
    shape = (bands, groups, 2, steps * tiles // 2, rows // steps // 2 * 2 * cells)
    shapes = [jax.ShapeDtypeStruct(shape, jnp.bfloat16)]
    scratch = [
        pltpu.VMEM((most, tiles * rows, cells), jnp.float32),
        pltpu.VMEM((2 * tiles + 8, cells), jnp.float32),
    ]
    if last is None:
        body = functools.partial(regrid_kernel, steps, listed)
        limit, moved = 12 << 20, len(jobs) * 3 << 20
    else:
        mine, theirs, halves = last
        height, width = mine.shape
        total = bands * groups * shape[3]
        body = functools.partial(finish_kernel, steps, halves, listed, len(operands))
        operands += [mine, theirs]
        specs += [vmem, pl.BlockSpec(memory_space=pl.ANY)]
        count = groups * steps * halves
        shapes.append(jax.ShapeDtypeStruct((count, total // count, width), jnp.bfloat16))
        scratch += [
            pltpu.VMEM((height, width), jnp.bfloat16),
            pltpu.VMEM((total, width), jnp.float32),
            pltpu.SemaphoreType.DMA((6,)),
        ]
        limit, moved = 24 << 20, 4 * height * width
        flops += 4 * total * height * width
    done = pl.pallas_call(
        body,
        out_shape=shapes,
        in_specs=specs,
        out_specs=[vmem] * len(shapes),
        scratch_shapes=scratch,
        input_output_aliases=aliases,
        cost_estimate=pl.CostEstimate(flops=flops, bytes_accessed=moved, transcendentals=0),
        compiler_params=pltpu.CompilerParams(vmem_limit_bytes=limit),
    )(*operands)
    return done[-1]


def embed_kernel(steps, halves, rows_x, mine, theirs, out, total):
    at = pl.program_id(0)
    sub, mine_group = lax.axis_index("sub"), lax.axis_index("grp")
    bands, groups, _, row_count, width = rows_x.shape
    rows = bands * groups * row_count

    @pl.when(at == 0)
    def _():
        total[...] = jnp.zeros_like(total)

    left = rows_x[:, :, sub].reshape(rows, width)
    right = rows_x[:, :, 1 - sub].reshape(rows, width)
    total[...] += jnp.dot(left, mine[...], preferred_element_type=jnp.float32) + jnp.dot(
        right, theirs[...], preferred_element_type=jnp.float32
    )

    @pl.when(at == pl.num_programs(0) - 1)
    def _():
        if out.ndim == 2:
            out[...] = total[...].astype(out.dtype)
        else:
            send_rows(steps, halves, rows_x.shape, mine_group, total, out)


def embed(rows_x, mine, theirs, steps, halves):
    bands, groups, _, row_count, half_width = rows_x.shape
    width = mine.shape[-1]
    grid = 6 if half_width % (6 * 256) == 0 else 3
    step_rows = half_width // grid
    rows = bands * groups * row_count
    chunks = groups * steps * halves
    share = row_count // (steps * halves)
    shape = (chunks, bands * share, width) if share % 4 == 0 else (rows, width)
    weight_spec = pl.BlockSpec((step_rows, width), lambda i: (i, 0))
    out = pl.pallas_call(
        functools.partial(embed_kernel, steps, halves),
        out_shape=jax.ShapeDtypeStruct(shape, jnp.bfloat16),
        grid=(grid,),
        in_specs=[
            pl.BlockSpec((bands, groups, 2, row_count, step_rows), lambda i: (0, 0, 0, 0, i)),
            weight_spec,
            weight_spec,
        ],
        out_specs=pl.BlockSpec(shape, lambda i: (0,) * len(shape)),
        scratch_shapes=[pltpu.VMEM((rows, width), jnp.float32)],
        cost_estimate=pl.CostEstimate(
            flops=4 * rows * mine.shape[0] * width,
            bytes_accessed=4 * mine.shape[0] * width,
            transcendentals=0,
        ),
        compiler_params=pltpu.CompilerParams(
            vmem_limit_bytes=(48 if rows > 1024 else 16) << 20
        ),
    )(rows_x, mine, theirs)
    if share % 4:
        out = out.reshape(bands, chunks, share, width).transpose(1, 0, 2, 3)
        out = out.reshape(chunks, bands * share, width)
    return out


def swap(x, axis):
    return lax.ppermute(x, axis, [(0, 1), (1, 0)])


def per_device(
    ocean_fields,
    ocean_dest,
    ocean_weights,
    ocean_tiles,
    atmos_fields,
    atmos_dest,
    atmos_weights,
    atmos_tiles,
    land_fraction,
    embed_weight,
    embed_bias,
    embed_gain,
):
    nb = lax.axis_size("band")
    nv = lax.axis_size("var")
    ng = lax.axis_size("grp")
    rep = nv * ng
    cap = ocean_weights.shape[3]
    cells = ocean_weights.shape[-1]
    block_count, steps, local_vars, _ = ocean_fields.shape
    patches = land_fraction.shape[2]
    tiles = 2 * patches
    slots = 2 * cap
    share = patches // nv
    me = lax.axis_index("band")
    x, y = lax.axis_index("var"), lax.axis_index("grp")
    quarter = y * nv + x

    flat = (nb, cap * cells, cells)
    ocean_w, atmos_w = ocean_weights.reshape(flat), atmos_weights.reshape(flat)
    ocean_ids, atmos_ids = ocean_tiles.reshape(nb, cap), atmos_tiles.reshape(nb, cap)
    land = land_fraction.reshape(tiles, cells)
    blocks = (block_count, steps * local_vars, cells)
    ocean_f, atmos_f = ocean_fields.reshape(blocks), atmos_fields.reshape(blocks)
    order = ([1, nb - 1] + list(range(2, nb - 1)))[: nb - 1]
    along = lambda shift: [(b, (b + shift) % nb) for b in range(nb)]
    call = functools.partial(
        regrid, bands=nb, steps=steps, tiles=tiles, rows=steps * local_vars, cells=cells
    )

    if ng == 2 and nv == 2 and cap % 2 == 0 and steps == nb:
        each = cap // 2
        pieces = []
        for shift in order:
            pieces.append((shift, 0, each, each))
        *packed, send = pack(
            60, pieces, ocean_w, atmos_w, ocean_ids, atmos_ids, land, ocean_f, atmos_f
        )
        sent = [
            lax.ppermute(piece, "band", along(shift))
            for piece, (shift, _, _, _) in zip(packed[:2], pieces)
        ]
        embed_other, own_land, send = lax.optimization_barrier((embed_weight, land, send))
        own_w = pack(60, [(0, 0, cap, None)], ocean_w, atmos_w, ocean_ids, atmos_ids, own_land)[0]
        embed_other = swap(embed_other, "sub")
        keep, theirs = (ocean_f, atmos_f), (swap(send, "grp"),)
        dest = jnp.where(y == 0, ocean_dest, atmos_dest)
        block_all, used_all = slot_tables(dest, nb, cap)
        def job_of(band, parts, sizes, firsts, fields):
            meta_at = sizes[0] * cells
            tile = parts[0][meta_at + 2 * tiles, :cap].astype(jnp.int32)
            block = lax.dynamic_index_in_dim(block_all, band, 0, keepdims=False)
            used = lax.dynamic_index_in_dim(used_all, band, 0, keepdims=False)
            scale = jnp.where(used, tile + y * tiles, 2 * tiles)
            table = jnp.stack([block, tile, scale]).astype(jnp.int32)
            where = jnp.stack([band] + firsts).astype(jnp.int32)
            return table, where, parts[0], meta_at, parts, sizes, fields

        def with_fields(job, fields):
            return job[:-1] + (fields,)

        def job_at(shift, fields):
            parts, sizes, firsts = [], [], []
            for piece, across, (of, first, size, _) in zip(sent, crossed, pieces):
                if of == shift:
                    parts += [piece, across]
                    sizes += [size, size]
                    firsts += [x * each + first, (1 - x) * each + first]
            return job_of((me - shift) % nb, parts, sizes, firsts, fields)

        ours, others = [(0, keep)], [(1, theirs)]
        jobs = [job_of(me, [own_w], [cap], [jnp.int32(0)], ours)]
        rows_x = call(jobs, None, groups=2)
        for at, (piece, (shift, _, _, _)) in enumerate(zip(packed[2:], pieces[2:])):
            piece, sent[at], rows_x = lax.optimization_barrier((piece, sent[at], rows_x))
            sent.append(lax.ppermute(piece, "band", along(shift)))
        crossed = [swap(piece, "var") for piece in sent]
        jobs += [job_at(shift, ours) for shift in order]
        rows_x = call(
            jobs[1:-1] + [with_fields(job, others) for job in jobs[:-1]], rows_x, groups=2
        )
        sent = call(
            [with_fields(jobs[-1], ours + others)],
            rows_x,
            groups=2,
            last=(embed_weight, embed_other, nv),
        )
        got = lax.all_to_all(sent, ("grp", "band", "var"), split_axis=0, concat_axis=0, tiled=True)
    else:
        embed_other = swap(embed_weight, "sub")
        both = jnp.concatenate([ocean_w, atmos_w], axis=1)
        fields = [(0, (jnp.concatenate([ocean_f, atmos_f], axis=0),))]
        ocean_block, ocean_used = slot_tables(ocean_dest, nb, cap)
        atmos_block, atmos_used = slot_tables(atmos_dest, nb, cap)
        block_all = jnp.concatenate([ocean_block, atmos_block + block_count], axis=1)
        used_all = jnp.concatenate([ocean_used, atmos_used], axis=1)
        grid_row = jnp.where(jnp.arange(slots) < cap, 0, tiles)

        def job_of(band, tile, meta, parts):
            block = lax.dynamic_index_in_dim(block_all, band, 0, keepdims=False)
            used = lax.dynamic_index_in_dim(used_all, band, 0, keepdims=False)
            scale = jnp.where(used, tile + grid_row, 2 * tiles)
            table = jnp.stack([block, tile, scale]).astype(jnp.int32)
            where = jnp.stack([band, jnp.int32(0)])
            return table, where, meta, 0, [parts], [slots], fields

        tile_ids = jnp.concatenate([ocean_ids, atmos_ids], axis=1)
        own_tile = lax.dynamic_index_in_dim(tile_ids, me, 0, keepdims=False)
        own_w = lax.dynamic_index_in_dim(both, me, 0, keepdims=False)
        rows_x = call([job_of(me, own_tile, land, own_w)], None, groups=1)
        share_rows = slots * cells // rep
        high = lax.reduce_precision(land, 8, 7)
        low = (land - high).astype(jnp.bfloat16)
        tile_rows = jnp.pad(tile_ids.astype(jnp.bfloat16), ((0, 0), (0, cells - slots)))
        for shift in order:
            target, band = (me + shift) % nb, (me - shift) % nb
            piece = lax.dynamic_slice(
                both, (target, quarter * share_rows, 0), (1, share_rows, cells)
            )[0]
            row = lax.dynamic_slice(tile_rows, (target, 0), (1, cells))
            row = jnp.broadcast_to(row, (16, cells))
            piece = jnp.concatenate([piece, high.astype(jnp.bfloat16), low, row], axis=0)
            parts = lax.all_gather(lax.ppermute(piece, "band", along(shift)), REPL, axis=0)
            meta = parts[0, share_rows:]
            tile = meta[2 * tiles, :slots].astype(jnp.int32)
            parts = parts[:, :share_rows].reshape(slots * cells, cells)
            rows_x = call([job_of(band, tile, meta, parts)], rows_x, groups=1)
        sent = embed(rows_x, embed_weight, embed_other, steps, nv)
        got = lax.all_to_all(sent, ("band", "var"), split_axis=0, concat_axis=0, tiled=True)
    shifted = jnp.sum(got.astype(jnp.float32), axis=0) + embed_bias
    inverse = lax.rsqrt(jnp.mean(shifted * shifted, axis=-1, keepdims=True) + 1e-05)
    finished = (shifted * inverse * embed_gain).astype(jnp.bfloat16)
    width = finished.shape[-1]
    finished = finished.reshape(nb, share, steps // nb, width).transpose(1, 0, 2, 3)
    return finished[None]


def solution(mesh):
    in_specs = (
        P(("grp", "band", "sub"), None, "var", None),
        P(("band", "sub"), None),
        P("band", "sub", None, None, None, None),
        P("band", "sub", None, None),
        P(("grp", "band", "sub"), None, "var", None),
        P(("band", "sub"), None),
        P("band", "sub", None, None, None, None),
        P("band", "sub", None, None),
        P("band", "sub", None, None, None),
        P(("var", "sub"), None),
        P(),
        P(),
    )
    out_specs = P("sub", "var", None, ("grp", "band"), None)
    return jax.shard_map(
        per_device, mesh=mesh, in_specs=in_specs, out_specs=out_specs, check_vma=False
    )
```

```python
import functools

import jax
import jax.numpy as jnp
from jax import lax
from jax.experimental import pallas as pl
from jax.experimental.pallas import tpu as pltpu
from jax.sharding import PartitionSpec as P

REPL = ("grp", "var")


def slot_tables(dest, band_count, cap):
    count = dest.shape[0]
    serial = jnp.arange(count, dtype=jnp.int32)
    band_of = dest[:, 0]
    earlier = (band_of[:, None] == band_of[None, :]) & (serial[None, :] < serial[:, None])
    position = jnp.sum(earlier.astype(jnp.int32), axis=1)
    slot = band_of * cap + position
    hit = slot[None, :] == jnp.arange(band_count * cap, dtype=jnp.int32)[:, None]
    block = jnp.sum(jnp.where(hit, serial[None, :], 0), axis=1)
    used = jnp.any(hit, axis=1)
    return block.reshape(band_count, cap), used.reshape(band_count, cap)


def pack_kernel(pieces, moved, *refs):
    ocean_w, atmos_w = refs[:2]
    fields, held = refs[5 : 5 + 2 * moved], refs[5 + 2 * moved :]
    count = len(pieces) + moved
    stages, (ocean_ids, atmos_ids, land, sem) = held[:count], held[count:]
    me, bands = lax.axis_index("band"), ocean_w.shape[0]
    x, y = lax.axis_index("var"), lax.axis_index("grp")
    cells, tiles = land.shape[-1], land.shape[0]
    cap = ocean_ids.shape[-1]

    def loads(weights, other):
        found = []
        for at, (stage, (shift, first, size, split)) in enumerate(zip(stages, pieces)):
            start = first if split is None else x * split + first
            found.append(
                pltpu.make_async_copy(
                    weights.at[
                        lax.rem(me + shift, bands),
                        pl.ds(pl.multiple_of(start * cells, cells), size * cells),
                        :,
                    ],
                    stage.at[pl.ds(0, size * cells), :],
                    sem.at[at],
                )
            )
        if moved:
            found.append(pltpu.make_async_copy(fields[other], stages[-1], sem.at[count - 1]))
        return found

    @pl.when(y == 0)
    def _():
        for copy in loads(ocean_w, 1):
            copy.start()

    @pl.when(y == 1)
    def _():
        for copy in loads(atmos_w, 0):
            copy.start()

    tables = [
        pltpu.make_async_copy(source, target, sem.at[count + at])
        for at, (source, target) in enumerate(zip(refs[2:5], (ocean_ids, atmos_ids, land)))
    ]
    for copy in tables:
        copy.start()
    for copy in tables:
        copy.wait()
    fraction = land[...]
    high = fraction.astype(jnp.bfloat16)
    low = (fraction - high.astype(jnp.float32)).astype(jnp.bfloat16)
    for stage, (shift, first, size, split) in zip(stages, pieces):
        if first:
            continue
        target, base = lax.rem(me + shift, bands), size * cells
        stage[pl.ds(base, tiles), :] = high
        stage[pl.ds(base + tiles, tiles), :] = low
        row = jnp.where(y == 0, ocean_ids[pl.ds(target, 1), :], atmos_ids[pl.ds(target, 1), :])
        row = jnp.broadcast_to(row.astype(jnp.float32), (16, cap)).astype(jnp.bfloat16)
        stage[pl.ds(base + 2 * tiles, 16), :] = jnp.zeros((16, cells), jnp.bfloat16)
        stage[pl.ds(base + 2 * tiles, 16), pl.ds(0, cap)] = row
    for load in loads(ocean_w, 1):
        load.wait()


def pack(limit, pieces, ocean_w, atmos_w, ocean_ids, atmos_ids, land, *fields):
    cells, tiles = land.shape[-1], land.shape[0]
    any_spec = pl.BlockSpec(memory_space=pl.ANY)
    vmem = pl.BlockSpec(memory_space=pltpu.VMEM)
    sizes = [size * cells + (0 if first else 2 * tiles + 16) for _, first, size, _ in pieces]
    shapes = [(n, cells) for n in sizes] + [f.shape for f in fields[:1]]
    return pl.pallas_call(
        functools.partial(pack_kernel, pieces, len(fields) // 2),
        out_shape=[jax.ShapeDtypeStruct(shape, jnp.bfloat16) for shape in shapes],
        in_specs=[any_spec] * (5 + len(fields)),
        out_specs=[vmem] * len(shapes),
        scratch_shapes=[pltpu.VMEM(a.shape, a.dtype) for a in (ocean_ids, atmos_ids, land)]
        + [pltpu.SemaphoreType.DMA((len(shapes) + 3,))],
        cost_estimate=pl.CostEstimate(flops=0, bytes_accessed=2 << 20, transcendentals=0),
        compiler_params=pltpu.CompilerParams(vmem_limit_bytes=limit << 20),
    )(ocean_w, atmos_w, ocean_ids, atmos_ids, land, *fields)


def run_jobs(steps, jobs, refs, out, acc, scale):
    local_rows, cells = acc.shape[1] // (scale.shape[0] // 2 - 4), acc.shape[2]
    tiles = acc.shape[1] // local_rows
    local_vars = local_rows // steps
    half_vars = local_vars // 2
    for table, where, meta, meta_at, parts, groups in jobs:
        table, where, meta = refs[table], refs[where], refs[meta]
        if meta.dtype == jnp.float32:
            land = meta[...]
        else:
            high = meta[pl.ds(meta_at, tiles), :].astype(jnp.float32)
            land = high + meta[pl.ds(meta_at + tiles, tiles), :].astype(jnp.float32)
        scale[pl.ds(0, tiles), :] = 1.0 - land
        scale[pl.ds(tiles, tiles), :] = land
        scale[pl.ds(2 * tiles, 8), :] = jnp.zeros((8, cells), jnp.float32)
        acc[pl.ds(0, len(groups))] = jnp.zeros((len(groups),) + acc.shape[1:], jnp.float32)
        for at, (part, size) in enumerate(parts):
            first = where[1 + at]
            for s in range(size):
                slot = first + s
                block = table[0, slot]
                moved = []
                for _, fields in groups:
                    piece = refs[fields[0]][block]
                    if len(fields) > 1:
                        piece = jnp.where(
                            lax.axis_index("grp") == 0, piece, refs[fields[1]][block]
                        )
                    moved.append(piece)
                moved = moved[0] if len(moved) == 1 else jnp.concatenate(moved, axis=0)
                dense = jnp.dot(
                    moved,
                    refs[part][pl.ds(s * cells, cells), :],
                    preferred_element_type=jnp.float32,
                )
                dense = dense * scale[pl.ds(table[2, slot], 1), :]
                span = pl.ds(pl.multiple_of(table[1, slot] * local_rows, local_rows), local_rows)
                for g in range(len(groups)):
                    acc[g, span, :] += dense[g * local_rows : (g + 1) * local_rows]
        for g, (to, _) in enumerate(groups):
            for v in range(local_vars):
                for q in range(2):
                    column = (v % half_vars * 2 + q) * cells
                    rows = [
                        acc[g, pl.ds(q * local_rows + t * local_vars + v, tiles // 2, 2 * local_rows), :]
                        for t in range(steps)
                    ]
                    out[where[0], to, v // half_vars, :, pl.ds(column, cells)] = jnp.concatenate(
                        rows, axis=0
                    ).astype(out.dtype)


def regrid_kernel(steps, jobs, *refs):
    run_jobs(steps, jobs, refs, *refs[-3:])


def finish_kernel(steps, halves, jobs, count, *refs):
    mine, theirs, rows_x, out, acc, scale, weight, total, sem = refs[count:]
    sub, mine_group = lax.axis_index("sub"), lax.axis_index("grp")
    chunks = sem.shape[0]
    height = mine.shape[0] // chunks

    def copy(chunk):
        span = pl.ds(pl.multiple_of(chunk * height, height), height)
        return pltpu.make_async_copy(theirs.at[span, :], weight.at[span, :], sem.at[chunk])

    for chunk in range(chunks):
        copy(chunk).start()
    run_jobs(steps, jobs, refs, rows_x, acc, scale)
    total[...] = jnp.zeros_like(total)

    @pl.loop(0, chunks)
    def _(chunk):
        span = pl.ds(pl.multiple_of(chunk * height, height), height)
        left, right = (
            rows_x[:, :, place, :, span].reshape(total.shape[0], height) for place in (sub, 1 - sub)
        )
        copy(chunk).wait()
        total[...] += jnp.dot(
            left, mine[span, :], preferred_element_type=jnp.float32
        ) + jnp.dot(right, weight[span, :], preferred_element_type=jnp.float32)

    send_rows(steps, halves, rows_x.shape, mine_group, total, out)


def send_rows(steps, halves, shape, mine_group, total, out):
    bands, groups, _, row_count, _ = shape
    count = steps * halves
    share = row_count // count
    for g in range(groups):
        base = (mine_group if g == 0 else 1 - mine_group) * count if groups > 1 else 0
        for chunk in range(count):
            pieces = [
                total[pl.ds((b * groups + g) * row_count + chunk * share, share), :]
                for b in range(bands)
            ]
            out[base + chunk] = jnp.concatenate(pieces, axis=0).astype(out.dtype)


def regrid(jobs, previous, bands, groups, steps, tiles, rows, cells, last=None):
    operands, specs, places = [], [], {}

    def place(array, space):
        if id(array) not in places:
            places[id(array)] = len(operands)
            operands.append(array)
            specs.append(pl.BlockSpec(memory_space=space))
        return places[id(array)]

    listed, flops, most = [], 0, 1
    for table, where, meta, meta_at, parts, sizes, fields in jobs:
        listed.append(
            (
                place(table, pltpu.SMEM),
                place(where, pltpu.SMEM),
                place(meta, pltpu.VMEM),
                meta_at,
                [(place(part, pltpu.VMEM), size) for part, size in zip(parts, sizes)],
                [(to, [place(f, pltpu.VMEM) for f in pair]) for to, pair in fields],
            )
        )
        flops += 2 * sum(sizes) * len(fields) * rows * cells * cells
        most = max(most, len(fields))
    aliases = {}
    vmem = pl.BlockSpec(memory_space=pltpu.VMEM)
    if previous is not None:
        aliases = {len(operands): 0}
        operands.append(previous)
        specs.append(vmem)
    shape = (bands, groups, 2, steps * tiles // 2, rows // steps // 2 * 2 * cells)
    shapes = [jax.ShapeDtypeStruct(shape, jnp.bfloat16)]
    scratch = [
        pltpu.VMEM((most, tiles * rows, cells), jnp.float32),
        pltpu.VMEM((2 * tiles + 8, cells), jnp.float32),
    ]
    if last is None:
        body = functools.partial(regrid_kernel, steps, listed)
        limit, moved = 12 << 20, len(jobs) * 3 << 20
    else:
        mine, theirs, halves = last
        height, width = mine.shape
        total = bands * groups * shape[3]
        body = functools.partial(finish_kernel, steps, halves, listed, len(operands))
        operands += [mine, theirs]
        specs += [vmem, pl.BlockSpec(memory_space=pl.ANY)]
        count = groups * steps * halves
        shapes.append(jax.ShapeDtypeStruct((count, total // count, width), jnp.bfloat16))
        scratch += [
            pltpu.VMEM((height, width), jnp.bfloat16),
            pltpu.VMEM((total, width), jnp.float32),
            pltpu.SemaphoreType.DMA((6,)),
        ]
        limit, moved = 24 << 20, 4 * height * width
        flops += 4 * total * height * width
    done = pl.pallas_call(
        body,
        out_shape=shapes,
        in_specs=specs,
        out_specs=[vmem] * len(shapes),
        scratch_shapes=scratch,
        input_output_aliases=aliases,
        cost_estimate=pl.CostEstimate(flops=flops, bytes_accessed=moved, transcendentals=0),
        compiler_params=pltpu.CompilerParams(vmem_limit_bytes=limit),
    )(*operands)
    return done[-1]


def embed_kernel(steps, halves, rows_x, mine, theirs, out, total):
    at = pl.program_id(0)
    sub, mine_group = lax.axis_index("sub"), lax.axis_index("grp")
    bands, groups, _, row_count, width = rows_x.shape
    rows = bands * groups * row_count

    @pl.when(at == 0)
    def _():
        total[...] = jnp.zeros_like(total)

    left = rows_x[:, :, sub].reshape(rows, width)
    right = rows_x[:, :, 1 - sub].reshape(rows, width)
    total[...] += jnp.dot(left, mine[...], preferred_element_type=jnp.float32) + jnp.dot(
        right, theirs[...], preferred_element_type=jnp.float32
    )

    @pl.when(at == pl.num_programs(0) - 1)
    def _():
        if out.ndim == 2:
            out[...] = total[...].astype(out.dtype)
        else:
            send_rows(steps, halves, rows_x.shape, mine_group, total, out)


def embed(rows_x, mine, theirs, steps, halves):
    bands, groups, _, row_count, half_width = rows_x.shape
    width = mine.shape[-1]
    grid = 6 if half_width % (6 * 256) == 0 else 3
    step_rows = half_width // grid
    rows = bands * groups * row_count
    chunks = groups * steps * halves
    share = row_count // (steps * halves)
    shape = (chunks, bands * share, width) if share % 4 == 0 else (rows, width)
    weight_spec = pl.BlockSpec((step_rows, width), lambda i: (i, 0))
    out = pl.pallas_call(
        functools.partial(embed_kernel, steps, halves),
        out_shape=jax.ShapeDtypeStruct(shape, jnp.bfloat16),
        grid=(grid,),
        in_specs=[
            pl.BlockSpec((bands, groups, 2, row_count, step_rows), lambda i: (0, 0, 0, 0, i)),
            weight_spec,
            weight_spec,
        ],
        out_specs=pl.BlockSpec(shape, lambda i: (0,) * len(shape)),
        scratch_shapes=[pltpu.VMEM((rows, width), jnp.float32)],
        cost_estimate=pl.CostEstimate(
            flops=4 * rows * mine.shape[0] * width,
            bytes_accessed=4 * mine.shape[0] * width,
            transcendentals=0,
        ),
        compiler_params=pltpu.CompilerParams(
            vmem_limit_bytes=(48 if rows > 1024 else 16) << 20
        ),
    )(rows_x, mine, theirs)
    if share % 4:
        out = out.reshape(bands, chunks, share, width).transpose(1, 0, 2, 3)
        out = out.reshape(chunks, bands * share, width)
    return out


def swap(x, axis):
    return lax.ppermute(x, axis, [(0, 1), (1, 0)])


def per_device(
    ocean_fields,
    ocean_dest,
    ocean_weights,
    ocean_tiles,
    atmos_fields,
    atmos_dest,
    atmos_weights,
    atmos_tiles,
    land_fraction,
    embed_weight,
    embed_bias,
    embed_gain,
):
    nb = lax.axis_size("band")
    nv = lax.axis_size("var")
    ng = lax.axis_size("grp")
    rep = nv * ng
    cap = ocean_weights.shape[3]
    cells = ocean_weights.shape[-1]
    block_count, steps, local_vars, _ = ocean_fields.shape
    patches = land_fraction.shape[2]
    tiles = 2 * patches
    slots = 2 * cap
    share = patches // nv
    me = lax.axis_index("band")
    x, y = lax.axis_index("var"), lax.axis_index("grp")
    quarter = y * nv + x

    flat = (nb, cap * cells, cells)
    ocean_w, atmos_w = ocean_weights.reshape(flat), atmos_weights.reshape(flat)
    ocean_ids, atmos_ids = ocean_tiles.reshape(nb, cap), atmos_tiles.reshape(nb, cap)
    land = land_fraction.reshape(tiles, cells)
    blocks = (block_count, steps * local_vars, cells)
    ocean_f, atmos_f = ocean_fields.reshape(blocks), atmos_fields.reshape(blocks)
    order = ([1, nb - 1] + list(range(2, nb - 1)))[: nb - 1]
    along = lambda shift: [(b, (b + shift) % nb) for b in range(nb)]
    call = functools.partial(
        regrid, bands=nb, steps=steps, tiles=tiles, rows=steps * local_vars, cells=cells
    )

    if ng == 2 and nv == 2 and cap % 2 == 0 and steps == nb:
        each = cap // 2
        pieces = []
        for shift in order:
            pieces.append((shift, 0, each, each))
        *packed, send = pack(
            60, pieces, ocean_w, atmos_w, ocean_ids, atmos_ids, land, ocean_f, atmos_f
        )
        sent = [
            lax.ppermute(piece, "band", along(shift))
            for piece, (shift, _, _, _) in zip(packed[:2], pieces)
        ]
        embed_other, own_land, send = lax.optimization_barrier((embed_weight, land, send))
        own_w = pack(60, [(0, 0, cap, None)], ocean_w, atmos_w, ocean_ids, atmos_ids, own_land)[0]
        embed_other = swap(embed_other, "sub")
        keep, theirs = (ocean_f, atmos_f), (swap(send, "grp"),)
        dest = jnp.where(y == 0, ocean_dest, atmos_dest)
        block_all, used_all = slot_tables(dest, nb, cap)
        def job_of(band, parts, sizes, firsts, fields):
            meta_at = sizes[0] * cells
            tile = parts[0][meta_at + 2 * tiles, :cap].astype(jnp.int32)
            block = lax.dynamic_index_in_dim(block_all, band, 0, keepdims=False)
            used = lax.dynamic_index_in_dim(used_all, band, 0, keepdims=False)
            scale = jnp.where(used, tile + y * tiles, 2 * tiles)
            table = jnp.stack([block, tile, scale]).astype(jnp.int32)
            where = jnp.stack([band] + firsts).astype(jnp.int32)
            return table, where, parts[0], meta_at, parts, sizes, fields

        def with_fields(job, fields):
            return job[:-1] + (fields,)

        def job_at(shift, fields):
            parts, sizes, firsts = [], [], []
            for piece, across, (of, first, size, _) in zip(sent, crossed, pieces):
                if of == shift:
                    parts += [piece, across]
                    sizes += [size, size]
                    firsts += [x * each + first, (1 - x) * each + first]
            return job_of((me - shift) % nb, parts, sizes, firsts, fields)

        ours, others = [(0, keep)], [(1, theirs)]
        jobs = [job_of(me, [own_w], [cap], [jnp.int32(0)], ours)]
        rows_x = call(jobs, None, groups=2)
        for piece, (shift, _, _, _) in zip(packed[2:], pieces[2:]):
            piece, rows_x = lax.optimization_barrier((piece, rows_x))
            sent.append(lax.ppermute(piece, "band", along(shift)))
        crossed = [swap(piece, "var") for piece in sent]
        jobs += [job_at(shift, ours) for shift in order]
        rows_x = call(
            jobs[1:-1] + [with_fields(job, others) for job in jobs[:-1]], rows_x, groups=2
        )
        sent = call(
            [with_fields(jobs[-1], ours + others)],
            rows_x,
            groups=2,
            last=(embed_weight, embed_other, nv),
        )
        got = lax.all_to_all(sent, ("grp", "band", "var"), split_axis=0, concat_axis=0, tiled=True)
    else:
        embed_other = swap(embed_weight, "sub")
        both = jnp.concatenate([ocean_w, atmos_w], axis=1)
        fields = [(0, (jnp.concatenate([ocean_f, atmos_f], axis=0),))]
        ocean_block, ocean_used = slot_tables(ocean_dest, nb, cap)
        atmos_block, atmos_used = slot_tables(atmos_dest, nb, cap)
        block_all = jnp.concatenate([ocean_block, atmos_block + block_count], axis=1)
        used_all = jnp.concatenate([ocean_used, atmos_used], axis=1)
        grid_row = jnp.where(jnp.arange(slots) < cap, 0, tiles)

        def job_of(band, tile, meta, parts):
            block = lax.dynamic_index_in_dim(block_all, band, 0, keepdims=False)
            used = lax.dynamic_index_in_dim(used_all, band, 0, keepdims=False)
            scale = jnp.where(used, tile + grid_row, 2 * tiles)
            table = jnp.stack([block, tile, scale]).astype(jnp.int32)
            where = jnp.stack([band, jnp.int32(0)])
            return table, where, meta, 0, [parts], [slots], fields

        tile_ids = jnp.concatenate([ocean_ids, atmos_ids], axis=1)
        own_tile = lax.dynamic_index_in_dim(tile_ids, me, 0, keepdims=False)
        own_w = lax.dynamic_index_in_dim(both, me, 0, keepdims=False)
        rows_x = call([job_of(me, own_tile, land, own_w)], None, groups=1)
        share_rows = slots * cells // rep
        high = lax.reduce_precision(land, 8, 7)
        low = (land - high).astype(jnp.bfloat16)
        tile_rows = jnp.pad(tile_ids.astype(jnp.bfloat16), ((0, 0), (0, cells - slots)))
        for shift in order:
            target, band = (me + shift) % nb, (me - shift) % nb
            piece = lax.dynamic_slice(
                both, (target, quarter * share_rows, 0), (1, share_rows, cells)
            )[0]
            row = lax.dynamic_slice(tile_rows, (target, 0), (1, cells))
            row = jnp.broadcast_to(row, (16, cells))
            piece = jnp.concatenate([piece, high.astype(jnp.bfloat16), low, row], axis=0)
            parts = lax.all_gather(lax.ppermute(piece, "band", along(shift)), REPL, axis=0)
            meta = parts[0, share_rows:]
            tile = meta[2 * tiles, :slots].astype(jnp.int32)
            parts = parts[:, :share_rows].reshape(slots * cells, cells)
            rows_x = call([job_of(band, tile, meta, parts)], rows_x, groups=1)
        sent = embed(rows_x, embed_weight, embed_other, steps, nv)
        got = lax.all_to_all(sent, ("band", "var"), split_axis=0, concat_axis=0, tiled=True)
    shifted = jnp.sum(got.astype(jnp.float32), axis=0) + embed_bias
    inverse = lax.rsqrt(jnp.mean(shifted * shifted, axis=-1, keepdims=True) + 1e-05)
    finished = (shifted * inverse * embed_gain).astype(jnp.bfloat16)
    width = finished.shape[-1]
    finished = finished.reshape(nb, share, steps // nb, width).transpose(1, 0, 2, 3)
    return finished[None]


def solution(mesh):
    in_specs = (
        P(("grp", "band", "sub"), None, "var", None),
        P(("band", "sub"), None),
        P("band", "sub", None, None, None, None),
        P("band", "sub", None, None),
        P(("grp", "band", "sub"), None, "var", None),
        P(("band", "sub"), None),
        P("band", "sub", None, None, None, None),
        P("band", "sub", None, None),
        P("band", "sub", None, None, None),
        P(("var", "sub"), None),
        P(),
        P(),
    )
    out_specs = P("sub", "var", None, ("grp", "band"), None)
    return jax.shard_map(
        per_device, mesh=mesh, in_specs=in_specs, out_specs=out_specs, check_vma=False
    )
```

```python
import functools

import jax
import jax.numpy as jnp
from jax import lax
from jax.experimental import pallas as pl
from jax.experimental.pallas import tpu as pltpu
from jax.sharding import PartitionSpec as P

REPL = ("grp", "var")


def slot_tables(dest, band_count, cap):
    count = dest.shape[0]
    serial = jnp.arange(count, dtype=jnp.int32)
    band_of = dest[:, 0]
    earlier = (band_of[:, None] == band_of[None, :]) & (serial[None, :] < serial[:, None])
    position = jnp.sum(earlier.astype(jnp.int32), axis=1)
    slot = band_of * cap + position
    hit = slot[None, :] == jnp.arange(band_count * cap, dtype=jnp.int32)[:, None]
    block = jnp.sum(jnp.where(hit, serial[None, :], 0), axis=1)
    used = jnp.any(hit, axis=1)
    return block.reshape(band_count, cap), used.reshape(band_count, cap)


def pack_kernel(pieces, moved, *refs):
    ocean_w, atmos_w = refs[:2]
    fields, held = refs[5 : 5 + 2 * moved], refs[5 + 2 * moved :]
    count = len(pieces) + moved
    stages, (ocean_ids, atmos_ids, land, sem) = held[:count], held[count:]
    me, bands = lax.axis_index("band"), ocean_w.shape[0]
    x, y = lax.axis_index("var"), lax.axis_index("grp")
    cells, tiles = land.shape[-1], land.shape[0]
    cap = ocean_ids.shape[-1]

    def loads(weights, other):
        found = []
        for at, (stage, (shift, first, size, split)) in enumerate(zip(stages, pieces)):
            start = first if split is None else x * split + first
            found.append(
                pltpu.make_async_copy(
                    weights.at[
                        lax.rem(me + shift, bands),
                        pl.ds(pl.multiple_of(start * cells, cells), size * cells),
                        :,
                    ],
                    stage.at[pl.ds(0, size * cells), :],
                    sem.at[at],
                )
            )
        if moved:
            found.append(pltpu.make_async_copy(fields[other], stages[-1], sem.at[count - 1]))
        return found

    @pl.when(y == 0)
    def _():
        for copy in loads(ocean_w, 1):
            copy.start()

    @pl.when(y == 1)
    def _():
        for copy in loads(atmos_w, 0):
            copy.start()

    tables = [
        pltpu.make_async_copy(source, target, sem.at[count + at])
        for at, (source, target) in enumerate(zip(refs[2:5], (ocean_ids, atmos_ids, land)))
    ]
    for copy in tables:
        copy.start()
    for copy in tables:
        copy.wait()
    fraction = land[...]
    high = fraction.astype(jnp.bfloat16)
    low = (fraction - high.astype(jnp.float32)).astype(jnp.bfloat16)
    for stage, (shift, first, size, split) in zip(stages, pieces):
        if first:
            continue
        target, base = lax.rem(me + shift, bands), size * cells
        stage[pl.ds(base, tiles), :] = high
        stage[pl.ds(base + tiles, tiles), :] = low
        row = jnp.where(y == 0, ocean_ids[pl.ds(target, 1), :], atmos_ids[pl.ds(target, 1), :])
        row = jnp.broadcast_to(row.astype(jnp.float32), (16, cap)).astype(jnp.bfloat16)
        stage[pl.ds(base + 2 * tiles, 16), :] = jnp.zeros((16, cells), jnp.bfloat16)
        stage[pl.ds(base + 2 * tiles, 16), pl.ds(0, cap)] = row
    for load in loads(ocean_w, 1):
        load.wait()


def pack(limit, pieces, ocean_w, atmos_w, ocean_ids, atmos_ids, land, *fields):
    cells, tiles = land.shape[-1], land.shape[0]
    any_spec = pl.BlockSpec(memory_space=pl.ANY)
    vmem = pl.BlockSpec(memory_space=pltpu.VMEM)
    sizes = [size * cells + (0 if first else 2 * tiles + 16) for _, first, size, _ in pieces]
    shapes = [(n, cells) for n in sizes] + [f.shape for f in fields[:1]]
    return pl.pallas_call(
        functools.partial(pack_kernel, pieces, len(fields) // 2),
        out_shape=[jax.ShapeDtypeStruct(shape, jnp.bfloat16) for shape in shapes],
        in_specs=[any_spec] * (5 + len(fields)),
        out_specs=[vmem] * len(shapes),
        scratch_shapes=[pltpu.VMEM(a.shape, a.dtype) for a in (ocean_ids, atmos_ids, land)]
        + [pltpu.SemaphoreType.DMA((len(shapes) + 3,))],
        cost_estimate=pl.CostEstimate(flops=0, bytes_accessed=2 << 20, transcendentals=0),
        compiler_params=pltpu.CompilerParams(vmem_limit_bytes=limit << 20),
    )(ocean_w, atmos_w, ocean_ids, atmos_ids, land, *fields)


def run_jobs(steps, jobs, refs, out, acc, scale):
    local_rows, cells = acc.shape[1] // (scale.shape[0] // 2 - 4), acc.shape[2]
    tiles = acc.shape[1] // local_rows
    local_vars = local_rows // steps
    half_vars = local_vars // 2
    for table, where, meta, meta_at, parts, groups in jobs:
        table, where, meta = refs[table], refs[where], refs[meta]
        if meta.dtype == jnp.float32:
            land = meta[...]
        else:
            high = meta[pl.ds(meta_at, tiles), :].astype(jnp.float32)
            land = high + meta[pl.ds(meta_at + tiles, tiles), :].astype(jnp.float32)
        scale[pl.ds(0, tiles), :] = 1.0 - land
        scale[pl.ds(tiles, tiles), :] = land
        scale[pl.ds(2 * tiles, 8), :] = jnp.zeros((8, cells), jnp.float32)
        acc[pl.ds(0, len(groups))] = jnp.zeros((len(groups),) + acc.shape[1:], jnp.float32)
        for at, (part, size) in enumerate(parts):
            first = where[1 + at]
            for s in range(size):
                slot = first + s
                block = table[0, slot]
                moved = []
                for _, fields in groups:
                    piece = refs[fields[0]][block]
                    if len(fields) > 1:
                        piece = jnp.where(
                            lax.axis_index("grp") == 0, piece, refs[fields[1]][block]
                        )
                    moved.append(piece)
                moved = moved[0] if len(moved) == 1 else jnp.concatenate(moved, axis=0)
                dense = jnp.dot(
                    moved,
                    refs[part][pl.ds(s * cells, cells), :],
                    preferred_element_type=jnp.float32,
                )
                dense = dense * scale[pl.ds(table[2, slot], 1), :]
                span = pl.ds(pl.multiple_of(table[1, slot] * local_rows, local_rows), local_rows)
                for g in range(len(groups)):
                    acc[g, span, :] += dense[g * local_rows : (g + 1) * local_rows]
        for g, (to, _) in enumerate(groups):
            for v in range(local_vars):
                for q in range(2):
                    column = (v % half_vars * 2 + q) * cells
                    rows = [
                        acc[g, pl.ds(q * local_rows + t * local_vars + v, tiles // 2, 2 * local_rows), :]
                        for t in range(steps)
                    ]
                    out[where[0], to, v // half_vars, :, pl.ds(column, cells)] = jnp.concatenate(
                        rows, axis=0
                    ).astype(out.dtype)


def regrid_kernel(steps, jobs, *refs):
    run_jobs(steps, jobs, refs, *refs[-3:])


def finish_kernel(steps, halves, jobs, count, *refs):
    mine, theirs, rows_x, out, acc, scale, weight, total, sem = refs[count:]
    sub, mine_group = lax.axis_index("sub"), lax.axis_index("grp")
    chunks = sem.shape[0]
    height = mine.shape[0] // chunks

    def copy(chunk):
        span = pl.ds(pl.multiple_of(chunk * height, height), height)
        return pltpu.make_async_copy(theirs.at[span, :], weight.at[span, :], sem.at[chunk])

    for chunk in range(chunks):
        copy(chunk).start()
    run_jobs(steps, jobs, refs, rows_x, acc, scale)
    total[...] = jnp.zeros_like(total)

    @pl.loop(0, chunks)
    def _(chunk):
        span = pl.ds(pl.multiple_of(chunk * height, height), height)
        left, right = (
            rows_x[:, :, place, :, span].reshape(total.shape[0], height) for place in (sub, 1 - sub)
        )
        copy(chunk).wait()
        total[...] += jnp.dot(
            left, mine[span, :], preferred_element_type=jnp.float32
        ) + jnp.dot(right, weight[span, :], preferred_element_type=jnp.float32)

    send_rows(steps, halves, rows_x.shape, mine_group, total, out)


def send_rows(steps, halves, shape, mine_group, total, out):
    bands, groups, _, row_count, _ = shape
    count = steps * halves
    share = row_count // count
    for g in range(groups):
        base = (mine_group if g == 0 else 1 - mine_group) * count if groups > 1 else 0
        for chunk in range(count):
            pieces = [
                total[pl.ds((b * groups + g) * row_count + chunk * share, share), :]
                for b in range(bands)
            ]
            out[base + chunk] = jnp.concatenate(pieces, axis=0).astype(out.dtype)


def regrid(jobs, previous, bands, groups, steps, tiles, rows, cells, last=None):
    operands, specs, places = [], [], {}

    def place(array, space):
        if id(array) not in places:
            places[id(array)] = len(operands)
            operands.append(array)
            specs.append(pl.BlockSpec(memory_space=space))
        return places[id(array)]

    listed, flops, most = [], 0, 1
    for table, where, meta, meta_at, parts, sizes, fields in jobs:
        listed.append(
            (
                place(table, pltpu.SMEM),
                place(where, pltpu.SMEM),
                place(meta, pltpu.VMEM),
                meta_at,
                [(place(part, pltpu.VMEM), size) for part, size in zip(parts, sizes)],
                [(to, [place(f, pltpu.VMEM) for f in pair]) for to, pair in fields],
            )
        )
        flops += 2 * sum(sizes) * len(fields) * rows * cells * cells
        most = max(most, len(fields))
    aliases = {}
    vmem = pl.BlockSpec(memory_space=pltpu.VMEM)
    if previous is not None:
        aliases = {len(operands): 0}
        operands.append(previous)
        specs.append(vmem)
    shape = (bands, groups, 2, steps * tiles // 2, rows // steps // 2 * 2 * cells)
    shapes = [jax.ShapeDtypeStruct(shape, jnp.bfloat16)]
    scratch = [
        pltpu.VMEM((most, tiles * rows, cells), jnp.float32),
        pltpu.VMEM((2 * tiles + 8, cells), jnp.float32),
    ]
    if last is None:
        body = functools.partial(regrid_kernel, steps, listed)
        limit, moved = 12 << 20, len(jobs) * 3 << 20
    else:
        mine, theirs, halves = last
        height, width = mine.shape
        total = bands * groups * shape[3]
        body = functools.partial(finish_kernel, steps, halves, listed, len(operands))
        operands += [mine, theirs]
        specs += [vmem, pl.BlockSpec(memory_space=pl.ANY)]
        count = groups * steps * halves
        shapes.append(jax.ShapeDtypeStruct((count, total // count, width), jnp.bfloat16))
        scratch += [
            pltpu.VMEM((height, width), jnp.bfloat16),
            pltpu.VMEM((total, width), jnp.float32),
            pltpu.SemaphoreType.DMA((6,)),
        ]
        limit, moved = 24 << 20, 4 * height * width
        flops += 4 * total * height * width
    done = pl.pallas_call(
        body,
        out_shape=shapes,
        in_specs=specs,
        out_specs=[vmem] * len(shapes),
        scratch_shapes=scratch,
        input_output_aliases=aliases,
        cost_estimate=pl.CostEstimate(flops=flops, bytes_accessed=moved, transcendentals=0),
        compiler_params=pltpu.CompilerParams(vmem_limit_bytes=limit),
    )(*operands)
    return done[-1]


def embed_kernel(steps, halves, rows_x, mine, theirs, out, total):
    at = pl.program_id(0)
    sub, mine_group = lax.axis_index("sub"), lax.axis_index("grp")
    bands, groups, _, row_count, width = rows_x.shape
    rows = bands * groups * row_count

    @pl.when(at == 0)
    def _():
        total[...] = jnp.zeros_like(total)

    left = rows_x[:, :, sub].reshape(rows, width)
    right = rows_x[:, :, 1 - sub].reshape(rows, width)
    total[...] += jnp.dot(left, mine[...], preferred_element_type=jnp.float32) + jnp.dot(
        right, theirs[...], preferred_element_type=jnp.float32
    )

    @pl.when(at == pl.num_programs(0) - 1)
    def _():
        if out.ndim == 2:
            out[...] = total[...].astype(out.dtype)
        else:
            send_rows(steps, halves, rows_x.shape, mine_group, total, out)


def embed(rows_x, mine, theirs, steps, halves):
    bands, groups, _, row_count, half_width = rows_x.shape
    width = mine.shape[-1]
    grid = 6 if half_width % (6 * 256) == 0 else 3
    step_rows = half_width // grid
    rows = bands * groups * row_count
    chunks = groups * steps * halves
    share = row_count // (steps * halves)
    shape = (chunks, bands * share, width) if share % 4 == 0 else (rows, width)
    weight_spec = pl.BlockSpec((step_rows, width), lambda i: (i, 0))
    out = pl.pallas_call(
        functools.partial(embed_kernel, steps, halves),
        out_shape=jax.ShapeDtypeStruct(shape, jnp.bfloat16),
        grid=(grid,),
        in_specs=[
            pl.BlockSpec((bands, groups, 2, row_count, step_rows), lambda i: (0, 0, 0, 0, i)),
            weight_spec,
            weight_spec,
        ],
        out_specs=pl.BlockSpec(shape, lambda i: (0,) * len(shape)),
        scratch_shapes=[pltpu.VMEM((rows, width), jnp.float32)],
        cost_estimate=pl.CostEstimate(
            flops=4 * rows * mine.shape[0] * width,
            bytes_accessed=4 * mine.shape[0] * width,
            transcendentals=0,
        ),
        compiler_params=pltpu.CompilerParams(
            vmem_limit_bytes=(48 if rows > 1024 else 16) << 20
        ),
    )(rows_x, mine, theirs)
    if share % 4:
        out = out.reshape(bands, chunks, share, width).transpose(1, 0, 2, 3)
        out = out.reshape(chunks, bands * share, width)
    return out


def swap(x, axis):
    return lax.ppermute(x, axis, [(0, 1), (1, 0)])


def per_device(
    ocean_fields,
    ocean_dest,
    ocean_weights,
    ocean_tiles,
    atmos_fields,
    atmos_dest,
    atmos_weights,
    atmos_tiles,
    land_fraction,
    embed_weight,
    embed_bias,
    embed_gain,
):
    nb = lax.axis_size("band")
    nv = lax.axis_size("var")
    ng = lax.axis_size("grp")
    rep = nv * ng
    cap = ocean_weights.shape[3]
    cells = ocean_weights.shape[-1]
    block_count, steps, local_vars, _ = ocean_fields.shape
    patches = land_fraction.shape[2]
    tiles = 2 * patches
    slots = 2 * cap
    share = patches // nv
    me = lax.axis_index("band")
    x, y = lax.axis_index("var"), lax.axis_index("grp")
    quarter = y * nv + x

    flat = (nb, cap * cells, cells)
    ocean_w, atmos_w = ocean_weights.reshape(flat), atmos_weights.reshape(flat)
    ocean_ids, atmos_ids = ocean_tiles.reshape(nb, cap), atmos_tiles.reshape(nb, cap)
    land = land_fraction.reshape(tiles, cells)
    blocks = (block_count, steps * local_vars, cells)
    ocean_f, atmos_f = ocean_fields.reshape(blocks), atmos_fields.reshape(blocks)
    order = ([1, nb - 1] + list(range(2, nb - 1)))[: nb - 1]
    along = lambda shift: [(b, (b + shift) % nb) for b in range(nb)]
    call = functools.partial(
        regrid, bands=nb, steps=steps, tiles=tiles, rows=steps * local_vars, cells=cells
    )

    if ng == 2 and nv == 2 and cap % 2 == 0 and steps == nb:
        each = cap // 2
        pieces = []
        for shift in order:
            pieces.append((shift, 0, each, each))
        *packed, send = pack(
            60, pieces, ocean_w, atmos_w, ocean_ids, atmos_ids, land, ocean_f, atmos_f
        )
        sent = [
            lax.ppermute(piece, "band", along(shift))
            for piece, (shift, _, _, _) in zip(packed[:2], pieces)
        ]
        embed_other, own_land, send = lax.optimization_barrier((embed_weight, land, send))
        own_w = pack(54, [(0, 0, cap, None)], ocean_w, atmos_w, ocean_ids, atmos_ids, own_land)[0]
        embed_other = swap(embed_other, "sub")
        keep, theirs = (ocean_f, atmos_f), (swap(send, "grp"),)
        dest = jnp.where(y == 0, ocean_dest, atmos_dest)
        block_all, used_all = slot_tables(dest, nb, cap)
        def job_of(band, parts, sizes, firsts, fields):
            meta_at = sizes[0] * cells
            tile = parts[0][meta_at + 2 * tiles, :cap].astype(jnp.int32)
            block = lax.dynamic_index_in_dim(block_all, band, 0, keepdims=False)
            used = lax.dynamic_index_in_dim(used_all, band, 0, keepdims=False)
            scale = jnp.where(used, tile + y * tiles, 2 * tiles)
            table = jnp.stack([block, tile, scale]).astype(jnp.int32)
            where = jnp.stack([band] + firsts).astype(jnp.int32)
            return table, where, parts[0], meta_at, parts, sizes, fields

        def with_fields(job, fields):
            return job[:-1] + (fields,)

        def job_at(shift, fields):
            parts, sizes, firsts = [], [], []
            for piece, across, (of, first, size, _) in zip(sent, crossed, pieces):
                if of == shift:
                    parts += [piece, across]
                    sizes += [size, size]
                    firsts += [x * each + first, (1 - x) * each + first]
            return job_of((me - shift) % nb, parts, sizes, firsts, fields)

        ours, others = [(0, keep)], [(1, theirs)]
        jobs = [job_of(me, [own_w], [cap], [jnp.int32(0)], ours)]
        rows_x = call(jobs, None, groups=2)
        for piece, (shift, _, _, _) in zip(packed[2:], pieces[2:]):
            piece, rows_x = lax.optimization_barrier((piece, rows_x))
            sent.append(lax.ppermute(piece, "band", along(shift)))
        crossed = [swap(piece, "var") for piece in sent]
        jobs += [job_at(shift, ours) for shift in order]
        rows_x = call(
            jobs[1:-1] + [with_fields(job, others) for job in jobs[:-1]], rows_x, groups=2
        )
        sent = call(
            [with_fields(jobs[-1], ours + others)],
            rows_x,
            groups=2,
            last=(embed_weight, embed_other, nv),
        )
        got = lax.all_to_all(sent, ("grp", "band", "var"), split_axis=0, concat_axis=0, tiled=True)
    else:
        embed_other = swap(embed_weight, "sub")
        both = jnp.concatenate([ocean_w, atmos_w], axis=1)
        fields = [(0, (jnp.concatenate([ocean_f, atmos_f], axis=0),))]
        ocean_block, ocean_used = slot_tables(ocean_dest, nb, cap)
        atmos_block, atmos_used = slot_tables(atmos_dest, nb, cap)
        block_all = jnp.concatenate([ocean_block, atmos_block + block_count], axis=1)
        used_all = jnp.concatenate([ocean_used, atmos_used], axis=1)
        grid_row = jnp.where(jnp.arange(slots) < cap, 0, tiles)

        def job_of(band, tile, meta, parts):
            block = lax.dynamic_index_in_dim(block_all, band, 0, keepdims=False)
            used = lax.dynamic_index_in_dim(used_all, band, 0, keepdims=False)
            scale = jnp.where(used, tile + grid_row, 2 * tiles)
            table = jnp.stack([block, tile, scale]).astype(jnp.int32)
            where = jnp.stack([band, jnp.int32(0)])
            return table, where, meta, 0, [parts], [slots], fields

        tile_ids = jnp.concatenate([ocean_ids, atmos_ids], axis=1)
        own_tile = lax.dynamic_index_in_dim(tile_ids, me, 0, keepdims=False)
        own_w = lax.dynamic_index_in_dim(both, me, 0, keepdims=False)
        rows_x = call([job_of(me, own_tile, land, own_w)], None, groups=1)
        share_rows = slots * cells // rep
        high = lax.reduce_precision(land, 8, 7)
        low = (land - high).astype(jnp.bfloat16)
        tile_rows = jnp.pad(tile_ids.astype(jnp.bfloat16), ((0, 0), (0, cells - slots)))
        for shift in order:
            target, band = (me + shift) % nb, (me - shift) % nb
            piece = lax.dynamic_slice(
                both, (target, quarter * share_rows, 0), (1, share_rows, cells)
            )[0]
            row = lax.dynamic_slice(tile_rows, (target, 0), (1, cells))
            row = jnp.broadcast_to(row, (16, cells))
            piece = jnp.concatenate([piece, high.astype(jnp.bfloat16), low, row], axis=0)
            parts = lax.all_gather(lax.ppermute(piece, "band", along(shift)), REPL, axis=0)
            meta = parts[0, share_rows:]
            tile = meta[2 * tiles, :slots].astype(jnp.int32)
            parts = parts[:, :share_rows].reshape(slots * cells, cells)
            rows_x = call([job_of(band, tile, meta, parts)], rows_x, groups=1)
        sent = embed(rows_x, embed_weight, embed_other, steps, nv)
        got = lax.all_to_all(sent, ("band", "var"), split_axis=0, concat_axis=0, tiled=True)
    shifted = jnp.sum(got.astype(jnp.float32), axis=0) + embed_bias
    inverse = lax.rsqrt(jnp.mean(shifted * shifted, axis=-1, keepdims=True) + 1e-05)
    finished = (shifted * inverse * embed_gain).astype(jnp.bfloat16)
    width = finished.shape[-1]
    finished = finished.reshape(nb, share, steps // nb, width).transpose(1, 0, 2, 3)
    return finished[None]


def solution(mesh):
    in_specs = (
        P(("grp", "band", "sub"), None, "var", None),
        P(("band", "sub"), None),
        P("band", "sub", None, None, None, None),
        P("band", "sub", None, None),
        P(("grp", "band", "sub"), None, "var", None),
        P(("band", "sub"), None),
        P("band", "sub", None, None, None, None),
        P("band", "sub", None, None),
        P("band", "sub", None, None, None),
        P(("var", "sub"), None),
        P(),
        P(),
    )
    out_specs = P("sub", "var", None, ("grp", "band"), None)
    return jax.shard_map(
        per_device, mesh=mesh, in_specs=in_specs, out_specs=out_specs, check_vma=False
    )
```

```python
import functools

import jax
import jax.numpy as jnp
from jax import lax
from jax.experimental import pallas as pl
from jax.experimental.pallas import tpu as pltpu
from jax.sharding import PartitionSpec as P

REPL = ("grp", "var")


def slot_tables(dest, band_count, cap):
    count = dest.shape[0]
    serial = jnp.arange(count, dtype=jnp.int32)
    band_of = dest[:, 0]
    earlier = (band_of[:, None] == band_of[None, :]) & (serial[None, :] < serial[:, None])
    position = jnp.sum(earlier.astype(jnp.int32), axis=1)
    slot = band_of * cap + position
    hit = slot[None, :] == jnp.arange(band_count * cap, dtype=jnp.int32)[:, None]
    block = jnp.sum(jnp.where(hit, serial[None, :], 0), axis=1)
    used = jnp.any(hit, axis=1)
    return block.reshape(band_count, cap), used.reshape(band_count, cap)


def pack_kernel(pieces, moved, *refs):
    ocean_w, atmos_w = refs[:2]
    fields, held = refs[5 : 5 + 2 * moved], refs[5 + 2 * moved :]
    count = len(pieces) + moved
    stages, (ocean_ids, atmos_ids, land, sem) = held[:count], held[count:]
    me, bands = lax.axis_index("band"), ocean_w.shape[0]
    x, y = lax.axis_index("var"), lax.axis_index("grp")
    cells, tiles = land.shape[-1], land.shape[0]
    cap = ocean_ids.shape[-1]

    def loads(weights, other):
        found = []
        for at, (stage, (shift, first, size, split)) in enumerate(zip(stages, pieces)):
            start = first if split is None else x * split + first
            found.append(
                pltpu.make_async_copy(
                    weights.at[
                        lax.rem(me + shift, bands),
                        pl.ds(pl.multiple_of(start * cells, cells), size * cells),
                        :,
                    ],
                    stage.at[pl.ds(0, size * cells), :],
                    sem.at[at],
                )
            )
        if moved:
            found.append(pltpu.make_async_copy(fields[other], stages[-1], sem.at[count - 1]))
        return found

    @pl.when(y == 0)
    def _():
        for copy in loads(ocean_w, 1):
            copy.start()

    @pl.when(y == 1)
    def _():
        for copy in loads(atmos_w, 0):
            copy.start()

    tables = [
        pltpu.make_async_copy(source, target, sem.at[count + at])
        for at, (source, target) in enumerate(zip(refs[2:5], (ocean_ids, atmos_ids, land)))
    ]
    for copy in tables:
        copy.start()
    for copy in tables:
        copy.wait()
    fraction = land[...]
    high = fraction.astype(jnp.bfloat16)
    low = (fraction - high.astype(jnp.float32)).astype(jnp.bfloat16)
    for stage, (shift, first, size, split) in zip(stages, pieces):
        if first:
            continue
        target, base = lax.rem(me + shift, bands), size * cells
        stage[pl.ds(base, tiles), :] = high
        stage[pl.ds(base + tiles, tiles), :] = low
        row = jnp.where(y == 0, ocean_ids[pl.ds(target, 1), :], atmos_ids[pl.ds(target, 1), :])
        row = jnp.broadcast_to(row.astype(jnp.float32), (16, cap)).astype(jnp.bfloat16)
        stage[pl.ds(base + 2 * tiles, 16), :] = jnp.zeros((16, cells), jnp.bfloat16)
        stage[pl.ds(base + 2 * tiles, 16), pl.ds(0, cap)] = row
    for load in loads(ocean_w, 1):
        load.wait()


def pack(limit, pieces, ocean_w, atmos_w, ocean_ids, atmos_ids, land, *fields):
    cells, tiles = land.shape[-1], land.shape[0]
    any_spec = pl.BlockSpec(memory_space=pl.ANY)
    vmem = pl.BlockSpec(memory_space=pltpu.VMEM)
    sizes = [size * cells + (0 if first else 2 * tiles + 16) for _, first, size, _ in pieces]
    shapes = [(n, cells) for n in sizes] + [f.shape for f in fields[:1]]
    return pl.pallas_call(
        functools.partial(pack_kernel, pieces, len(fields) // 2),
        out_shape=[jax.ShapeDtypeStruct(shape, jnp.bfloat16) for shape in shapes],
        in_specs=[any_spec] * (5 + len(fields)),
        out_specs=[vmem] * len(shapes),
        scratch_shapes=[pltpu.VMEM(a.shape, a.dtype) for a in (ocean_ids, atmos_ids, land)]
        + [pltpu.SemaphoreType.DMA((len(shapes) + 3,))],
        cost_estimate=pl.CostEstimate(flops=0, bytes_accessed=2 << 20, transcendentals=0),
        compiler_params=pltpu.CompilerParams(vmem_limit_bytes=limit << 20),
    )(ocean_w, atmos_w, ocean_ids, atmos_ids, land, *fields)


def run_jobs(steps, jobs, refs, out, acc, scale):
    local_rows, cells = acc.shape[1] // (scale.shape[0] // 2 - 4), acc.shape[2]
    tiles = acc.shape[1] // local_rows
    local_vars = local_rows // steps
    half_vars = local_vars // 2
    for table, where, meta, meta_at, parts, groups in jobs:
        table, where, meta = refs[table], refs[where], refs[meta]
        if meta.dtype == jnp.float32:
            land = meta[...]
        else:
            high = meta[pl.ds(meta_at, tiles), :].astype(jnp.float32)
            land = high + meta[pl.ds(meta_at + tiles, tiles), :].astype(jnp.float32)
        scale[pl.ds(0, tiles), :] = 1.0 - land
        scale[pl.ds(tiles, tiles), :] = land
        scale[pl.ds(2 * tiles, 8), :] = jnp.zeros((8, cells), jnp.float32)
        acc[pl.ds(0, len(groups))] = jnp.zeros((len(groups),) + acc.shape[1:], jnp.float32)
        for at, (part, size) in enumerate(parts):
            first = where[1 + at]
            for s in range(size):
                slot = first + s
                block = table[0, slot]
                moved = []
                for _, fields in groups:
                    piece = refs[fields[0]][block]
                    if len(fields) > 1:
                        piece = jnp.where(
                            lax.axis_index("grp") == 0, piece, refs[fields[1]][block]
                        )
                    moved.append(piece)
                moved = moved[0] if len(moved) == 1 else jnp.concatenate(moved, axis=0)
                dense = jnp.dot(
                    moved,
                    refs[part][pl.ds(s * cells, cells), :],
                    preferred_element_type=jnp.float32,
                )
                dense = dense * scale[pl.ds(table[2, slot], 1), :]
                span = pl.ds(pl.multiple_of(table[1, slot] * local_rows, local_rows), local_rows)
                for g in range(len(groups)):
                    acc[g, span, :] += dense[g * local_rows : (g + 1) * local_rows]
        for g, (to, _) in enumerate(groups):
            for v in range(local_vars):
                for q in range(2):
                    column = (v % half_vars * 2 + q) * cells
                    rows = [
                        acc[g, pl.ds(q * local_rows + t * local_vars + v, tiles // 2, 2 * local_rows), :]
                        for t in range(steps)
                    ]
                    out[where[0], to, v // half_vars, :, pl.ds(column, cells)] = jnp.concatenate(
                        rows, axis=0
                    ).astype(out.dtype)


def regrid_kernel(steps, jobs, *refs):
    run_jobs(steps, jobs, refs, *refs[-3:])


def finish_kernel(steps, halves, jobs, count, *refs):
    mine, theirs, rows_x, out, acc, scale, weight, total, sem = refs[count:]
    sub, mine_group = lax.axis_index("sub"), lax.axis_index("grp")
    chunks = sem.shape[0]
    height = mine.shape[0] // chunks

    def copy(chunk):
        span = pl.ds(pl.multiple_of(chunk * height, height), height)
        return pltpu.make_async_copy(theirs.at[span, :], weight.at[span, :], sem.at[chunk])

    for chunk in range(chunks):
        copy(chunk).start()
    run_jobs(steps, jobs, refs, rows_x, acc, scale)
    total[...] = jnp.zeros_like(total)

    @pl.loop(0, chunks)
    def _(chunk):
        span = pl.ds(pl.multiple_of(chunk * height, height), height)
        left, right = (
            rows_x[:, :, place, :, span].reshape(total.shape[0], height) for place in (sub, 1 - sub)
        )
        copy(chunk).wait()
        total[...] += jnp.dot(
            left, mine[span, :], preferred_element_type=jnp.float32
        ) + jnp.dot(right, weight[span, :], preferred_element_type=jnp.float32)

    send_rows(steps, halves, rows_x.shape, mine_group, total, out)


def send_rows(steps, halves, shape, mine_group, total, out):
    bands, groups, _, row_count, _ = shape
    count = steps * halves
    share = row_count // count
    for g in range(groups):
        base = (mine_group if g == 0 else 1 - mine_group) * count if groups > 1 else 0
        for chunk in range(count):
            pieces = [
                total[pl.ds((b * groups + g) * row_count + chunk * share, share), :]
                for b in range(bands)
            ]
            out[base + chunk] = jnp.concatenate(pieces, axis=0).astype(out.dtype)


def regrid(jobs, previous, bands, groups, steps, tiles, rows, cells, last=None):
    operands, specs, places = [], [], {}

    def place(array, space):
        if id(array) not in places:
            places[id(array)] = len(operands)
            operands.append(array)
            specs.append(pl.BlockSpec(memory_space=space))
        return places[id(array)]

    listed, flops, most = [], 0, 1
    for table, where, meta, meta_at, parts, sizes, fields in jobs:
        listed.append(
            (
                place(table, pltpu.SMEM),
                place(where, pltpu.SMEM),
                place(meta, pltpu.VMEM),
                meta_at,
                [(place(part, pltpu.VMEM), size) for part, size in zip(parts, sizes)],
                [(to, [place(f, pltpu.VMEM) for f in pair]) for to, pair in fields],
            )
        )
        flops += 2 * sum(sizes) * len(fields) * rows * cells * cells
        most = max(most, len(fields))
    aliases = {}
    vmem = pl.BlockSpec(memory_space=pltpu.VMEM)
    if previous is not None:
        aliases = {len(operands): 0}
        operands.append(previous)
        specs.append(vmem)
    shape = (bands, groups, 2, steps * tiles // 2, rows // steps // 2 * 2 * cells)
    shapes = [jax.ShapeDtypeStruct(shape, jnp.bfloat16)]
    scratch = [
        pltpu.VMEM((most, tiles * rows, cells), jnp.float32),
        pltpu.VMEM((2 * tiles + 8, cells), jnp.float32),
    ]
    if last is None:
        body = functools.partial(regrid_kernel, steps, listed)
        limit, moved = 12 << 20, len(jobs) * 3 << 20
    else:
        mine, theirs, halves = last
        height, width = mine.shape
        total = bands * groups * shape[3]
        body = functools.partial(finish_kernel, steps, halves, listed, len(operands))
        operands += [mine, theirs]
        specs += [vmem, pl.BlockSpec(memory_space=pl.ANY)]
        count = groups * steps * halves
        shapes.append(jax.ShapeDtypeStruct((count, total // count, width), jnp.bfloat16))
        scratch += [
            pltpu.VMEM((height, width), jnp.bfloat16),
            pltpu.VMEM((total, width), jnp.float32),
            pltpu.SemaphoreType.DMA((6,)),
        ]
        limit, moved = 24 << 20, 4 * height * width
        flops += 4 * total * height * width
    done = pl.pallas_call(
        body,
        out_shape=shapes,
        in_specs=specs,
        out_specs=[vmem] * len(shapes),
        scratch_shapes=scratch,
        input_output_aliases=aliases,
        cost_estimate=pl.CostEstimate(flops=flops, bytes_accessed=moved, transcendentals=0),
        compiler_params=pltpu.CompilerParams(vmem_limit_bytes=limit),
    )(*operands)
    return done[-1]


def embed_kernel(steps, halves, rows_x, mine, theirs, out, total):
    at = pl.program_id(0)
    sub, mine_group = lax.axis_index("sub"), lax.axis_index("grp")
    bands, groups, _, row_count, width = rows_x.shape
    rows = bands * groups * row_count

    @pl.when(at == 0)
    def _():
        total[...] = jnp.zeros_like(total)

    left = rows_x[:, :, sub].reshape(rows, width)
    right = rows_x[:, :, 1 - sub].reshape(rows, width)
    total[...] += jnp.dot(left, mine[...], preferred_element_type=jnp.float32) + jnp.dot(
        right, theirs[...], preferred_element_type=jnp.float32
    )

    @pl.when(at == pl.num_programs(0) - 1)
    def _():
        if out.ndim == 2:
            out[...] = total[...].astype(out.dtype)
        else:
            send_rows(steps, halves, rows_x.shape, mine_group, total, out)


def embed(rows_x, mine, theirs, steps, halves):
    bands, groups, _, row_count, half_width = rows_x.shape
    width = mine.shape[-1]
    grid = 6 if half_width % (6 * 256) == 0 else 3
    step_rows = half_width // grid
    rows = bands * groups * row_count
    chunks = groups * steps * halves
    share = row_count // (steps * halves)
    shape = (chunks, bands * share, width) if share % 4 == 0 else (rows, width)
    weight_spec = pl.BlockSpec((step_rows, width), lambda i: (i, 0))
    out = pl.pallas_call(
        functools.partial(embed_kernel, steps, halves),
        out_shape=jax.ShapeDtypeStruct(shape, jnp.bfloat16),
        grid=(grid,),
        in_specs=[
            pl.BlockSpec((bands, groups, 2, row_count, step_rows), lambda i: (0, 0, 0, 0, i)),
            weight_spec,
            weight_spec,
        ],
        out_specs=pl.BlockSpec(shape, lambda i: (0,) * len(shape)),
        scratch_shapes=[pltpu.VMEM((rows, width), jnp.float32)],
        cost_estimate=pl.CostEstimate(
            flops=4 * rows * mine.shape[0] * width,
            bytes_accessed=4 * mine.shape[0] * width,
            transcendentals=0,
        ),
        compiler_params=pltpu.CompilerParams(
            vmem_limit_bytes=(48 if rows > 1024 else 16) << 20
        ),
    )(rows_x, mine, theirs)
    if share % 4:
        out = out.reshape(bands, chunks, share, width).transpose(1, 0, 2, 3)
        out = out.reshape(chunks, bands * share, width)
    return out


def swap(x, axis):
    return lax.ppermute(x, axis, [(0, 1), (1, 0)])


def per_device(
    ocean_fields,
    ocean_dest,
    ocean_weights,
    ocean_tiles,
    atmos_fields,
    atmos_dest,
    atmos_weights,
    atmos_tiles,
    land_fraction,
    embed_weight,
    embed_bias,
    embed_gain,
):
    nb = lax.axis_size("band")
    nv = lax.axis_size("var")
    ng = lax.axis_size("grp")
    rep = nv * ng
    cap = ocean_weights.shape[3]
    cells = ocean_weights.shape[-1]
    block_count, steps, local_vars, _ = ocean_fields.shape
    patches = land_fraction.shape[2]
    tiles = 2 * patches
    slots = 2 * cap
    share = patches // nv
    me = lax.axis_index("band")
    x, y = lax.axis_index("var"), lax.axis_index("grp")
    quarter = y * nv + x

    flat = (nb, cap * cells, cells)
    ocean_w, atmos_w = ocean_weights.reshape(flat), atmos_weights.reshape(flat)
    ocean_ids, atmos_ids = ocean_tiles.reshape(nb, cap), atmos_tiles.reshape(nb, cap)
    land = land_fraction.reshape(tiles, cells)
    blocks = (block_count, steps * local_vars, cells)
    ocean_f, atmos_f = ocean_fields.reshape(blocks), atmos_fields.reshape(blocks)
    order = ([1, nb - 1] + list(range(2, nb - 1)))[: nb - 1]
    along = lambda shift: [(b, (b + shift) % nb) for b in range(nb)]
    call = functools.partial(
        regrid, bands=nb, steps=steps, tiles=tiles, rows=steps * local_vars, cells=cells
    )

    if ng == 2 and nv == 2 and cap % 2 == 0 and steps == nb:
        each = cap // 2
        pieces = []
        for shift in order:
            pieces.append((shift, 0, each, each))
        *packed, send = pack(
            60, pieces, ocean_w, atmos_w, ocean_ids, atmos_ids, land, ocean_f, atmos_f
        )
        sent = [
            lax.ppermute(piece, "band", along(shift))
            for piece, (shift, _, _, _) in zip(packed[:2], pieces)
        ]
        embed_other, own_land, send = lax.optimization_barrier((embed_weight, land, send))
        own_w = pack(60, [(0, 0, cap, None)], ocean_w, atmos_w, ocean_ids, atmos_ids, own_land)[0]
        embed_other = swap(embed_other, "sub")
        keep, theirs = (ocean_f, atmos_f), (swap(send, "grp"),)
        dest = jnp.where(y == 0, ocean_dest, atmos_dest)
        block_all, used_all = slot_tables(dest, nb, cap)
        def job_of(band, parts, sizes, firsts, fields):
            meta_at = sizes[0] * cells
            tile = parts[0][meta_at + 2 * tiles, :cap].astype(jnp.int32)
            block = lax.dynamic_index_in_dim(block_all, band, 0, keepdims=False)
            used = lax.dynamic_index_in_dim(used_all, band, 0, keepdims=False)
            scale = jnp.where(used, tile + y * tiles, 2 * tiles)
            table = jnp.stack([block, tile, scale]).astype(jnp.int32)
            where = jnp.stack([band] + firsts).astype(jnp.int32)
            return table, where, parts[0], meta_at, parts, sizes, fields

        def with_fields(job, fields):
            return job[:-1] + (fields,)

        def job_at(shift, fields):
            parts, sizes, firsts = [], [], []
            for piece, across, (of, first, size, _) in zip(sent, crossed, pieces):
                if of == shift:
                    parts += [piece, across]
                    sizes += [size, size]
                    firsts += [x * each + first, (1 - x) * each + first]
            return job_of((me - shift) % nb, parts, sizes, firsts, fields)

        ours, others = [(0, keep)], [(1, theirs)]
        jobs = [job_of(me, [own_w], [cap], [jnp.int32(0)], ours)]
        rows_x = call(jobs, None, groups=2)
        for at, (piece, (shift, _, _, _)) in enumerate(zip(packed[2:], pieces[2:])):
            piece, sent[at], rows_x = lax.optimization_barrier((piece, sent[at], rows_x))
            sent.append(lax.ppermute(piece, "band", along(shift)))
        crossed = [swap(piece, "var") for piece in sent]
        jobs += [job_at(shift, ours) for shift in order]
        rows_x = call(
            jobs[1:-1] + [with_fields(job, others) for job in jobs[:-1]], rows_x, groups=2
        )
        sent = call(
            [with_fields(jobs[-1], ours + others)],
            rows_x,
            groups=2,
            last=(embed_weight, embed_other, nv),
        )
        got = lax.all_to_all(sent, ("grp", "band", "var"), split_axis=0, concat_axis=0, tiled=True)
    else:
        embed_other = swap(embed_weight, "sub")
        both = jnp.concatenate([ocean_w, atmos_w], axis=1)
        fields = [(0, (jnp.concatenate([ocean_f, atmos_f], axis=0),))]
        ocean_block, ocean_used = slot_tables(ocean_dest, nb, cap)
        atmos_block, atmos_used = slot_tables(atmos_dest, nb, cap)
        block_all = jnp.concatenate([ocean_block, atmos_block + block_count], axis=1)
        used_all = jnp.concatenate([ocean_used, atmos_used], axis=1)
        grid_row = jnp.where(jnp.arange(slots) < cap, 0, tiles)

        def job_of(band, tile, meta, parts):
            block = lax.dynamic_index_in_dim(block_all, band, 0, keepdims=False)
            used = lax.dynamic_index_in_dim(used_all, band, 0, keepdims=False)
            scale = jnp.where(used, tile + grid_row, 2 * tiles)
            table = jnp.stack([block, tile, scale]).astype(jnp.int32)
            where = jnp.stack([band, jnp.int32(0)])
            return table, where, meta, 0, [parts], [slots], fields

        tile_ids = jnp.concatenate([ocean_ids, atmos_ids], axis=1)
        own_tile = lax.dynamic_index_in_dim(tile_ids, me, 0, keepdims=False)
        own_w = lax.dynamic_index_in_dim(both, me, 0, keepdims=False)
        rows_x = call([job_of(me, own_tile, land, own_w)], None, groups=1)
        share_rows = slots * cells // rep
        high = lax.reduce_precision(land, 8, 7)
        low = (land - high).astype(jnp.bfloat16)
        tile_rows = jnp.pad(tile_ids.astype(jnp.bfloat16), ((0, 0), (0, cells - slots)))
        for shift in order:
            target, band = (me + shift) % nb, (me - shift) % nb
            piece = lax.dynamic_slice(
                both, (target, quarter * share_rows, 0), (1, share_rows, cells)
            )[0]
            row = lax.dynamic_slice(tile_rows, (target, 0), (1, cells))
            row = jnp.broadcast_to(row, (16, cells))
            piece = jnp.concatenate([piece, high.astype(jnp.bfloat16), low, row], axis=0)
            parts = lax.all_gather(lax.ppermute(piece, "band", along(shift)), REPL, axis=0)
            meta = parts[0, share_rows:]
            tile = meta[2 * tiles, :slots].astype(jnp.int32)
            parts = parts[:, :share_rows].reshape(slots * cells, cells)
            rows_x = call([job_of(band, tile, meta, parts)], rows_x, groups=1)
        sent = embed(rows_x, embed_weight, embed_other, steps, nv)
        got = lax.all_to_all(sent, ("band", "var"), split_axis=0, concat_axis=0, tiled=True)
    shifted = jnp.sum(got.astype(jnp.float32), axis=0) + embed_bias
    inverse = lax.rsqrt(jnp.mean(shifted * shifted, axis=-1, keepdims=True) + 1e-05)
    finished = (shifted * inverse * embed_gain).astype(jnp.bfloat16)
    width = finished.shape[-1]
    finished = finished.reshape(nb, share, steps // nb, width).transpose(1, 0, 2, 3)
    return finished[None]


def solution(mesh):
    in_specs = (
        P(("grp", "band", "sub"), None, "var", None),
        P(("band", "sub"), None),
        P("band", "sub", None, None, None, None),
        P("band", "sub", None, None),
        P(("grp", "band", "sub"), None, "var", None),
        P(("band", "sub"), None),
        P("band", "sub", None, None, None, None),
        P("band", "sub", None, None),
        P("band", "sub", None, None, None),
        P(("var", "sub"), None),
        P(),
        P(),
    )
    out_specs = P("sub", "var", None, ("grp", "band"), None)
    return jax.shard_map(
        per_device, mesh=mesh, in_specs=in_specs, out_specs=out_specs, check_vma=False
    )
```

```python
import functools

import jax
import jax.numpy as jnp
from jax import lax
from jax.experimental import pallas as pl
from jax.experimental.pallas import tpu as pltpu
from jax.sharding import PartitionSpec as P

REPL = ("grp", "var")


def slot_tables(dest, band_count, cap):
    count = dest.shape[0]
    serial = jnp.arange(count, dtype=jnp.int32)
    band_of = dest[:, 0]
    earlier = (band_of[:, None] == band_of[None, :]) & (serial[None, :] < serial[:, None])
    position = jnp.sum(earlier.astype(jnp.int32), axis=1)
    slot = band_of * cap + position
    hit = slot[None, :] == jnp.arange(band_count * cap, dtype=jnp.int32)[:, None]
    block = jnp.sum(jnp.where(hit, serial[None, :], 0), axis=1)
    used = jnp.any(hit, axis=1)
    return block.reshape(band_count, cap), used.reshape(band_count, cap)


def pack_kernel(pieces, moved, *refs):
    ocean_w, atmos_w = refs[:2]
    fields, held = refs[5 : 5 + 2 * moved], refs[5 + 2 * moved :]
    count = len(pieces) + moved
    stages, (ocean_ids, atmos_ids, land, sem) = held[:count], held[count:]
    me, bands = lax.axis_index("band"), ocean_w.shape[0]
    x, y = lax.axis_index("var"), lax.axis_index("grp")
    cells, tiles = land.shape[-1], land.shape[0]
    cap = ocean_ids.shape[-1]

    def loads(weights, other):
        found = []
        for at, (stage, (shift, first, size, split)) in enumerate(zip(stages, pieces)):
            start = first if split is None else x * split + first
            found.append(
                pltpu.make_async_copy(
                    weights.at[
                        lax.rem(me + shift, bands),
                        pl.ds(pl.multiple_of(start * cells, cells), size * cells),
                        :,
                    ],
                    stage.at[pl.ds(0, size * cells), :],
                    sem.at[at],
                )
            )
        if moved:
            found.append(pltpu.make_async_copy(fields[other], stages[-1], sem.at[count - 1]))
        return found

    @pl.when(y == 0)
    def _():
        for copy in loads(ocean_w, 1):
            copy.start()

    @pl.when(y == 1)
    def _():
        for copy in loads(atmos_w, 0):
            copy.start()

    tables = [
        pltpu.make_async_copy(source, target, sem.at[count + at])
        for at, (source, target) in enumerate(zip(refs[2:5], (ocean_ids, atmos_ids, land)))
    ]
    for copy in tables:
        copy.start()
    for copy in tables:
        copy.wait()
    fraction = land[...]
    high = fraction.astype(jnp.bfloat16)
    low = (fraction - high.astype(jnp.float32)).astype(jnp.bfloat16)
    for stage, (shift, first, size, split) in zip(stages, pieces):
        if first:
            continue
        target, base = lax.rem(me + shift, bands), size * cells
        stage[pl.ds(base, tiles), :] = high
        stage[pl.ds(base + tiles, tiles), :] = low
        row = jnp.where(y == 0, ocean_ids[pl.ds(target, 1), :], atmos_ids[pl.ds(target, 1), :])
        row = jnp.broadcast_to(row.astype(jnp.float32), (16, cap)).astype(jnp.bfloat16)
        stage[pl.ds(base + 2 * tiles, 16), :] = jnp.zeros((16, cells), jnp.bfloat16)
        stage[pl.ds(base + 2 * tiles, 16), pl.ds(0, cap)] = row
    for load in loads(ocean_w, 1):
        load.wait()


def pack(limit, pieces, ocean_w, atmos_w, ocean_ids, atmos_ids, land, *fields):
    cells, tiles = land.shape[-1], land.shape[0]
    any_spec = pl.BlockSpec(memory_space=pl.ANY)
    vmem = pl.BlockSpec(memory_space=pltpu.VMEM)
    sizes = [size * cells + (0 if first else 2 * tiles + 16) for _, first, size, _ in pieces]
    shapes = [(n, cells) for n in sizes] + [f.shape for f in fields[:1]]
    return pl.pallas_call(
        functools.partial(pack_kernel, pieces, len(fields) // 2),
        out_shape=[jax.ShapeDtypeStruct(shape, jnp.bfloat16) for shape in shapes],
        in_specs=[any_spec] * (5 + len(fields)),
        out_specs=[vmem] * len(shapes),
        scratch_shapes=[pltpu.VMEM(a.shape, a.dtype) for a in (ocean_ids, atmos_ids, land)]
        + [pltpu.SemaphoreType.DMA((len(shapes) + 3,))],
        cost_estimate=pl.CostEstimate(flops=0, bytes_accessed=2 << 20, transcendentals=0),
        compiler_params=pltpu.CompilerParams(vmem_limit_bytes=limit << 20),
    )(ocean_w, atmos_w, ocean_ids, atmos_ids, land, *fields)


def run_jobs(steps, jobs, refs, out, acc, scale):
    local_rows, cells = acc.shape[1] // (scale.shape[0] // 2 - 4), acc.shape[2]
    tiles = acc.shape[1] // local_rows
    local_vars = local_rows // steps
    half_vars = local_vars // 2
    for table, where, meta, meta_at, parts, groups in jobs:
        table, where, meta = refs[table], refs[where], refs[meta]
        if meta.dtype == jnp.float32:
            land = meta[...]
        else:
            high = meta[pl.ds(meta_at, tiles), :].astype(jnp.float32)
            land = high + meta[pl.ds(meta_at + tiles, tiles), :].astype(jnp.float32)
        scale[pl.ds(0, tiles), :] = 1.0 - land
        scale[pl.ds(tiles, tiles), :] = land
        scale[pl.ds(2 * tiles, 8), :] = jnp.zeros((8, cells), jnp.float32)
        acc[pl.ds(0, len(groups))] = jnp.zeros((len(groups),) + acc.shape[1:], jnp.float32)
        for at, (part, size) in enumerate(parts):
            first = where[1 + at]
            for s in range(size):
                slot = first + s
                block = table[0, slot]
                moved = []
                for _, fields in groups:
                    piece = refs[fields[0]][block]
                    if len(fields) > 1:
                        piece = jnp.where(
                            lax.axis_index("grp") == 0, piece, refs[fields[1]][block]
                        )
                    moved.append(piece)
                moved = moved[0] if len(moved) == 1 else jnp.concatenate(moved, axis=0)
                dense = jnp.dot(
                    moved,
                    refs[part][pl.ds(s * cells, cells), :],
                    preferred_element_type=jnp.float32,
                )
                dense = dense * scale[pl.ds(table[2, slot], 1), :]
                span = pl.ds(pl.multiple_of(table[1, slot] * local_rows, local_rows), local_rows)
                for g in range(len(groups)):
                    acc[g, span, :] += dense[g * local_rows : (g + 1) * local_rows]
        for g, (to, _) in enumerate(groups):
            for v in range(local_vars):
                for q in range(2):
                    column = (v % half_vars * 2 + q) * cells
                    rows = [
                        acc[g, pl.ds(q * local_rows + t * local_vars + v, tiles // 2, 2 * local_rows), :]
                        for t in range(steps)
                    ]
                    out[where[0], to, v // half_vars, :, pl.ds(column, cells)] = jnp.concatenate(
                        rows, axis=0
                    ).astype(out.dtype)


def regrid_kernel(steps, jobs, *refs):
    run_jobs(steps, jobs, refs, *refs[-3:])


def finish_kernel(steps, halves, jobs, count, *refs):
    mine, theirs, rows_x, out, acc, scale, weight, total, sem = refs[count:]
    sub, mine_group = lax.axis_index("sub"), lax.axis_index("grp")
    chunks = sem.shape[0]
    height = mine.shape[0] // chunks

    def copy(chunk):
        span = pl.ds(pl.multiple_of(chunk * height, height), height)
        return pltpu.make_async_copy(theirs.at[span, :], weight.at[span, :], sem.at[chunk])

    for chunk in range(chunks):
        copy(chunk).start()
    run_jobs(steps, jobs, refs, rows_x, acc, scale)
    total[...] = jnp.zeros_like(total)

    @pl.loop(0, chunks)
    def _(chunk):
        span = pl.ds(pl.multiple_of(chunk * height, height), height)
        left, right = (
            rows_x[:, :, place, :, span].reshape(total.shape[0], height) for place in (sub, 1 - sub)
        )
        copy(chunk).wait()
        total[...] += jnp.dot(
            left, mine[span, :], preferred_element_type=jnp.float32
        ) + jnp.dot(right, weight[span, :], preferred_element_type=jnp.float32)

    send_rows(steps, halves, rows_x.shape, mine_group, total, out)


def send_rows(steps, halves, shape, mine_group, total, out):
    bands, groups, _, row_count, _ = shape
    count = steps * halves
    share = row_count // count
    for g in range(groups):
        base = (mine_group if g == 0 else 1 - mine_group) * count if groups > 1 else 0
        for chunk in range(count):
            pieces = [
                total[pl.ds((b * groups + g) * row_count + chunk * share, share), :]
                for b in range(bands)
            ]
            out[base + chunk] = jnp.concatenate(pieces, axis=0).astype(out.dtype)


def regrid(jobs, previous, bands, groups, steps, tiles, rows, cells, last=None):
    operands, specs, places = [], [], {}

    def place(array, space):
        if id(array) not in places:
            places[id(array)] = len(operands)
            operands.append(array)
            specs.append(pl.BlockSpec(memory_space=space))
        return places[id(array)]

    listed, flops, most = [], 0, 1
    for table, where, meta, meta_at, parts, sizes, fields in jobs:
        listed.append(
            (
                place(table, pltpu.SMEM),
                place(where, pltpu.SMEM),
                place(meta, pltpu.VMEM),
                meta_at,
                [(place(part, pltpu.VMEM), size) for part, size in zip(parts, sizes)],
                [(to, [place(f, pltpu.VMEM) for f in pair]) for to, pair in fields],
            )
        )
        flops += 2 * sum(sizes) * len(fields) * rows * cells * cells
        most = max(most, len(fields))
    aliases = {}
    vmem = pl.BlockSpec(memory_space=pltpu.VMEM)
    if previous is not None:
        aliases = {len(operands): 0}
        operands.append(previous)
        specs.append(vmem)
    shape = (bands, groups, 2, steps * tiles // 2, rows // steps // 2 * 2 * cells)
    shapes = [jax.ShapeDtypeStruct(shape, jnp.bfloat16)]
    scratch = [
        pltpu.VMEM((most, tiles * rows, cells), jnp.float32),
        pltpu.VMEM((2 * tiles + 8, cells), jnp.float32),
    ]
    if last is None:
        body = functools.partial(regrid_kernel, steps, listed)
        limit, moved = 12 << 20, len(jobs) * 3 << 20
    else:
        mine, theirs, halves = last
        height, width = mine.shape
        total = bands * groups * shape[3]
        body = functools.partial(finish_kernel, steps, halves, listed, len(operands))
        operands += [mine, theirs]
        specs += [vmem, pl.BlockSpec(memory_space=pl.ANY)]
        count = groups * steps * halves
        shapes.append(jax.ShapeDtypeStruct((count, total // count, width), jnp.bfloat16))
        scratch += [
            pltpu.VMEM((height, width), jnp.bfloat16),
            pltpu.VMEM((total, width), jnp.float32),
            pltpu.SemaphoreType.DMA((6,)),
        ]
        limit, moved = 24 << 20, 4 * height * width
        flops += 4 * total * height * width
    done = pl.pallas_call(
        body,
        out_shape=shapes,
        in_specs=specs,
        out_specs=[vmem] * len(shapes),
        scratch_shapes=scratch,
        input_output_aliases=aliases,
        cost_estimate=pl.CostEstimate(flops=flops, bytes_accessed=moved, transcendentals=0),
        compiler_params=pltpu.CompilerParams(vmem_limit_bytes=limit),
    )(*operands)
    return done[-1]


def embed_kernel(steps, halves, rows_x, mine, theirs, out, total):
    at = pl.program_id(0)
    sub, mine_group = lax.axis_index("sub"), lax.axis_index("grp")
    bands, groups, _, row_count, width = rows_x.shape
    rows = bands * groups * row_count

    @pl.when(at == 0)
    def _():
        total[...] = jnp.zeros_like(total)

    left = rows_x[:, :, sub].reshape(rows, width)
    right = rows_x[:, :, 1 - sub].reshape(rows, width)
    total[...] += jnp.dot(left, mine[...], preferred_element_type=jnp.float32) + jnp.dot(
        right, theirs[...], preferred_element_type=jnp.float32
    )

    @pl.when(at == pl.num_programs(0) - 1)
    def _():
        if out.ndim == 2:
            out[...] = total[...].astype(out.dtype)
        else:
            send_rows(steps, halves, rows_x.shape, mine_group, total, out)


def embed(rows_x, mine, theirs, steps, halves):
    bands, groups, _, row_count, half_width = rows_x.shape
    width = mine.shape[-1]
    grid = 6 if half_width % (6 * 256) == 0 else 3
    step_rows = half_width // grid
    rows = bands * groups * row_count
    chunks = groups * steps * halves
    share = row_count // (steps * halves)
    shape = (chunks, bands * share, width) if share % 4 == 0 else (rows, width)
    weight_spec = pl.BlockSpec((step_rows, width), lambda i: (i, 0))
    out = pl.pallas_call(
        functools.partial(embed_kernel, steps, halves),
        out_shape=jax.ShapeDtypeStruct(shape, jnp.bfloat16),
        grid=(grid,),
        in_specs=[
            pl.BlockSpec((bands, groups, 2, row_count, step_rows), lambda i: (0, 0, 0, 0, i)),
            weight_spec,
            weight_spec,
        ],
        out_specs=pl.BlockSpec(shape, lambda i: (0,) * len(shape)),
        scratch_shapes=[pltpu.VMEM((rows, width), jnp.float32)],
        cost_estimate=pl.CostEstimate(
            flops=4 * rows * mine.shape[0] * width,
            bytes_accessed=4 * mine.shape[0] * width,
            transcendentals=0,
        ),
        compiler_params=pltpu.CompilerParams(
            vmem_limit_bytes=(48 if rows > 1024 else 16) << 20
        ),
    )(rows_x, mine, theirs)
    if share % 4:
        out = out.reshape(bands, chunks, share, width).transpose(1, 0, 2, 3)
        out = out.reshape(chunks, bands * share, width)
    return out


def swap(x, axis):
    return lax.ppermute(x, axis, [(0, 1), (1, 0)])


def per_device(
    ocean_fields,
    ocean_dest,
    ocean_weights,
    ocean_tiles,
    atmos_fields,
    atmos_dest,
    atmos_weights,
    atmos_tiles,
    land_fraction,
    embed_weight,
    embed_bias,
    embed_gain,
):
    nb = lax.axis_size("band")
    nv = lax.axis_size("var")
    ng = lax.axis_size("grp")
    rep = nv * ng
    cap = ocean_weights.shape[3]
    cells = ocean_weights.shape[-1]
    block_count, steps, local_vars, _ = ocean_fields.shape
    patches = land_fraction.shape[2]
    tiles = 2 * patches
    slots = 2 * cap
    share = patches // nv
    me = lax.axis_index("band")
    x, y = lax.axis_index("var"), lax.axis_index("grp")
    quarter = y * nv + x

    flat = (nb, cap * cells, cells)
    ocean_w, atmos_w = ocean_weights.reshape(flat), atmos_weights.reshape(flat)
    ocean_ids, atmos_ids = ocean_tiles.reshape(nb, cap), atmos_tiles.reshape(nb, cap)
    land = land_fraction.reshape(tiles, cells)
    blocks = (block_count, steps * local_vars, cells)
    ocean_f, atmos_f = ocean_fields.reshape(blocks), atmos_fields.reshape(blocks)
    order = list(range(1, nb))
    along = lambda shift: [(b, (b + shift) % nb) for b in range(nb)]
    call = functools.partial(
        regrid, bands=nb, steps=steps, tiles=tiles, rows=steps * local_vars, cells=cells
    )

    if ng == 2 and nv == 2 and cap % 2 == 0 and steps == nb:
        each = cap // 2
        pieces = []
        for shift in order:
            pieces.append((shift, 0, each, each))
        *packed, send = pack(
            60, pieces, ocean_w, atmos_w, ocean_ids, atmos_ids, land, ocean_f, atmos_f
        )
        sent = [
            lax.ppermute(piece, "band", along(shift))
            for piece, (shift, _, _, _) in zip(packed[:2], pieces)
        ]
        embed_other, own_land, send = lax.optimization_barrier((embed_weight, land, send))
        own_w = pack(60, [(0, 0, cap, None)], ocean_w, atmos_w, ocean_ids, atmos_ids, own_land)[0]
        embed_other = swap(embed_other, "sub")
        keep, theirs = (ocean_f, atmos_f), (swap(send, "grp"),)
        dest = jnp.where(y == 0, ocean_dest, atmos_dest)
        block_all, used_all = slot_tables(dest, nb, cap)
        def job_of(band, parts, sizes, firsts, fields):
            meta_at = sizes[0] * cells
            tile = parts[0][meta_at + 2 * tiles, :cap].astype(jnp.int32)
            block = lax.dynamic_index_in_dim(block_all, band, 0, keepdims=False)
            used = lax.dynamic_index_in_dim(used_all, band, 0, keepdims=False)
            scale = jnp.where(used, tile + y * tiles, 2 * tiles)
            table = jnp.stack([block, tile, scale]).astype(jnp.int32)
            where = jnp.stack([band] + firsts).astype(jnp.int32)
            return table, where, parts[0], meta_at, parts, sizes, fields

        def with_fields(job, fields):
            return job[:-1] + (fields,)

        def job_at(shift, fields):
            parts, sizes, firsts = [], [], []
            for piece, across, (of, first, size, _) in zip(sent, crossed, pieces):
                if of == shift:
                    parts += [piece, across]
                    sizes += [size, size]
                    firsts += [x * each + first, (1 - x) * each + first]
            return job_of((me - shift) % nb, parts, sizes, firsts, fields)

        ours, others = [(0, keep)], [(1, theirs)]
        jobs = [job_of(me, [own_w], [cap], [jnp.int32(0)], ours)]
        rows_x = call(jobs, None, groups=2)
        for at, (piece, (shift, _, _, _)) in enumerate(zip(packed[2:], pieces[2:])):
            piece, sent[at], rows_x = lax.optimization_barrier((piece, sent[at], rows_x))
            sent.append(lax.ppermute(piece, "band", along(shift)))
        crossed = [swap(piece, "var") for piece in sent]
        jobs += [job_at(shift, ours) for shift in order]
        rows_x = call(
            jobs[1:-1] + [with_fields(job, others) for job in jobs[:-1]], rows_x, groups=2
        )
        sent = call(
            [with_fields(jobs[-1], ours + others)],
            rows_x,
            groups=2,
            last=(embed_weight, embed_other, nv),
        )
        got = lax.all_to_all(sent, ("grp", "band", "var"), split_axis=0, concat_axis=0, tiled=True)
    else:
        embed_other = swap(embed_weight, "sub")
        both = jnp.concatenate([ocean_w, atmos_w], axis=1)
        fields = [(0, (jnp.concatenate([ocean_f, atmos_f], axis=0),))]
        ocean_block, ocean_used = slot_tables(ocean_dest, nb, cap)
        atmos_block, atmos_used = slot_tables(atmos_dest, nb, cap)
        block_all = jnp.concatenate([ocean_block, atmos_block + block_count], axis=1)
        used_all = jnp.concatenate([ocean_used, atmos_used], axis=1)
        grid_row = jnp.where(jnp.arange(slots) < cap, 0, tiles)

        def job_of(band, tile, meta, parts):
            block = lax.dynamic_index_in_dim(block_all, band, 0, keepdims=False)
            used = lax.dynamic_index_in_dim(used_all, band, 0, keepdims=False)
            scale = jnp.where(used, tile + grid_row, 2 * tiles)
            table = jnp.stack([block, tile, scale]).astype(jnp.int32)
            where = jnp.stack([band, jnp.int32(0)])
            return table, where, meta, 0, [parts], [slots], fields

        tile_ids = jnp.concatenate([ocean_ids, atmos_ids], axis=1)
        own_tile = lax.dynamic_index_in_dim(tile_ids, me, 0, keepdims=False)
        own_w = lax.dynamic_index_in_dim(both, me, 0, keepdims=False)
        rows_x = call([job_of(me, own_tile, land, own_w)], None, groups=1)
        share_rows = slots * cells // rep
        high = lax.reduce_precision(land, 8, 7)
        low = (land - high).astype(jnp.bfloat16)
        tile_rows = jnp.pad(tile_ids.astype(jnp.bfloat16), ((0, 0), (0, cells - slots)))
        for shift in order:
            target, band = (me + shift) % nb, (me - shift) % nb
            piece = lax.dynamic_slice(
                both, (target, quarter * share_rows, 0), (1, share_rows, cells)
            )[0]
            row = lax.dynamic_slice(tile_rows, (target, 0), (1, cells))
            row = jnp.broadcast_to(row, (16, cells))
            piece = jnp.concatenate([piece, high.astype(jnp.bfloat16), low, row], axis=0)
            parts = lax.all_gather(lax.ppermute(piece, "band", along(shift)), REPL, axis=0)
            meta = parts[0, share_rows:]
            tile = meta[2 * tiles, :slots].astype(jnp.int32)
            parts = parts[:, :share_rows].reshape(slots * cells, cells)
            rows_x = call([job_of(band, tile, meta, parts)], rows_x, groups=1)
        sent = embed(rows_x, embed_weight, embed_other, steps, nv)
        got = lax.all_to_all(sent, ("band", "var"), split_axis=0, concat_axis=0, tiled=True)
    shifted = jnp.sum(got.astype(jnp.float32), axis=0) + embed_bias
    inverse = lax.rsqrt(jnp.mean(shifted * shifted, axis=-1, keepdims=True) + 1e-05)
    finished = (shifted * inverse * embed_gain).astype(jnp.bfloat16)
    width = finished.shape[-1]
    finished = finished.reshape(nb, share, steps // nb, width).transpose(1, 0, 2, 3)
    return finished[None]


def solution(mesh):
    in_specs = (
        P(("grp", "band", "sub"), None, "var", None),
        P(("band", "sub"), None),
        P("band", "sub", None, None, None, None),
        P("band", "sub", None, None),
        P(("grp", "band", "sub"), None, "var", None),
        P(("band", "sub"), None),
        P("band", "sub", None, None, None, None),
        P("band", "sub", None, None),
        P("band", "sub", None, None, None),
        P(("var", "sub"), None),
        P(),
        P(),
    )
    out_specs = P("sub", "var", None, ("grp", "band"), None)
    return jax.shard_map(
        per_device, mesh=mesh, in_specs=in_specs, out_specs=out_specs, check_vma=False
    )
```

```python
import functools

import jax
import jax.numpy as jnp
from jax import lax
from jax.experimental import pallas as pl
from jax.experimental.pallas import tpu as pltpu
from jax.sharding import PartitionSpec as P

REPL = ("grp", "var")


def slot_tables(dest, band_count, cap):
    count = dest.shape[0]
    serial = jnp.arange(count, dtype=jnp.int32)
    band_of = dest[:, 0]
    earlier = (band_of[:, None] == band_of[None, :]) & (serial[None, :] < serial[:, None])
    position = jnp.sum(earlier.astype(jnp.int32), axis=1)
    slot = band_of * cap + position
    hit = slot[None, :] == jnp.arange(band_count * cap, dtype=jnp.int32)[:, None]
    block = jnp.sum(jnp.where(hit, serial[None, :], 0), axis=1)
    used = jnp.any(hit, axis=1)
    return block.reshape(band_count, cap), used.reshape(band_count, cap)


def pack_kernel(pieces, moved, *refs):
    ocean_w, atmos_w = refs[:2]
    fields, held = refs[5 : 5 + 2 * moved], refs[5 + 2 * moved :]
    count = len(pieces) + moved
    stages, (ocean_ids, atmos_ids, land, sem) = held[:count], held[count:]
    me, bands = lax.axis_index("band"), ocean_w.shape[0]
    x, y = lax.axis_index("var"), lax.axis_index("grp")
    cells, tiles = land.shape[-1], land.shape[0]
    cap = ocean_ids.shape[-1]

    def loads(weights, other):
        found = []
        for at, (stage, (shift, first, size, split)) in enumerate(zip(stages, pieces)):
            start = first if split is None else x * split + first
            found.append(
                pltpu.make_async_copy(
                    weights.at[
                        lax.rem(me + shift, bands),
                        pl.ds(pl.multiple_of(start * cells, cells), size * cells),
                        :,
                    ],
                    stage.at[pl.ds(0, size * cells), :],
                    sem.at[at],
                )
            )
        if moved:
            found.append(pltpu.make_async_copy(fields[other], stages[-1], sem.at[count - 1]))
        return found

    @pl.when(y == 0)
    def _():
        for copy in loads(ocean_w, 1):
            copy.start()

    @pl.when(y == 1)
    def _():
        for copy in loads(atmos_w, 0):
            copy.start()

    tables = [
        pltpu.make_async_copy(source, target, sem.at[count + at])
        for at, (source, target) in enumerate(zip(refs[2:5], (ocean_ids, atmos_ids, land)))
    ]
    for copy in tables:
        copy.start()
    for copy in tables:
        copy.wait()
    fraction = land[...]
    high = fraction.astype(jnp.bfloat16)
    low = (fraction - high.astype(jnp.float32)).astype(jnp.bfloat16)
    for stage, (shift, first, size, split) in zip(stages, pieces):
        if first:
            continue
        target, base = lax.rem(me + shift, bands), size * cells
        stage[pl.ds(base, tiles), :] = high
        stage[pl.ds(base + tiles, tiles), :] = low
        row = jnp.where(y == 0, ocean_ids[pl.ds(target, 1), :], atmos_ids[pl.ds(target, 1), :])
        row = jnp.broadcast_to(row.astype(jnp.float32), (16, cap)).astype(jnp.bfloat16)
        stage[pl.ds(base + 2 * tiles, 16), :] = jnp.zeros((16, cells), jnp.bfloat16)
        stage[pl.ds(base + 2 * tiles, 16), pl.ds(0, cap)] = row
    for load in loads(ocean_w, 1):
        load.wait()


def pack(limit, pieces, ocean_w, atmos_w, ocean_ids, atmos_ids, land, *fields):
    cells, tiles = land.shape[-1], land.shape[0]
    any_spec = pl.BlockSpec(memory_space=pl.ANY)
    vmem = pl.BlockSpec(memory_space=pltpu.VMEM)
    sizes = [size * cells + (0 if first else 2 * tiles + 16) for _, first, size, _ in pieces]
    shapes = [(n, cells) for n in sizes] + [f.shape for f in fields[:1]]
    return pl.pallas_call(
        functools.partial(pack_kernel, pieces, len(fields) // 2),
        out_shape=[jax.ShapeDtypeStruct(shape, jnp.bfloat16) for shape in shapes],
        in_specs=[any_spec] * (5 + len(fields)),
        out_specs=[vmem] * len(shapes),
        scratch_shapes=[pltpu.VMEM(a.shape, a.dtype) for a in (ocean_ids, atmos_ids, land)]
        + [pltpu.SemaphoreType.DMA((len(shapes) + 3,))],
        cost_estimate=pl.CostEstimate(flops=0, bytes_accessed=2 << 20, transcendentals=0),
        compiler_params=pltpu.CompilerParams(vmem_limit_bytes=limit << 20),
    )(ocean_w, atmos_w, ocean_ids, atmos_ids, land, *fields)


def run_jobs(steps, jobs, refs, out, acc, scale):
    tiles, cells = scale.shape[0] // 2 - 4, acc.shape[2]
    stride = acc.shape[1] // (tiles // 2)
    local_rows = (stride - 8) // 2
    local_vars = local_rows // steps
    half_vars = local_vars // 2
    for table, where, meta, meta_at, parts, groups in jobs:
        table, where, meta = refs[table], refs[where], refs[meta]
        if meta.dtype == jnp.float32:
            land = meta[...]
        else:
            high = meta[pl.ds(meta_at, tiles), :].astype(jnp.float32)
            land = high + meta[pl.ds(meta_at + tiles, tiles), :].astype(jnp.float32)
        scale[pl.ds(0, tiles), :] = 1.0 - land
        scale[pl.ds(tiles, tiles), :] = land
        scale[pl.ds(2 * tiles, 8), :] = jnp.zeros((8, cells), jnp.float32)
        acc[pl.ds(0, len(groups))] = jnp.zeros((len(groups),) + acc.shape[1:], jnp.float32)
        for at, (part, size) in enumerate(parts):
            first = where[1 + at]
            for s in range(size):
                slot = first + s
                block = table[0, slot]
                moved = []
                for _, fields in groups:
                    piece = refs[fields[0]][block]
                    if len(fields) > 1:
                        piece = jnp.where(
                            lax.axis_index("grp") == 0, piece, refs[fields[1]][block]
                        )
                    moved.append(piece)
                moved = moved[0] if len(moved) == 1 else jnp.concatenate(moved, axis=0)
                dense = jnp.dot(
                    moved,
                    refs[part][pl.ds(s * cells, cells), :],
                    preferred_element_type=jnp.float32,
                )
                dense = dense * scale[pl.ds(table[2, slot], 1), :]
                tile = table[1, slot]
                start = lax.shift_right_logical(tile, 1) * stride + (tile & 1) * local_rows
                span = pl.ds(pl.multiple_of(start, 8), local_rows)
                for g in range(len(groups)):
                    acc[g, span, :] += dense[g * local_rows : (g + 1) * local_rows]
        for g, (to, _) in enumerate(groups):
            for v in range(local_vars):
                for q in range(2):
                    column = (v % half_vars * 2 + q) * cells
                    rows = [
                        acc[g, pl.ds(q * local_rows + t * local_vars + v, tiles // 2, stride), :]
                        for t in range(steps)
                    ]
                    out[where[0], to, v // half_vars, :, pl.ds(column, cells)] = jnp.concatenate(
                        rows, axis=0
                    ).astype(out.dtype)


def regrid_kernel(steps, jobs, *refs):
    run_jobs(steps, jobs, refs, *refs[-3:])


def finish_kernel(steps, halves, jobs, count, *refs):
    mine, theirs, rows_x, out, acc, scale, weight, total, sem = refs[count:]
    sub, mine_group = lax.axis_index("sub"), lax.axis_index("grp")
    chunks = sem.shape[0]
    height = mine.shape[0] // chunks

    def copy(chunk):
        span = pl.ds(pl.multiple_of(chunk * height, height), height)
        return pltpu.make_async_copy(theirs.at[span, :], weight.at[span, :], sem.at[chunk])

    for chunk in range(chunks):
        copy(chunk).start()
    run_jobs(steps, jobs, refs, rows_x, acc, scale)
    total[...] = jnp.zeros_like(total)

    @pl.loop(0, chunks)
    def _(chunk):
        span = pl.ds(pl.multiple_of(chunk * height, height), height)
        left, right = (
            rows_x[:, :, place, :, span].reshape(total.shape[0], height) for place in (sub, 1 - sub)
        )
        copy(chunk).wait()
        total[...] += jnp.dot(
            left, mine[span, :], preferred_element_type=jnp.float32
        ) + jnp.dot(right, weight[span, :], preferred_element_type=jnp.float32)

    send_rows(steps, halves, rows_x.shape, mine_group, total, out)


def send_rows(steps, halves, shape, mine_group, total, out):
    bands, groups, _, row_count, _ = shape
    count = steps * halves
    share = row_count // count
    for g in range(groups):
        base = (mine_group if g == 0 else 1 - mine_group) * count if groups > 1 else 0
        for chunk in range(count):
            pieces = [
                total[pl.ds((b * groups + g) * row_count + chunk * share, share), :]
                for b in range(bands)
            ]
            out[base + chunk] = jnp.concatenate(pieces, axis=0).astype(out.dtype)


def regrid(jobs, previous, bands, groups, steps, tiles, rows, cells, last=None):
    operands, specs, places = [], [], {}

    def place(array, space):
        if id(array) not in places:
            places[id(array)] = len(operands)
            operands.append(array)
            specs.append(pl.BlockSpec(memory_space=space))
        return places[id(array)]

    listed, flops, most = [], 0, 1
    for table, where, meta, meta_at, parts, sizes, fields in jobs:
        listed.append(
            (
                place(table, pltpu.SMEM),
                place(where, pltpu.SMEM),
                place(meta, pltpu.VMEM),
                meta_at,
                [(place(part, pltpu.VMEM), size) for part, size in zip(parts, sizes)],
                [(to, [place(f, pltpu.VMEM) for f in pair]) for to, pair in fields],
            )
        )
        flops += 2 * sum(sizes) * len(fields) * rows * cells * cells
        most = max(most, len(fields))
    aliases = {}
    vmem = pl.BlockSpec(memory_space=pltpu.VMEM)
    if previous is not None:
        aliases = {len(operands): 0}
        operands.append(previous)
        specs.append(vmem)
    shape = (bands, groups, 2, steps * tiles // 2, rows // steps // 2 * 2 * cells)
    shapes = [jax.ShapeDtypeStruct(shape, jnp.bfloat16)]
    scratch = [
        pltpu.VMEM((most, tiles // 2 * (2 * rows + 8), cells), jnp.float32),
        pltpu.VMEM((2 * tiles + 8, cells), jnp.float32),
    ]
    if last is None:
        body = functools.partial(regrid_kernel, steps, listed)
        limit, moved = 12 << 20, len(jobs) * 3 << 20
    else:
        mine, theirs, halves = last
        height, width = mine.shape
        total = bands * groups * shape[3]
        body = functools.partial(finish_kernel, steps, halves, listed, len(operands))
        operands += [mine, theirs]
        specs += [vmem, pl.BlockSpec(memory_space=pl.ANY)]
        count = groups * steps * halves
        shapes.append(jax.ShapeDtypeStruct((count, total // count, width), jnp.bfloat16))
        scratch += [
            pltpu.VMEM((height, width), jnp.bfloat16),
            pltpu.VMEM((total, width), jnp.float32),
            pltpu.SemaphoreType.DMA((6,)),
        ]
        limit, moved = 24 << 20, 4 * height * width
        flops += 4 * total * height * width
    done = pl.pallas_call(
        body,
        out_shape=shapes,
        in_specs=specs,
        out_specs=[vmem] * len(shapes),
        scratch_shapes=scratch,
        input_output_aliases=aliases,
        cost_estimate=pl.CostEstimate(flops=flops, bytes_accessed=moved, transcendentals=0),
        compiler_params=pltpu.CompilerParams(vmem_limit_bytes=limit),
    )(*operands)
    return done[-1]


def embed_kernel(steps, halves, rows_x, mine, theirs, out, total):
    at = pl.program_id(0)
    sub, mine_group = lax.axis_index("sub"), lax.axis_index("grp")
    bands, groups, _, row_count, width = rows_x.shape
    rows = bands * groups * row_count

    @pl.when(at == 0)
    def _():
        total[...] = jnp.zeros_like(total)

    left = rows_x[:, :, sub].reshape(rows, width)
    right = rows_x[:, :, 1 - sub].reshape(rows, width)
    total[...] += jnp.dot(left, mine[...], preferred_element_type=jnp.float32) + jnp.dot(
        right, theirs[...], preferred_element_type=jnp.float32
    )

    @pl.when(at == pl.num_programs(0) - 1)
    def _():
        if out.ndim == 2:
            out[...] = total[...].astype(out.dtype)
        else:
            send_rows(steps, halves, rows_x.shape, mine_group, total, out)


def embed(rows_x, mine, theirs, steps, halves):
    bands, groups, _, row_count, half_width = rows_x.shape
    width = mine.shape[-1]
    grid = 6 if half_width % (6 * 256) == 0 else 3
    step_rows = half_width // grid
    rows = bands * groups * row_count
    chunks = groups * steps * halves
    share = row_count // (steps * halves)
    shape = (chunks, bands * share, width) if share % 4 == 0 else (rows, width)
    weight_spec = pl.BlockSpec((step_rows, width), lambda i: (i, 0))
    out = pl.pallas_call(
        functools.partial(embed_kernel, steps, halves),
        out_shape=jax.ShapeDtypeStruct(shape, jnp.bfloat16),
        grid=(grid,),
        in_specs=[
            pl.BlockSpec((bands, groups, 2, row_count, step_rows), lambda i: (0, 0, 0, 0, i)),
            weight_spec,
            weight_spec,
        ],
        out_specs=pl.BlockSpec(shape, lambda i: (0,) * len(shape)),
        scratch_shapes=[pltpu.VMEM((rows, width), jnp.float32)],
        cost_estimate=pl.CostEstimate(
            flops=4 * rows * mine.shape[0] * width,
            bytes_accessed=4 * mine.shape[0] * width,
            transcendentals=0,
        ),
        compiler_params=pltpu.CompilerParams(
            vmem_limit_bytes=(48 if rows > 1024 else 16) << 20
        ),
    )(rows_x, mine, theirs)
    if share % 4:
        out = out.reshape(bands, chunks, share, width).transpose(1, 0, 2, 3)
        out = out.reshape(chunks, bands * share, width)
    return out


def swap(x, axis):
    return lax.ppermute(x, axis, [(0, 1), (1, 0)])


def per_device(
    ocean_fields,
    ocean_dest,
    ocean_weights,
    ocean_tiles,
    atmos_fields,
    atmos_dest,
    atmos_weights,
    atmos_tiles,
    land_fraction,
    embed_weight,
    embed_bias,
    embed_gain,
):
    nb = lax.axis_size("band")
    nv = lax.axis_size("var")
    ng = lax.axis_size("grp")
    rep = nv * ng
    cap = ocean_weights.shape[3]
    cells = ocean_weights.shape[-1]
    block_count, steps, local_vars, _ = ocean_fields.shape
    patches = land_fraction.shape[2]
    tiles = 2 * patches
    slots = 2 * cap
    share = patches // nv
    me = lax.axis_index("band")
    x, y = lax.axis_index("var"), lax.axis_index("grp")
    quarter = y * nv + x

    flat = (nb, cap * cells, cells)
    ocean_w, atmos_w = ocean_weights.reshape(flat), atmos_weights.reshape(flat)
    ocean_ids, atmos_ids = ocean_tiles.reshape(nb, cap), atmos_tiles.reshape(nb, cap)
    land = land_fraction.reshape(tiles, cells)
    blocks = (block_count, steps * local_vars, cells)
    ocean_f, atmos_f = ocean_fields.reshape(blocks), atmos_fields.reshape(blocks)
    order = ([1, nb - 1] + list(range(2, nb - 1)))[: nb - 1]
    along = lambda shift: [(b, (b + shift) % nb) for b in range(nb)]
    call = functools.partial(
        regrid, bands=nb, steps=steps, tiles=tiles, rows=steps * local_vars, cells=cells
    )

    if ng == 2 and nv == 2 and cap % 2 == 0 and steps == nb:
        each = cap // 2
        pieces = []
        for shift in order:
            pieces.append((shift, 0, each, each))
        *packed, send = pack(
            60, pieces, ocean_w, atmos_w, ocean_ids, atmos_ids, land, ocean_f, atmos_f
        )
        sent = [
            lax.ppermute(piece, "band", along(shift))
            for piece, (shift, _, _, _) in zip(packed[:2], pieces)
        ]
        embed_other, own_land, send = lax.optimization_barrier((embed_weight, land, send))
        own_w = pack(60, [(0, 0, cap, None)], ocean_w, atmos_w, ocean_ids, atmos_ids, own_land)[0]
        embed_other = swap(embed_other, "sub")
        keep, theirs = (ocean_f, atmos_f), (swap(send, "grp"),)
        dest = jnp.where(y == 0, ocean_dest, atmos_dest)
        block_all, used_all = slot_tables(dest, nb, cap)
        def job_of(band, parts, sizes, firsts, fields):
            meta_at = sizes[0] * cells
            tile = parts[0][meta_at + 2 * tiles, :cap].astype(jnp.int32)
            block = lax.dynamic_index_in_dim(block_all, band, 0, keepdims=False)
            used = lax.dynamic_index_in_dim(used_all, band, 0, keepdims=False)
            scale = jnp.where(used, tile + y * tiles, 2 * tiles)
            table = jnp.stack([block, tile, scale]).astype(jnp.int32)
            where = jnp.stack([band] + firsts).astype(jnp.int32)
            return table, where, parts[0], meta_at, parts, sizes, fields

        def with_fields(job, fields):
            return job[:-1] + (fields,)

        def job_at(shift, fields):
            parts, sizes, firsts = [], [], []
            for piece, across, (of, first, size, _) in zip(sent, crossed, pieces):
                if of == shift:
                    parts += [piece, across]
                    sizes += [size, size]
                    firsts += [x * each + first, (1 - x) * each + first]
            return job_of((me - shift) % nb, parts, sizes, firsts, fields)

        ours, others = [(0, keep)], [(1, theirs)]
        jobs = [job_of(me, [own_w], [cap], [jnp.int32(0)], ours)]
        rows_x = call(jobs, None, groups=2)
        for at, (piece, (shift, _, _, _)) in enumerate(zip(packed[2:], pieces[2:])):
            piece, sent[at], rows_x = lax.optimization_barrier((piece, sent[at], rows_x))
            sent.append(lax.ppermute(piece, "band", along(shift)))
        crossed = [swap(piece, "var") for piece in sent]
        jobs += [job_at(shift, ours) for shift in order]
        rows_x = call(
            jobs[1:-1] + [with_fields(job, others) for job in jobs[:-1]], rows_x, groups=2
        )
        sent = call(
            [with_fields(jobs[-1], ours + others)],
            rows_x,
            groups=2,
            last=(embed_weight, embed_other, nv),
        )
        got = lax.all_to_all(sent, ("grp", "band", "var"), split_axis=0, concat_axis=0, tiled=True)
    else:
        embed_other = swap(embed_weight, "sub")
        both = jnp.concatenate([ocean_w, atmos_w], axis=1)
        fields = [(0, (jnp.concatenate([ocean_f, atmos_f], axis=0),))]
        ocean_block, ocean_used = slot_tables(ocean_dest, nb, cap)
        atmos_block, atmos_used = slot_tables(atmos_dest, nb, cap)
        block_all = jnp.concatenate([ocean_block, atmos_block + block_count], axis=1)
        used_all = jnp.concatenate([ocean_used, atmos_used], axis=1)
        grid_row = jnp.where(jnp.arange(slots) < cap, 0, tiles)

        def job_of(band, tile, meta, parts):
            block = lax.dynamic_index_in_dim(block_all, band, 0, keepdims=False)
            used = lax.dynamic_index_in_dim(used_all, band, 0, keepdims=False)
            scale = jnp.where(used, tile + grid_row, 2 * tiles)
            table = jnp.stack([block, tile, scale]).astype(jnp.int32)
            where = jnp.stack([band, jnp.int32(0)])
            return table, where, meta, 0, [parts], [slots], fields

        tile_ids = jnp.concatenate([ocean_ids, atmos_ids], axis=1)
        own_tile = lax.dynamic_index_in_dim(tile_ids, me, 0, keepdims=False)
        own_w = lax.dynamic_index_in_dim(both, me, 0, keepdims=False)
        rows_x = call([job_of(me, own_tile, land, own_w)], None, groups=1)
        share_rows = slots * cells // rep
        high = lax.reduce_precision(land, 8, 7)
        low = (land - high).astype(jnp.bfloat16)
        tile_rows = jnp.pad(tile_ids.astype(jnp.bfloat16), ((0, 0), (0, cells - slots)))
        for shift in order:
            target, band = (me + shift) % nb, (me - shift) % nb
            piece = lax.dynamic_slice(
                both, (target, quarter * share_rows, 0), (1, share_rows, cells)
            )[0]
            row = lax.dynamic_slice(tile_rows, (target, 0), (1, cells))
            row = jnp.broadcast_to(row, (16, cells))
            piece = jnp.concatenate([piece, high.astype(jnp.bfloat16), low, row], axis=0)
            parts = lax.all_gather(lax.ppermute(piece, "band", along(shift)), REPL, axis=0)
            meta = parts[0, share_rows:]
            tile = meta[2 * tiles, :slots].astype(jnp.int32)
            parts = parts[:, :share_rows].reshape(slots * cells, cells)
            rows_x = call([job_of(band, tile, meta, parts)], rows_x, groups=1)
        sent = embed(rows_x, embed_weight, embed_other, steps, nv)
        got = lax.all_to_all(sent, ("band", "var"), split_axis=0, concat_axis=0, tiled=True)
    shifted = jnp.sum(got.astype(jnp.float32), axis=0) + embed_bias
    inverse = lax.rsqrt(jnp.mean(shifted * shifted, axis=-1, keepdims=True) + 1e-05)
    finished = (shifted * inverse * embed_gain).astype(jnp.bfloat16)
    width = finished.shape[-1]
    finished = finished.reshape(nb, share, steps // nb, width).transpose(1, 0, 2, 3)
    return finished[None]


def solution(mesh):
    in_specs = (
        P(("grp", "band", "sub"), None, "var", None),
        P(("band", "sub"), None),
        P("band", "sub", None, None, None, None),
        P("band", "sub", None, None),
        P(("grp", "band", "sub"), None, "var", None),
        P(("band", "sub"), None),
        P("band", "sub", None, None, None, None),
        P("band", "sub", None, None),
        P("band", "sub", None, None, None),
        P(("var", "sub"), None),
        P(),
        P(),
    )
    out_specs = P("sub", "var", None, ("grp", "band"), None)
    return jax.shard_map(
        per_device, mesh=mesh, in_specs=in_specs, out_specs=out_specs, check_vma=False
    )
```

```python
import functools

import jax
import jax.numpy as jnp
from jax import lax
from jax.experimental import pallas as pl
from jax.experimental.pallas import tpu as pltpu
from jax.sharding import PartitionSpec as P

REPL = ("grp", "var")


def slot_tables(dest, band_count, cap):
    count = dest.shape[0]
    serial = jnp.arange(count, dtype=jnp.int32)
    band_of = dest[:, 0]
    earlier = (band_of[:, None] == band_of[None, :]) & (serial[None, :] < serial[:, None])
    position = jnp.sum(earlier.astype(jnp.int32), axis=1)
    slot = band_of * cap + position
    hit = slot[None, :] == jnp.arange(band_count * cap, dtype=jnp.int32)[:, None]
    block = jnp.sum(jnp.where(hit, serial[None, :], 0), axis=1)
    used = jnp.any(hit, axis=1)
    return block.reshape(band_count, cap), used.reshape(band_count, cap)


def pack_kernel(pieces, moved, *refs):
    ocean_w, atmos_w = refs[:2]
    fields, held = refs[5 : 5 + 2 * moved], refs[5 + 2 * moved :]
    count = len(pieces) + moved
    stages, (ocean_ids, atmos_ids, land, sem) = held[:count], held[count:]
    me, bands = lax.axis_index("band"), ocean_w.shape[0]
    x, y = lax.axis_index("var"), lax.axis_index("grp")
    cells, tiles = land.shape[-1], land.shape[0]
    cap = ocean_ids.shape[-1]

    def loads(weights, other):
        found = []
        for at, (stage, (shift, first, size, split)) in enumerate(zip(stages, pieces)):
            start = first if split is None else x * split + first
            found.append(
                pltpu.make_async_copy(
                    weights.at[
                        lax.rem(me + shift, bands),
                        pl.ds(pl.multiple_of(start * cells, cells), size * cells),
                        :,
                    ],
                    stage.at[pl.ds(0, size * cells), :],
                    sem.at[at],
                )
            )
        if moved:
            found.append(pltpu.make_async_copy(fields[other], stages[-1], sem.at[count - 1]))
        return found

    @pl.when(y == 0)
    def _():
        for copy in loads(ocean_w, 1):
            copy.start()

    @pl.when(y == 1)
    def _():
        for copy in loads(atmos_w, 0):
            copy.start()

    tables = [
        pltpu.make_async_copy(source, target, sem.at[count + at])
        for at, (source, target) in enumerate(zip(refs[2:5], (ocean_ids, atmos_ids, land)))
    ]
    for copy in tables:
        copy.start()
    for copy in tables:
        copy.wait()
    fraction = land[...]
    high = fraction.astype(jnp.bfloat16)
    low = (fraction - high.astype(jnp.float32)).astype(jnp.bfloat16)
    for stage, (shift, first, size, split) in zip(stages, pieces):
        if first:
            continue
        target, base = lax.rem(me + shift, bands), size * cells
        stage[pl.ds(base, tiles), :] = high
        stage[pl.ds(base + tiles, tiles), :] = low
        row = jnp.where(y == 0, ocean_ids[pl.ds(target, 1), :], atmos_ids[pl.ds(target, 1), :])
        row = jnp.broadcast_to(row.astype(jnp.float32), (16, cap)).astype(jnp.bfloat16)
        stage[pl.ds(base + 2 * tiles, 16), :] = jnp.zeros((16, cells), jnp.bfloat16)
        stage[pl.ds(base + 2 * tiles, 16), pl.ds(0, cap)] = row
    for load in loads(ocean_w, 1):
        load.wait()


def pack(limit, pieces, ocean_w, atmos_w, ocean_ids, atmos_ids, land, *fields):
    cells, tiles = land.shape[-1], land.shape[0]
    any_spec = pl.BlockSpec(memory_space=pl.ANY)
    vmem = pl.BlockSpec(memory_space=pltpu.VMEM)
    sizes = [size * cells + (0 if first else 2 * tiles + 16) for _, first, size, _ in pieces]
    shapes = [(n, cells) for n in sizes] + [f.shape for f in fields[:1]]
    return pl.pallas_call(
        functools.partial(pack_kernel, pieces, len(fields) // 2),
        out_shape=[jax.ShapeDtypeStruct(shape, jnp.bfloat16) for shape in shapes],
        in_specs=[any_spec] * (5 + len(fields)),
        out_specs=[vmem] * len(shapes),
        scratch_shapes=[pltpu.VMEM(a.shape, a.dtype) for a in (ocean_ids, atmos_ids, land)]
        + [pltpu.SemaphoreType.DMA((len(shapes) + 3,))],
        cost_estimate=pl.CostEstimate(flops=0, bytes_accessed=2 << 20, transcendentals=0),
        compiler_params=pltpu.CompilerParams(vmem_limit_bytes=limit << 20),
    )(ocean_w, atmos_w, ocean_ids, atmos_ids, land, *fields)


def run_jobs(steps, jobs, refs, out, acc, scale):
    tiles, cells = scale.shape[0] // 2 - 4, acc.shape[2]
    stride = acc.shape[1] // (tiles // 2)
    local_rows = (stride - 8) // 2
    local_vars = local_rows // steps
    half_vars = local_vars // 2
    for table, where, meta, meta_at, parts, groups in jobs:
        table, where, meta = refs[table], refs[where], refs[meta]
        if meta.dtype == jnp.float32:
            land = meta[...]
        else:
            high = meta[pl.ds(meta_at, tiles), :].astype(jnp.float32)
            land = high + meta[pl.ds(meta_at + tiles, tiles), :].astype(jnp.float32)
        scale[pl.ds(0, tiles), :] = 1.0 - land
        scale[pl.ds(tiles, tiles), :] = land
        scale[pl.ds(2 * tiles, 8), :] = jnp.zeros((8, cells), jnp.float32)
        acc[pl.ds(0, len(groups))] = jnp.zeros((len(groups),) + acc.shape[1:], jnp.float32)
        for at, (part, size) in enumerate(parts):
            first = where[1 + at]
            for s in range(size):
                slot = first + s
                block = table[0, slot]
                moved = []
                for _, fields in groups:
                    piece = refs[fields[0]][block]
                    if len(fields) > 1:
                        piece = jnp.where(
                            lax.axis_index("grp") == 0, piece, refs[fields[1]][block]
                        )
                    moved.append(piece)
                moved = moved[0] if len(moved) == 1 else jnp.concatenate(moved, axis=0)
                dense = jnp.dot(
                    moved,
                    refs[part][pl.ds(s * cells, cells), :],
                    preferred_element_type=jnp.float32,
                )
                dense = dense * scale[pl.ds(table[2, slot], 1), :]
                tile = table[1, slot]
                start = lax.shift_right_logical(tile, 1) * stride + (tile & 1) * local_rows
                span = pl.ds(pl.multiple_of(start, 8), local_rows)
                for g in range(len(groups)):
                    acc[g, span, :] += dense[g * local_rows : (g + 1) * local_rows]
        for g, (to, _) in enumerate(groups):
            for v in range(local_vars):
                for q in range(2):
                    column = (v % half_vars * 2 + q) * cells
                    rows = [
                        acc[g, pl.ds(q * local_rows + t * local_vars + v, tiles // 2, stride), :]
                        for t in range(steps)
                    ]
                    out[where[0], to, v // half_vars, :, pl.ds(column, cells)] = jnp.concatenate(
                        rows, axis=0
                    ).astype(out.dtype)


def regrid_kernel(steps, jobs, *refs):
    run_jobs(steps, jobs, refs, *refs[-3:])


def finish_kernel(steps, halves, jobs, count, *refs):
    mine, theirs, rows_x, out, acc, scale, weight, total, sem = refs[count:]
    sub, mine_group = lax.axis_index("sub"), lax.axis_index("grp")
    chunks = sem.shape[0]
    height = mine.shape[0] // chunks

    def copy(chunk):
        span = pl.ds(pl.multiple_of(chunk * height, height), height)
        return pltpu.make_async_copy(theirs.at[span, :], weight.at[span, :], sem.at[chunk])

    for chunk in range(chunks):
        copy(chunk).start()
    run_jobs(steps, jobs, refs, rows_x, acc, scale)
    total[...] = jnp.zeros_like(total)

    @pl.loop(0, chunks)
    def _(chunk):
        span = pl.ds(pl.multiple_of(chunk * height, height), height)
        left, right = (
            rows_x[:, :, place, :, span].reshape(total.shape[0], height) for place in (sub, 1 - sub)
        )
        copy(chunk).wait()
        total[...] += jnp.dot(
            left, mine[span, :], preferred_element_type=jnp.float32
        ) + jnp.dot(right, weight[span, :], preferred_element_type=jnp.float32)

    send_rows(steps, halves, rows_x.shape, mine_group, total, out)


def send_rows(steps, halves, shape, mine_group, total, out):
    bands, groups, _, row_count, _ = shape
    count = steps * halves
    share = row_count // count
    for g in range(groups):
        base = (mine_group if g == 0 else 1 - mine_group) * count if groups > 1 else 0
        for chunk in range(count):
            pieces = [
                total[pl.ds((b * groups + g) * row_count + chunk * share, share), :]
                for b in range(bands)
            ]
            out[base + chunk] = jnp.concatenate(pieces, axis=0).astype(out.dtype)


def regrid(jobs, previous, bands, groups, steps, tiles, rows, cells, last=None):
    operands, specs, places = [], [], {}

    def place(array, space):
        if id(array) not in places:
            places[id(array)] = len(operands)
            operands.append(array)
            specs.append(pl.BlockSpec(memory_space=space))
        return places[id(array)]

    listed, flops, most = [], 0, 1
    for table, where, meta, meta_at, parts, sizes, fields in jobs:
        listed.append(
            (
                place(table, pltpu.SMEM),
                place(where, pltpu.SMEM),
                place(meta, pltpu.VMEM),
                meta_at,
                [(place(part, pltpu.VMEM), size) for part, size in zip(parts, sizes)],
                [(to, [place(f, pltpu.VMEM) for f in pair]) for to, pair in fields],
            )
        )
        flops += 2 * sum(sizes) * len(fields) * rows * cells * cells
        most = max(most, len(fields))
    aliases = {}
    vmem = pl.BlockSpec(memory_space=pltpu.VMEM)
    if previous is not None:
        aliases = {len(operands): 0}
        operands.append(previous)
        specs.append(vmem)
    shape = (bands, groups, 2, steps * tiles // 2, rows // steps // 2 * 2 * cells)
    shapes = [jax.ShapeDtypeStruct(shape, jnp.bfloat16)]
    scratch = [
        pltpu.VMEM((most, tiles // 2 * (2 * rows + 8), cells), jnp.float32),
        pltpu.VMEM((2 * tiles + 8, cells), jnp.float32),
    ]
    if last is None:
        body = functools.partial(regrid_kernel, steps, listed)
        limit, moved = 12 << 20, len(jobs) * 3 << 20
    else:
        mine, theirs, halves = last
        height, width = mine.shape
        total = bands * groups * shape[3]
        body = functools.partial(finish_kernel, steps, halves, listed, len(operands))
        operands += [mine, theirs]
        specs += [vmem, pl.BlockSpec(memory_space=pl.ANY)]
        count = groups * steps * halves
        shapes.append(jax.ShapeDtypeStruct((count, total // count, width), jnp.bfloat16))
        scratch += [
            pltpu.VMEM((height, width), jnp.bfloat16),
            pltpu.VMEM((total, width), jnp.float32),
            pltpu.SemaphoreType.DMA((3,)),
        ]
        limit, moved = 24 << 20, 4 * height * width
        flops += 4 * total * height * width
    done = pl.pallas_call(
        body,
        out_shape=shapes,
        in_specs=specs,
        out_specs=[vmem] * len(shapes),
        scratch_shapes=scratch,
        input_output_aliases=aliases,
        cost_estimate=pl.CostEstimate(flops=flops, bytes_accessed=moved, transcendentals=0),
        compiler_params=pltpu.CompilerParams(vmem_limit_bytes=limit),
    )(*operands)
    return done[-1]


def embed_kernel(steps, halves, rows_x, mine, theirs, out, total):
    at = pl.program_id(0)
    sub, mine_group = lax.axis_index("sub"), lax.axis_index("grp")
    bands, groups, _, row_count, width = rows_x.shape
    rows = bands * groups * row_count

    @pl.when(at == 0)
    def _():
        total[...] = jnp.zeros_like(total)

    left = rows_x[:, :, sub].reshape(rows, width)
    right = rows_x[:, :, 1 - sub].reshape(rows, width)
    total[...] += jnp.dot(left, mine[...], preferred_element_type=jnp.float32) + jnp.dot(
        right, theirs[...], preferred_element_type=jnp.float32
    )

    @pl.when(at == pl.num_programs(0) - 1)
    def _():
        if out.ndim == 2:
            out[...] = total[...].astype(out.dtype)
        else:
            send_rows(steps, halves, rows_x.shape, mine_group, total, out)


def embed(rows_x, mine, theirs, steps, halves):
    bands, groups, _, row_count, half_width = rows_x.shape
    width = mine.shape[-1]
    grid = 6 if half_width % (6 * 256) == 0 else 3
    step_rows = half_width // grid
    rows = bands * groups * row_count
    chunks = groups * steps * halves
    share = row_count // (steps * halves)
    shape = (chunks, bands * share, width) if share % 4 == 0 else (rows, width)
    weight_spec = pl.BlockSpec((step_rows, width), lambda i: (i, 0))
    out = pl.pallas_call(
        functools.partial(embed_kernel, steps, halves),
        out_shape=jax.ShapeDtypeStruct(shape, jnp.bfloat16),
        grid=(grid,),
        in_specs=[
            pl.BlockSpec((bands, groups, 2, row_count, step_rows), lambda i: (0, 0, 0, 0, i)),
            weight_spec,
            weight_spec,
        ],
        out_specs=pl.BlockSpec(shape, lambda i: (0,) * len(shape)),
        scratch_shapes=[pltpu.VMEM((rows, width), jnp.float32)],
        cost_estimate=pl.CostEstimate(
            flops=4 * rows * mine.shape[0] * width,
            bytes_accessed=4 * mine.shape[0] * width,
            transcendentals=0,
        ),
        compiler_params=pltpu.CompilerParams(
            vmem_limit_bytes=(48 if rows > 1024 else 16) << 20
        ),
    )(rows_x, mine, theirs)
    if share % 4:
        out = out.reshape(bands, chunks, share, width).transpose(1, 0, 2, 3)
        out = out.reshape(chunks, bands * share, width)
    return out


def swap(x, axis):
    return lax.ppermute(x, axis, [(0, 1), (1, 0)])


def per_device(
    ocean_fields,
    ocean_dest,
    ocean_weights,
    ocean_tiles,
    atmos_fields,
    atmos_dest,
    atmos_weights,
    atmos_tiles,
    land_fraction,
    embed_weight,
    embed_bias,
    embed_gain,
):
    nb = lax.axis_size("band")
    nv = lax.axis_size("var")
    ng = lax.axis_size("grp")
    rep = nv * ng
    cap = ocean_weights.shape[3]
    cells = ocean_weights.shape[-1]
    block_count, steps, local_vars, _ = ocean_fields.shape
    patches = land_fraction.shape[2]
    tiles = 2 * patches
    slots = 2 * cap
    share = patches // nv
    me = lax.axis_index("band")
    x, y = lax.axis_index("var"), lax.axis_index("grp")
    quarter = y * nv + x

    flat = (nb, cap * cells, cells)
    ocean_w, atmos_w = ocean_weights.reshape(flat), atmos_weights.reshape(flat)
    ocean_ids, atmos_ids = ocean_tiles.reshape(nb, cap), atmos_tiles.reshape(nb, cap)
    land = land_fraction.reshape(tiles, cells)
    blocks = (block_count, steps * local_vars, cells)
    ocean_f, atmos_f = ocean_fields.reshape(blocks), atmos_fields.reshape(blocks)
    order = ([1, nb - 1] + list(range(2, nb - 1)))[: nb - 1]
    along = lambda shift: [(b, (b + shift) % nb) for b in range(nb)]
    call = functools.partial(
        regrid, bands=nb, steps=steps, tiles=tiles, rows=steps * local_vars, cells=cells
    )

    if ng == 2 and nv == 2 and cap % 2 == 0 and steps == nb:
        each = cap // 2
        pieces = []
        for shift in order:
            pieces.append((shift, 0, each, each))
        *packed, send = pack(
            60, pieces, ocean_w, atmos_w, ocean_ids, atmos_ids, land, ocean_f, atmos_f
        )
        sent = [
            lax.ppermute(piece, "band", along(shift))
            for piece, (shift, _, _, _) in zip(packed[:2], pieces)
        ]
        embed_other, own_land, send = lax.optimization_barrier((embed_weight, land, send))
        own_w = pack(60, [(0, 0, cap, None)], ocean_w, atmos_w, ocean_ids, atmos_ids, own_land)[0]
        embed_other = swap(embed_other, "sub")
        keep, theirs = (ocean_f, atmos_f), (swap(send, "grp"),)
        dest = jnp.where(y == 0, ocean_dest, atmos_dest)
        block_all, used_all = slot_tables(dest, nb, cap)
        def job_of(band, parts, sizes, firsts, fields):
            meta_at = sizes[0] * cells
            tile = parts[0][meta_at + 2 * tiles, :cap].astype(jnp.int32)
            block = lax.dynamic_index_in_dim(block_all, band, 0, keepdims=False)
            used = lax.dynamic_index_in_dim(used_all, band, 0, keepdims=False)
            scale = jnp.where(used, tile + y * tiles, 2 * tiles)
            table = jnp.stack([block, tile, scale]).astype(jnp.int32)
            where = jnp.stack([band] + firsts).astype(jnp.int32)
            return table, where, parts[0], meta_at, parts, sizes, fields

        def with_fields(job, fields):
            return job[:-1] + (fields,)

        def job_at(shift, fields):
            parts, sizes, firsts = [], [], []
            for piece, across, (of, first, size, _) in zip(sent, crossed, pieces):
                if of == shift:
                    parts += [piece, across]
                    sizes += [size, size]
                    firsts += [x * each + first, (1 - x) * each + first]
            return job_of((me - shift) % nb, parts, sizes, firsts, fields)

        ours, others = [(0, keep)], [(1, theirs)]
        jobs = [job_of(me, [own_w], [cap], [jnp.int32(0)], ours)]
        rows_x = call(jobs, None, groups=2)
        for at, (piece, (shift, _, _, _)) in enumerate(zip(packed[2:], pieces[2:])):
            piece, sent[at], rows_x = lax.optimization_barrier((piece, sent[at], rows_x))
            sent.append(lax.ppermute(piece, "band", along(shift)))
        crossed = [swap(piece, "var") for piece in sent]
        jobs += [job_at(shift, ours) for shift in order]
        rows_x = call(
            jobs[1:-1] + [with_fields(job, others) for job in jobs[:-1]], rows_x, groups=2
        )
        sent = call(
            [with_fields(jobs[-1], ours + others)],
            rows_x,
            groups=2,
            last=(embed_weight, embed_other, nv),
        )
        got = lax.all_to_all(sent, ("grp", "band", "var"), split_axis=0, concat_axis=0, tiled=True)
    else:
        embed_other = swap(embed_weight, "sub")
        both = jnp.concatenate([ocean_w, atmos_w], axis=1)
        fields = [(0, (jnp.concatenate([ocean_f, atmos_f], axis=0),))]
        ocean_block, ocean_used = slot_tables(ocean_dest, nb, cap)
        atmos_block, atmos_used = slot_tables(atmos_dest, nb, cap)
        block_all = jnp.concatenate([ocean_block, atmos_block + block_count], axis=1)
        used_all = jnp.concatenate([ocean_used, atmos_used], axis=1)
        grid_row = jnp.where(jnp.arange(slots) < cap, 0, tiles)

        def job_of(band, tile, meta, parts):
            block = lax.dynamic_index_in_dim(block_all, band, 0, keepdims=False)
            used = lax.dynamic_index_in_dim(used_all, band, 0, keepdims=False)
            scale = jnp.where(used, tile + grid_row, 2 * tiles)
            table = jnp.stack([block, tile, scale]).astype(jnp.int32)
            where = jnp.stack([band, jnp.int32(0)])
            return table, where, meta, 0, [parts], [slots], fields

        tile_ids = jnp.concatenate([ocean_ids, atmos_ids], axis=1)
        own_tile = lax.dynamic_index_in_dim(tile_ids, me, 0, keepdims=False)
        own_w = lax.dynamic_index_in_dim(both, me, 0, keepdims=False)
        rows_x = call([job_of(me, own_tile, land, own_w)], None, groups=1)
        share_rows = slots * cells // rep
        high = lax.reduce_precision(land, 8, 7)
        low = (land - high).astype(jnp.bfloat16)
        tile_rows = jnp.pad(tile_ids.astype(jnp.bfloat16), ((0, 0), (0, cells - slots)))
        for shift in order:
            target, band = (me + shift) % nb, (me - shift) % nb
            piece = lax.dynamic_slice(
                both, (target, quarter * share_rows, 0), (1, share_rows, cells)
            )[0]
            row = lax.dynamic_slice(tile_rows, (target, 0), (1, cells))
            row = jnp.broadcast_to(row, (16, cells))
            piece = jnp.concatenate([piece, high.astype(jnp.bfloat16), low, row], axis=0)
            parts = lax.all_gather(lax.ppermute(piece, "band", along(shift)), REPL, axis=0)
            meta = parts[0, share_rows:]
            tile = meta[2 * tiles, :slots].astype(jnp.int32)
            parts = parts[:, :share_rows].reshape(slots * cells, cells)
            rows_x = call([job_of(band, tile, meta, parts)], rows_x, groups=1)
        sent = embed(rows_x, embed_weight, embed_other, steps, nv)
        got = lax.all_to_all(sent, ("band", "var"), split_axis=0, concat_axis=0, tiled=True)
    shifted = jnp.sum(got.astype(jnp.float32), axis=0) + embed_bias
    inverse = lax.rsqrt(jnp.mean(shifted * shifted, axis=-1, keepdims=True) + 1e-05)
    finished = (shifted * inverse * embed_gain).astype(jnp.bfloat16)
    width = finished.shape[-1]
    finished = finished.reshape(nb, share, steps // nb, width).transpose(1, 0, 2, 3)
    return finished[None]


def solution(mesh):
    in_specs = (
        P(("grp", "band", "sub"), None, "var", None),
        P(("band", "sub"), None),
        P("band", "sub", None, None, None, None),
        P("band", "sub", None, None),
        P(("grp", "band", "sub"), None, "var", None),
        P(("band", "sub"), None),
        P("band", "sub", None, None, None, None),
        P("band", "sub", None, None),
        P("band", "sub", None, None, None),
        P(("var", "sub"), None),
        P(),
        P(),
    )
    out_specs = P("sub", "var", None, ("grp", "band"), None)
    return jax.shard_map(
        per_device, mesh=mesh, in_specs=in_specs, out_specs=out_specs, check_vma=False
    )
```
